32 devices in a mesh: seq: 8 (over z, y), batch: 4 (over x, core).
Axes of the slice: x: 2, y: 2, z: 4, core: 2. Of those that a mesh axis runs over, the one named last changes fastest.
Arguments:
- queries: bfloat16 [12288, 8192], P(('batch', 'seq')), parts along dimension 0, may hold values from -6 to 6
- keys: bfloat16 [12288, 8192], P(('batch', 'seq')), parts along dimension 0, may hold values from -6 to 6
- values: bfloat16 [12288, 8192], P(('batch', 'seq')), parts along dimension 0, may hold values from -6 to 6
- gain: float32 [8192], replicated, may hold values from 0.1 to 1.9
Outputs:
- mixed: bfloat16 [12288, 8192], P('batch', 'seq'), parts along dimension 0
The draws below stay inside these ranges and needn't reach their ends.
There are 4 independent parts, one for each index of `batch`. The reference program is written for one: setup_inputs(seed, part) draws one part's arguments, and reference() takes and returns one part's arrays. A program takes and returns all parts, laid end to end along the dimension named above; an argument that names none is the same for every part. Nothing has to cross between parts.
All inputs are finite; a program needn't handle non-finite values.
Results may differ from the reference program's by a relative error of at most 0.005.
Values may be sent and summed in bfloat16 or wider, within the bound.
No kernel may reach another device: no remote copies, remote signals or barrier semaphores. Data moves between devices by JAX's collectives and lax.ppermute only.
A program may use at most 384 MiB of HBM per device.

```python
import jax
import jax.numpy as jnp
from jax import lax

HEADS = 64
HEAD = 128
D = 8192
TOK_DEV = 384
LENGTH = 3072


def levels(own_key, dims, cuts, low, top_value):
    def one(axis_at, blocks):
        draws = jax.random.uniform(jax.random.fold_in(jax.random.fold_in(own_key, 6), axis_at), (blocks,), jnp.float32, low / len(cuts), top_value / len(cuts))
        return jnp.repeat(jnp.exp(draws), dims[axis_at] // blocks).reshape((-1,) + (1,) * (len(dims) - axis_at - 1))

    level = one(*cuts[0])
    for cut in cuts[1:]:
        level = level * one(*cut)
    return level


def centred(own_key, shape, deviation, reach, cuts=(), kind=jnp.bfloat16):
    entries = jax.random.normal(own_key, shape, jnp.float32) * deviation
    if len(cuts) > 0:
        entries = levels(own_key, shape, cuts, -0.22, 0.18) * entries
    return jnp.clip(entries, min=-reach, max=reach).astype(kind)


def setup_inputs(seed: int = 0, part: int = 0) -> dict:
    seeds = jax.random.split(jax.random.key(seed), 5)
    part_keys = jax.random.split(jax.random.fold_in(seeds[4], part), 5)
    return {
        "queries": centred(part_keys[0], (LENGTH, D), 1.0, 6.0, ((0, 8),)),
        "keys": centred(part_keys[1], (LENGTH, D), 1.0, 6.0, ((0, 8),)),
        "values": centred(part_keys[2], (LENGTH, D), 1.0, 6.0, ((0, 8),)),
        "gain": jnp.clip(1.0 + 0.18 * jax.random.normal(seeds[3], (D,), jnp.float32), 0.1, 1.9),
    }


def normalize(attended, gain):
    square = lax.optimization_barrier(jnp.mean(attended * attended, axis=-1, keepdims=True))
    return attended * lax.rsqrt(square + 1e-05) * gain.reshape(HEADS, HEAD)

def reference(queries, keys, values, gain):
    blocks = LENGTH // TOK_DEV
    qall = queries.reshape(blocks, TOK_DEV, HEADS, HEAD)
    kall = keys.reshape(blocks, TOK_DEV, HEADS, HEAD)
    vall = values.reshape(blocks, TOK_DEV, HEADS, HEAD)
    causal = jnp.tril(jnp.ones((TOK_DEV, TOK_DEV), dtype=bool))

    def advance(carry, parts):
        qblk, kblk, vblk = parts
        qf = qblk.astype(jnp.float32)
        kf = kblk.astype(jnp.float32)
        vf = vblk.astype(jnp.float32)
        local = jnp.einsum('thd,the->hde', kf, vf)
        state = lax.optimization_barrier(carry.astype(jnp.bfloat16)).astype(jnp.float32)
        scores = jnp.einsum('thd,shd->hts', qf, kf)
        scores = jnp.where(causal[None], scores, 0.0)
        scores = lax.optimization_barrier(scores.astype(jnp.bfloat16)).astype(jnp.float32)
        attended = jnp.einsum('hts,she->the', scores, vf) + jnp.einsum('thd,hde->the', qf, state)
        mixed = normalize(attended, gain).astype(jnp.bfloat16).reshape(TOK_DEV, D)
        return (carry + local, mixed)
    start = jnp.zeros((HEADS, HEAD, HEAD), dtype=jnp.float32)
    _, outs = lax.scan(advance, start, (qall, kall, vall))
    return outs.reshape(LENGTH, D)
```

```python
import functools

import jax
import jax.numpy as jnp
from jax import lax
from jax.experimental import pallas as pl
from jax.experimental.pallas import tpu as pltpu
from jax.sharding import PartitionSpec as P

HEADS = 64
HEAD = 128
WIDTHS = (2, 2, 2, 2)
BLOCK = 128
VMEM = 48 * 1024 * 1024


def params():
    return pltpu.CompilerParams(vmem_limit_bytes=VMEM)


def local_body(width, place, kown, vown, koth, voth, own, oth):
    for head in range(width):
        cols = slice(head * HEAD, (head + 1) * HEAD)
        own[0, head] = lax.dot_general(
            kown[:, cols], vown[:, cols], (((0,), (0,)), ((), ())), preferred_element_type=jnp.float32
        )
        oth[0, head] = lax.dot_general(
            koth[:, cols], voth[:, cols], (((0,), (0,)), ((), ())), preferred_element_type=jnp.float32
        ).astype(oth.dtype)


def column_maps(per_dest, low, width, turn):
    def row_of(i, place, rows):
        return lax.rem(i + place[0], rows) if turn else i

    def own(i, place, rows):
        return ((2 * row_of(i, place, rows) + place[1]) * per_dest + low) // width

    def oth(i, place, rows):
        return ((2 * row_of(i, place, rows) + 1 - place[1]) * per_dest + low) // width

    return row_of, own, oth


def local_states(place, keys, values, n, low, width):
    rows, m = keys.shape[0], n // 2
    _, own, oth = column_maps(HEADS // n, low, width, False)
    spec_own = pl.BlockSpec((rows, width * HEAD), lambda i, place: (0, own(i, place, m)))
    spec_oth = pl.BlockSpec((rows, width * HEAD), lambda i, place: (0, oth(i, place, m)))
    out = pl.BlockSpec((1, width, HEAD, HEAD), lambda i, place: (i, 0, 0, 0))
    shape = (m, width, HEAD, HEAD)
    return pl.pallas_call(
        functools.partial(local_body, width),
        grid_spec=pltpu.PrefetchScalarGridSpec(
            num_scalar_prefetch=1,
            grid=(m,),
            in_specs=[spec_own, spec_own, spec_oth, spec_oth],
            out_specs=[out, out],
        ),
        out_shape=[jax.ShapeDtypeStruct(shape, jnp.float32), jax.ShapeDtypeStruct(shape, jnp.bfloat16)],
        compiler_params=params(),
        cost_estimate=pl.CostEstimate(
            flops=4 * m * width * rows * HEAD * HEAD, bytes_accessed=8 * rows * m * width * HEAD, transcendentals=0
        ),
        name="local",
    )(place, keys, values, keys, values)


def attend_head(query, key, value, state, gain):
    rows = query.shape[0]
    spot = lax.broadcasted_iota(jnp.int32, (BLOCK, BLOCK), 0)
    other = lax.broadcasted_iota(jnp.int32, (BLOCK, BLOCK), 1)
    keep = other <= spot
    pieces = []
    for block in range(rows // BLOCK):
        low, high = block * BLOCK, (block + 1) * BLOCK
        qpart = query[low:high]
        scores = lax.dot_general(
            qpart, key[:high], (((1,), (1,)), ((), ())), preferred_element_type=jnp.float32
        )
        last = jnp.where(keep, scores[:, low:], 0.0)
        scores = jnp.concatenate([scores[:, :low], last], axis=1) if block else last
        left = jnp.concatenate([scores.astype(jnp.bfloat16), qpart], axis=1)
        right = jnp.concatenate([value[:high], state], axis=0)
        attended = jnp.dot(left, right, preferred_element_type=jnp.float32)
        square = jnp.mean(attended * attended, axis=-1, keepdims=True)
        pieces.append((attended * lax.rsqrt(square + 1e-05) * gain).astype(jnp.bfloat16))
    return jnp.concatenate(pieces, axis=0)


def attend_body(width, m, place, qown, kown, vown, sown, gown, qoth, koth, voth, soth, goth, *outs):
    step = pl.program_id(0)
    sides = ((qown, kown, vown, sown, gown), (qoth, koth, voth, soth, goth))
    for side, (q, k, v, s, g) in enumerate(sides):
        for head in range(width):
            cols = slice(head * HEAD, (head + 1) * HEAD)
            mixed = attend_head(q[:, cols], k[:, cols], v[:, cols], s[0, head], g[:, cols])
            for row in range(m):

                @pl.when(step == row)
                def _(row=row, cols=cols, mixed=mixed, side=side):
                    outs[2 * row + side][:, cols] = mixed


def attend(place, queries, keys, values, gain, state_own, state_oth, n, low, width):
    rows, m = queries.shape[0], n // 2
    row_of, own, oth = column_maps(HEADS // n, low, width, True)
    wide = width * HEAD

    def specs(col):
        tok = pl.BlockSpec((rows, wide), lambda i, place: (0, col(i, place, m)))
        state = pl.BlockSpec((1, width, HEAD, HEAD), lambda i, place: (row_of(i, place, m), 0, 0, 0))
        return [tok, tok, tok, state, pl.BlockSpec((1, wide), lambda i, place: (0, col(i, place, m)))]

    flops = 2 * m * width * rows * HEAD * (3 * rows + 2 * HEAD)
    return pl.pallas_call(
        functools.partial(attend_body, width, m),
        grid_spec=pltpu.PrefetchScalarGridSpec(
            num_scalar_prefetch=1,
            grid=(m,),
            in_specs=specs(own) + specs(oth),
            out_specs=[pl.BlockSpec((rows, wide), lambda i, place: (0, 0))] * n,
        ),
        out_shape=[jax.ShapeDtypeStruct((rows, wide), jnp.bfloat16)] * n,
        compiler_params=params(),
        cost_estimate=pl.CostEstimate(
            flops=flops, bytes_accessed=16 * rows * m * wide, transcendentals=2 * m * width * rows
        ),
        name="attend",
    )(place, queries, keys, values, state_own, gain, queries, keys, values, state_oth, gain)


def place_body(n, low, first, place, *refs):
    parts, out, sems = refs[:n], refs[-2], refs[-1]
    m = n // 2
    rows, wide = parts[0].shape
    copies = []
    for shift in range(n):
        row = lax.rem(place[0] + m - shift // 2, m)
        col = place[1] if shift % 2 == 0 else 1 - place[1]
        start = pl.multiple_of((2 * row + col) * rows, rows)
        copies.append(
            pltpu.make_async_copy(
                parts[shift], out.at[pl.ds(start, rows), pl.ds(low * HEAD, wide)], sems.at[shift]
            )
        )
    for copy in copies:
        copy.start()
    for copy in copies:
        copy.wait()


def put(place, parts, out, n, low):
    rows, first = parts[0].shape[0], out is None
    anywhere = pl.BlockSpec(memory_space=pl.ANY)
    return pl.pallas_call(
        functools.partial(place_body, n, low, first),
        grid_spec=pltpu.PrefetchScalarGridSpec(
            num_scalar_prefetch=1,
            grid=(1,),
            in_specs=[anywhere] * (n if first else n + 1),
            out_specs=anywhere,
            scratch_shapes=[pltpu.SemaphoreType.DMA((n,))],
        ),
        out_shape=jax.ShapeDtypeStruct((n * rows, HEADS // n * HEAD), jnp.bfloat16),
        input_output_aliases={} if first else {n + 1: 0},
        compiler_params=params(),
        name="put",
    )(place, *parts, *(() if first else (out,)))


def per_device(n, queries, keys, values, gain):
    m, per_dest = n // 2, HEADS // n
    me = lax.axis_index("seq")
    row, col = me // 2, me % 2
    place = jnp.stack([row, col]).astype(jnp.int32)
    gain = gain.reshape(1, HEADS * HEAD)
    f32, bf16 = jnp.float32, jnp.bfloat16

    def index(z, y):
        return 2 * (z % m) + y % 2

    swap = [(d, d ^ 1) for d in range(n)]
    chunks, low = [], 0
    for width in WIDTHS:
        if low < per_dest:
            width = min(width, per_dest - low)
            chunks.append((low, width))
            low += width

    states = []
    for low, width in chunks:
        own, oth = local_states(place, keys, values, n, low, width)
        near = lax.ppermute(oth, "seq", swap).astype(f32)
        both = own + near
        carried = jnp.zeros(own.shape, bf16)
        message = both.astype(bf16)
        for hop in range(m - 1):
            pairs = [(index(hop, y), index(hop + 1, y)) for y in range(2)]
            arrived = lax.ppermute(message, "seq", pairs)
            carried = carried + arrived
            message = (arrived.astype(f32) + both).astype(bf16)
        prefix = carried.astype(f32)
        state_own = (prefix + jnp.where(col == 1, near, 0.0)).astype(bf16)
        state_oth = lax.ppermute((prefix + jnp.where(col == 0, own, 0.0)).astype(bf16), "seq", swap)
        states.append((state_own, state_oth))

    out = None
    for (low, width), (state_own, state_oth) in zip(chunks, states):
        parts = attend(place, queries, keys, values, gain, state_own, state_oth, n, low, width)
        arrived = [parts[0]]
        for shift in range(1, n):
            pairs = [(index(z, y), index(z + shift // 2, y + shift)) for z in range(m) for y in range(2)]
            arrived.append(lax.ppermute(parts[shift], "seq", pairs))
        out = put(place, arrived, out, n, low)
    return out


def solution(mesh):
    tokens = P(("batch", "seq"), None)
    return jax.shard_map(
        functools.partial(per_device, mesh.shape["seq"]),
        mesh=mesh,
        in_specs=(tokens, tokens, tokens, P()),
        out_specs=P("batch", "seq"),
        check_vma=False,
    )
```

```python
import functools

import jax
import jax.numpy as jnp
from jax import lax
from jax.experimental import pallas as pl
from jax.experimental.pallas import tpu as pltpu
from jax.sharding import PartitionSpec as P

HEADS = 64
HEAD = 128
WIDTHS = (1, 1, 2, 2, 2)
TILE = 256
VMEM = 48 * 1024 * 1024


def params():
    return pltpu.CompilerParams(vmem_limit_bytes=VMEM)


def local_body(width, place, kown, vown, koth, voth, *refs):
    own, oth = refs[-2], refs[-1]
    for k, v, out in ((kown, vown, own), (koth, voth, oth)):
        both = lax.dot_general(k[...], v[...], (((0,), (0,)), ((), ())), preferred_element_type=jnp.float32)
        for head in range(width):
            cols = slice(head * HEAD, (head + 1) * HEAD)
            out[0, head] = both[cols, cols].astype(out.dtype)


def column_maps(per_dest, low, width, turn):
    def row_of(i, place, rows):
        return lax.rem(i + place[0], rows) if turn else i

    def own(i, place, rows):
        return ((2 * row_of(i, place, rows) + place[1]) * per_dest + low) // width

    def oth(i, place, rows):
        return ((2 * row_of(i, place, rows) + 1 - place[1]) * per_dest + low) // width

    return row_of, own, oth


def local_states(place, keys, values, n, low, width, after):
    rows, m = keys.shape[0], n // 2
    _, own, oth = column_maps(HEADS // n, low, width, False)
    spec_own = pl.BlockSpec((rows, width * HEAD), lambda i, place: (0, own(i, place, m)))
    spec_oth = pl.BlockSpec((rows, width * HEAD), lambda i, place: (0, oth(i, place, m)))
    out = pl.BlockSpec((1, width, HEAD, HEAD), lambda i, place: (i, 0, 0, 0))
    shape = (m, width, HEAD, HEAD)
    return pl.pallas_call(
        functools.partial(local_body, width),
        grid_spec=pltpu.PrefetchScalarGridSpec(
            num_scalar_prefetch=1,
            grid=(m,),
            in_specs=[spec_own, spec_own, spec_oth, spec_oth] + [pl.BlockSpec(memory_space=pl.ANY)] * len(after),
            out_specs=[out, out],
        ),
        out_shape=[jax.ShapeDtypeStruct(shape, jnp.float32), jax.ShapeDtypeStruct(shape, jnp.bfloat16)],
        compiler_params=params(),
        cost_estimate=pl.CostEstimate(
            flops=4 * m * width * rows * HEAD * HEAD, bytes_accessed=8 * rows * m * width * HEAD, transcendentals=0
        ),
        name="local",
    )(place, keys, values, keys, values, *after)


def masked_scores(query, key):
    rows = query.shape[0]
    tiles = []
    for low in range(0, rows, TILE):
        high = min(low + TILE, rows)
        part = lax.dot_general(
            query[low:], key[low:high], (((1,), (1,)), ((), ())), preferred_element_type=jnp.float32
        )
        spot = lax.broadcasted_iota(jnp.int32, part.shape, 0)
        other = lax.broadcasted_iota(jnp.int32, part.shape, 1)
        part = jnp.where(other <= spot, part, 0.0).astype(jnp.bfloat16)
        if low:
            part = jnp.concatenate([jnp.zeros((low, high - low), jnp.bfloat16), part], axis=0)
        tiles.append(part)
    return tiles


def attend_body(width, m, place, qown, kown, vown, sown, gown, qoth, koth, voth, soth, goth, *refs):
    outs, held, sems = refs[: 2 * m], refs[-2], refs[-1]
    step = pl.program_id(0)
    sides = ((qown, kown, vown, sown, gown), (qoth, koth, voth, soth, goth))
    heads = [
        (side, head, slice(head * HEAD, (head + 1) * HEAD)) for side in range(2) for head in range(width)
    ]
    scores = [masked_scores(sides[side][0][:, cols], sides[side][1][:, cols]) for side, _, cols in heads]
    attended = []
    for (side, head, cols), tiles in zip(heads, scores):
        q, _, v, s, _ = sides[side]
        left = jnp.concatenate([*tiles, q[:, cols]], axis=1)
        right = jnp.concatenate([v[:, cols], s[0, head]], axis=0)
        attended.append(jnp.dot(left, right, preferred_element_type=jnp.float32))
    for (side, _, cols), value in zip(heads, attended):
        square = jnp.mean(value * value, axis=-1, keepdims=True)
        mixed = value * lax.rsqrt(square + 1e-05) * sides[side][4][:, cols]
        held[2 * step + side, :, cols] = mixed.astype(held.dtype)

    def sends(row):
        return [
            pltpu.make_async_copy(held.at[2 * row + side], outs[2 * row + side], sems.at[2 * row + side])
            for side in range(2)
        ]

    for row in range(m):

        @pl.when(step == row)
        def _(row=row):
            for copy in sends(row):
                copy.start()

    @pl.when(step == m - 1)
    def _():
        for row in range(m):
            for copy in sends(row):
                copy.wait()


def attend(place, queries, keys, values, gain, state_own, state_oth, n, low, width):
    rows, m = queries.shape[0], n // 2
    row_of, own, oth = column_maps(HEADS // n, low, width, True)
    wide = width * HEAD

    def specs(col):
        tok = pl.BlockSpec((rows, wide), lambda i, place: (0, col(i, place, m)))
        state = pl.BlockSpec((1, width, HEAD, HEAD), lambda i, place: (row_of(i, place, m), 0, 0, 0))
        return [tok, tok, tok, state, pl.BlockSpec((1, wide), lambda i, place: (0, col(i, place, m)))]

    flops = 2 * m * width * rows * HEAD * (3 * rows + 2 * HEAD)
    return pl.pallas_call(
        functools.partial(attend_body, width, m),
        grid_spec=pltpu.PrefetchScalarGridSpec(
            num_scalar_prefetch=1,
            grid=(m,),
            in_specs=specs(own) + specs(oth),
            out_specs=[pl.BlockSpec(memory_space=pl.ANY)] * n,
            scratch_shapes=[pltpu.VMEM((n, rows, wide), jnp.bfloat16), pltpu.SemaphoreType.DMA((n,))],
        ),
        out_shape=[jax.ShapeDtypeStruct((rows, wide), jnp.bfloat16)] * n,
        compiler_params=params(),
        cost_estimate=pl.CostEstimate(
            flops=flops, bytes_accessed=16 * rows * m * wide, transcendentals=2 * m * width * rows
        ),
        name="attend",
    )(place, queries, keys, values, state_own, gain, queries, keys, values, state_oth, gain)


def place_body(n, low, first, place, *refs):
    parts, out, sems = refs[:n], refs[-2], refs[-1]
    m = n // 2
    rows, wide = parts[0].shape
    copies = []
    for shift in range(n):
        row = lax.rem(place[0] + m - shift // 2, m)
        col = place[1] if shift % 2 == 0 else 1 - place[1]
        start = pl.multiple_of((2 * row + col) * rows, rows)
        copies.append(
            pltpu.make_async_copy(
                parts[shift], out.at[pl.ds(start, rows), pl.ds(low * HEAD, wide)], sems.at[shift]
            )
        )
    for copy in copies:
        copy.start()
    for copy in copies:
        copy.wait()


def put(place, parts, out, n, low):
    rows, first = parts[0].shape[0], out is None
    anywhere = pl.BlockSpec(memory_space=pl.ANY)
    return pl.pallas_call(
        functools.partial(place_body, n, low, first),
        grid_spec=pltpu.PrefetchScalarGridSpec(
            num_scalar_prefetch=1,
            grid=(1,),
            in_specs=[anywhere] * (n if first else n + 1),
            out_specs=anywhere,
            scratch_shapes=[pltpu.SemaphoreType.DMA((n,))],
        ),
        out_shape=jax.ShapeDtypeStruct((n * rows, HEADS // n * HEAD), jnp.bfloat16),
        input_output_aliases={} if first else {n + 1: 0},
        compiler_params=params(),
        name="put",
    )(place, *parts, *(() if first else (out,)))


def per_device(n, queries, keys, values, gain):
    m, per_dest = n // 2, HEADS // n
    me = lax.axis_index("seq")
    row, col = me // 2, me % 2
    place = jnp.stack([row, col]).astype(jnp.int32)
    gain = gain.reshape(1, HEADS * HEAD)
    f32, bf16 = jnp.float32, jnp.bfloat16

    def index(z, y):
        return 2 * (z % m) + y % 2

    swap = [(d, d ^ 1) for d in range(n)]
    chunks, low = [], 0
    for width in WIDTHS:
        if low < per_dest:
            width = min(width, per_dest - low)
            chunks.append((low, width))
            low += width

    states, lead = [], []
    for spot, (low, width) in enumerate(chunks):
        after = lead[min(spot - 2, len(lead) - 1)] if spot >= 2 else None
        own, oth = local_states(place, keys, values, n, low, width, () if after is None else (after,))
        near = lax.ppermute(oth, "seq", swap).astype(f32)
        both = own + near
        carried = jnp.zeros(own.shape, bf16)
        message = both.astype(bf16)
        for hop in range(m - 1):
            if spot == 0:
                lead.append(message)
            pairs = [(index(hop, y), index(hop + 1, y)) for y in range(2)]
            arrived = lax.ppermute(message, "seq", pairs)
            carried = carried + arrived
            message = (arrived.astype(f32) + both).astype(bf16)
        prefix = carried.astype(f32)
        state_own = (prefix + jnp.where(col == 1, near, 0.0)).astype(bf16)
        state_oth = lax.ppermute((prefix + jnp.where(col == 0, own, 0.0)).astype(bf16), "seq", swap)
        states.append((state_own, state_oth))

    out = None
    for (low, width), (state_own, state_oth) in zip(chunks, states):
        parts = attend(place, queries, keys, values, gain, state_own, state_oth, n, low, width)
        arrived = [parts[0]]
        for shift in range(1, n):
            pairs = [(index(z, y), index(z + shift // 2, y + shift)) for z in range(m) for y in range(2)]
            arrived.append(lax.ppermute(parts[shift], "seq", pairs))
        out = put(place, arrived, out, n, low)
    return out


def solution(mesh):
    tokens = P(("batch", "seq"), None)
    return jax.shard_map(
        functools.partial(per_device, mesh.shape["seq"]),
        mesh=mesh,
        in_specs=(tokens, tokens, tokens, P()),
        out_specs=P("batch", "seq"),
        check_vma=False,
    )
```

```python
import functools

import jax
import jax.numpy as jnp
from jax import lax
from jax.experimental import pallas as pl
from jax.experimental.pallas import tpu as pltpu
from jax.sharding import PartitionSpec as P

HEADS = 64
HEAD = 128
WIDTHS = (1, 1, 2, 2, 2)
TILE = 256
WINDOW = 4
VMEM = 48 * 1024 * 1024
ORDER = {
    ("local", 2): [("message", 0, 1)],
    ("local", 3): [("message", 0, 2)],
    ("local", 4): [("sent", 0, 1)],
    ("message", 2, 3): [("mixed", 0)],
    ("sent", 0, 4): [("message", 2, 3)],
    ("sent", 0, 5): [("message", 3, 2)],
    ("mixed", 1): [("sent", 0, 2)],
    ("message", 2, 4): [("sent", 0, 4)],
    ("sent", 1, 3): [("message", 2, 4)],
    ("message", 3, 3): [("sent", 0, 6)],
    ("sent", 1, 4): [("message", 3, 3)],
    ("message", 4, 1): [("sent", 0, 7)],
    ("sent", 1, 5): [("message", 4, 1)],
    ("mixed", 2): [("sent", 1, 2)],
    ("sent", 1, 7): [("mixed", 2)],
    ("message", 3, 4): [("sent", 1, 6)],
    ("sent", 2, 2): [("message", 3, 4)],
    ("message", 4, 2): [("sent", 1, 6)],
    ("sent", 2, 3): [("message", 4, 2)],
    ("message", 4, 3): [("sent", 2, 2)],
    ("sent", 2, 5): [("message", 4, 3)],
    ("mixed", 3): [("sent", 2, 3)],
    ("sent", 2, 7): [("mixed", 3)],
    ("message", 4, 4): [("sent", 2, 5)],
    ("sent", 3, 2): [("message", 4, 4)],
    ("mixed", 4): [("sent", 3, 3)],
    ("sent", 3, 7): [("mixed", 4)],
}


def params():
    return pltpu.CompilerParams(vmem_limit_bytes=VMEM)


def column(place, row, side, n, low):
    col = place[1] if side == 0 else 1 - place[1]
    return pl.multiple_of(((2 * row + col) * (HEADS // n) + low) * HEAD, HEAD)


def local_body(n, low, width, place, keys, values, own, oth, kbuf, vbuf, sems):
    m = n // 2
    copies = []
    for slot in range(n):
        cols = pl.ds(column(place, slot // 2, slot % 2, n, low), width * HEAD)
        copies.append(
            [
                pltpu.make_async_copy(source.at[:, cols], buf.at[slot], sems.at[which, slot])
                for which, (source, buf) in enumerate(((keys, kbuf), (values, vbuf)))
            ]
        )
    for pair in copies:
        for copy in pair:
            copy.start()
    for slot in range(n):
        for copy in copies[slot]:
            copy.wait()
        both = lax.dot_general(
            kbuf[slot], vbuf[slot], (((0,), (0,)), ((), ())), preferred_element_type=jnp.float32
        )
        out = own if slot % 2 == 0 else oth
        for head in range(width):
            cols = slice(head * HEAD, (head + 1) * HEAD)
            out[slot // 2, head] = both[cols, cols].astype(out.dtype)


def local_states(place, keys, values, n, low, width):
    rows, m = keys.shape[0], n // 2
    shape = (m, width, HEAD, HEAD)
    buf = pltpu.VMEM((n, rows, width * HEAD), keys.dtype)
    whole = pl.BlockSpec(memory_space=pltpu.VMEM)
    return pl.pallas_call(
        functools.partial(local_body, n, low, width),
        in_specs=[pl.BlockSpec(memory_space=pltpu.SMEM)] + [pl.BlockSpec(memory_space=pl.ANY)] * 2,
        out_specs=[whole, whole],
        out_shape=[jax.ShapeDtypeStruct(shape, jnp.float32), jax.ShapeDtypeStruct(shape, jnp.bfloat16)],
        scratch_shapes=[buf, buf, pltpu.SemaphoreType.DMA((2, n))],
        compiler_params=params(),
        cost_estimate=pl.CostEstimate(
            flops=2 * n * width * rows * HEAD * HEAD, bytes_accessed=4 * rows * n * width * HEAD, transcendentals=0
        ),
        name="local",
    )(place, keys, values)


def masked_scores(query, key):
    rows = query.shape[0]
    tiles = []
    for low in range(0, rows, TILE):
        high = min(low + TILE, rows)
        part = lax.dot_general(
            query[low:], key[low:high], (((1,), (1,)), ((), ())), preferred_element_type=jnp.float32
        )
        size = high - low
        spot = lax.broadcasted_iota(jnp.int32, (size, size), 0)
        other = lax.broadcasted_iota(jnp.int32, (size, size), 1)
        pieces = [jnp.where(other <= spot, part[:size], 0.0).astype(jnp.bfloat16)]
        if low:
            pieces.insert(0, jnp.zeros((low, size), jnp.bfloat16))
        if high < rows:
            pieces.append(part[size:].astype(jnp.bfloat16))
        tiles.append(jnp.concatenate(pieces, axis=0) if len(pieces) > 1 else pieces[0])
    return tiles


def attend_body(n, low, width, place, queries, keys, values, own, oth, gain, *refs):
    outs = refs[:n]
    qbuf, kbuf, vbuf, sown, soth, gbuf, held, sems, extra = refs[n:]
    m = n // 2
    wide = width * HEAD
    spots = [lax.rem(place[0] + row, m) for row in range(m)]
    small = [
        pltpu.make_async_copy(source, buf, extra.at[which])
        for which, (source, buf) in enumerate(((own, sown), (oth, soth), (gain, gbuf)))
    ]
    copies = []
    for slot in range(n):
        cols = pl.ds(column(place, spots[slot // 2], slot % 2, n, low), wide)
        copies.append(
            [
                pltpu.make_async_copy(source.at[:, cols], buf.at[slot], sems.at[which, slot])
                for which, (source, buf) in enumerate(((queries, qbuf), (keys, kbuf), (values, vbuf)))
            ]
        )
    for slot in range(n):
        for copy in copies[slot]:
            copy.start()
        if slot == 1:
            for copy in small:
                copy.start()
    sends = [pltpu.make_async_copy(held.at[slot], outs[slot], sems.at[3, slot]) for slot in range(n)]
    group = max(1, 4 // width)
    for first in range(0, n, group):
        slots = range(first, min(first + group, n))
        for slot in slots:
            for copy in copies[slot]:
                copy.wait()
        heads = [(slot, head, slice(head * HEAD, (head + 1) * HEAD)) for slot in slots for head in range(width)]
        scores = [masked_scores(qbuf[slot, :, cols], kbuf[slot, :, cols]) for slot, _, cols in heads]
        if first == 0:
            for copy in small:
                copy.wait()
        attended = []
        for (slot, head, cols), tiles in zip(heads, scores):
            state = (sown if slot % 2 == 0 else soth)[spots[slot // 2], head]
            left = jnp.concatenate([*tiles, qbuf[slot, :, cols]], axis=1)
            right = jnp.concatenate([vbuf[slot, :, cols], state], axis=0)
            attended.append(jnp.dot(left, right, preferred_element_type=jnp.float32))
        for (slot, head, cols), value in zip(heads, attended):
            square = jnp.mean(value * value, axis=-1, keepdims=True)
            start = column(place, spots[slot // 2], slot % 2, n, low + head)
            mixed = value * lax.rsqrt(square + 1e-05) * gbuf[:, pl.ds(start, HEAD)]
            held[slot, :, cols] = mixed.astype(held.dtype)
        for slot in slots:
            sends[slot].start()
    for copy in sends:
        copy.wait()


def attend(place, queries, keys, values, gain, state_own, state_oth, n, low, width):
    rows, m = queries.shape[0], n // 2
    wide = width * HEAD
    tokens = pltpu.VMEM((n, rows, wide), jnp.bfloat16)
    state = pltpu.VMEM((m, width, HEAD, HEAD), jnp.bfloat16)
    return pl.pallas_call(
        functools.partial(attend_body, n, low, width),
        in_specs=[pl.BlockSpec(memory_space=pltpu.SMEM)] + [pl.BlockSpec(memory_space=pl.ANY)] * 6,
        out_specs=[pl.BlockSpec(memory_space=pl.ANY)] * n,
        out_shape=[jax.ShapeDtypeStruct((rows, wide), jnp.bfloat16)] * n,
        scratch_shapes=[
            tokens,
            tokens,
            tokens,
            state,
            state,
            pltpu.VMEM((1, HEADS * HEAD), jnp.float32),
            tokens,
            pltpu.SemaphoreType.DMA((4, n)),
            pltpu.SemaphoreType.DMA((3,)),
        ],
        compiler_params=params(),
        cost_estimate=pl.CostEstimate(
            flops=2 * n * width * rows * HEAD * (2 * rows + HEAD),
            bytes_accessed=8 * rows * n * wide,
            transcendentals=n * width * rows,
        ),
        name="attend",
    )(place, queries, keys, values, state_own, state_oth, gain)


def put_body(n, low, place, *refs):
    parts, out, again, sems = refs[:n], refs[-3], refs[-2], refs[-1]
    m = n // 2
    rows, wide = parts[0].shape
    copies = []
    for shift in range(n):
        row = lax.rem(place[0] + m - shift // 2, m)
        col = place[1] if shift % 2 == 0 else 1 - place[1]
        start = pl.multiple_of((2 * row + col) * rows, rows)
        copies.append(
            pltpu.make_async_copy(
                parts[shift], out.at[pl.ds(start, rows), pl.ds(low * HEAD, wide)], sems.at[shift]
            )
        )
    for copy in copies:
        copy.start()
    for index in range(2):
        again[index] = place[index]
    for copy in copies:
        copy.wait()


def put(place, parts, out, n, low):
    rows, first = parts[0].shape[0], out is None
    anywhere = pl.BlockSpec(memory_space=pl.ANY)
    return pl.pallas_call(
        functools.partial(put_body, n, low),
        in_specs=[pl.BlockSpec(memory_space=pltpu.SMEM)] + [anywhere] * (n if first else n + 1),
        out_specs=[anywhere, pl.BlockSpec(memory_space=pltpu.SMEM)],
        out_shape=[
            jax.ShapeDtypeStruct((n * rows, HEADS // n * HEAD), jnp.bfloat16),
            jax.ShapeDtypeStruct((2,), jnp.int32),
        ],
        scratch_shapes=[pltpu.SemaphoreType.DMA((n,))],
        input_output_aliases={} if first else {n + 1: 0},
        compiler_params=params(),
        name="put",
    )(place, *parts, *(() if first else (out,)))


def split(per_dest):
    chunks, low = [], 0
    for width in WIDTHS:
        if low < per_dest:
            width = min(width, per_dest - low)
            chunks.append((low, width))
            low += width
    return chunks


class Plan:
    def __init__(self, n, queries, keys, values, gain):
        self.n, self.m = n, n // 2
        me = lax.axis_index("seq")
        self.col = me % 2
        self.place = jnp.stack([me // 2, self.col]).astype(jnp.int32)
        self.arrays = queries, keys, values
        self.gain = gain.reshape(1, HEADS * HEAD)
        self.chunks = split(HEADS // n)
        self.made = {}

    def has(self, key):
        limit = {"message": self.m, "prefix": self.m, "sent": self.n - 1}.get(key[0], 0)
        return key[1] < len(self.chunks) and (len(key) < 3 or key[2] <= limit)

    def get(self, *key):
        if key not in self.made:
            self.made[key] = getattr(self, key[0])(*key[1:])
        return self.made[key]

    def hold(self, value, *key):
        others, steps = [], list(ORDER.get(key, ()))
        if key[0] == "sent":
            flat = key[1] * (self.n - 1) + key[2] - 1 - WINDOW
            if flat >= 0:
                steps.append(("sent", flat // (self.n - 1), flat % (self.n - 1) + 1))
        for other in steps:
            if self.has(other):
                result = self.get(*other)
                others.append(result[1] if other[0] == "mixed" else result)
        return lax.optimization_barrier((value, *others))[0] if others else value

    def local(self, c):
        low, width = self.chunks[c]
        _, keys, values = self.arrays
        return local_states(self.hold(self.place, "local", c), keys, values, self.n, low, width)

    def both(self, c):
        return self.get("local", c)[0] + self.get("prefix", c, 0).astype(jnp.float32)

    def total(self, c):
        parts = [self.get("prefix", c, s) for s in range(1, self.m)]
        return sum(parts[1:], parts[0]).astype(jnp.float32)

    def message(self, c, s):
        if s == 0:
            value = self.get("local", c)[1]
        elif s < self.m:
            value = self.get("both", c)
            if s > 1:
                value = self.get("prefix", c, s - 1).astype(jnp.float32) + value
        else:
            value = self.get("total", c) + jnp.where(self.col == 0, self.get("local", c)[0], 0.0)
        return self.hold(value.astype(jnp.bfloat16), "message", c, s)

    def prefix(self, c, s):
        if s in (0, self.m):
            pairs = [(d, d ^ 1) for d in range(self.n)]
        else:
            pairs = [(2 * (s - 1) + y, 2 * s + y) for y in range(2)]
        return lax.ppermute(self.get("message", c, s), "seq", pairs)

    def mixed(self, c):
        low, width = self.chunks[c]
        near = self.get("prefix", c, 0).astype(jnp.float32)
        own = (self.get("total", c) + jnp.where(self.col == 1, near, 0.0)).astype(jnp.bfloat16)
        oth = self.get("prefix", c, self.m)
        place = self.get("put", c - 2)[1] if c > 1 else self.place
        place = self.hold(place, "mixed", c)
        return attend(place, *self.arrays, self.gain, own, oth, self.n, low, width)

    def sent(self, c, k):
        pairs = [
            (2 * z + y, 2 * ((z + k // 2) % self.m) + (y + k) % 2) for z in range(self.m) for y in range(2)
        ]
        return lax.ppermute(self.hold(self.get("mixed", c)[k], "sent", c, k), "seq", pairs)

    def put(self, c):
        parts = [self.get("mixed", c)[0]] + [self.get("sent", c, k) for k in range(1, self.n)]
        out = self.get("put", c - 1)[0] if c else None
        return put(self.place, parts, out, self.n, self.chunks[c][0])


def per_device(n, *arrays):
    plan = Plan(n, *arrays)
    return plan.get("put", len(plan.chunks) - 1)[0]


def solution(mesh):
    tokens = P(("batch", "seq"), None)
    return jax.shard_map(
        functools.partial(per_device, mesh.shape["seq"]),
        mesh=mesh,
        in_specs=(tokens, tokens, tokens, P()),
        out_specs=P("batch", "seq"),
        check_vma=False,
    )
```

```python
import functools

import jax
import jax.numpy as jnp
from jax import lax
from jax.experimental import pallas as pl
from jax.experimental.pallas import tpu as pltpu
from jax.sharding import PartitionSpec as P

HEADS = 64
HEAD = 128
LOCAL = (2, 6)
PREFIX = (1, 1, 2, 2, 2)
MIXED = (2, 2, 2, 2)
TILE = 256
VMEM = 48 * 1024 * 1024
ORDER = {}


def params():
    return pltpu.CompilerParams(vmem_limit_bytes=VMEM)


def column(place, row, side, n, low):
    col = place[1] if side == 0 else 1 - place[1]
    return pl.multiple_of(((2 * row + col) * (HEADS // n) + low) * HEAD, HEAD)


def local_body(n, low, widths, place, keys, values, *refs):
    outs, (kbuf, vbuf, sems) = refs[:-3], refs[-3:]
    total = sum(widths)
    copies = []
    for slot in range(n):
        cols = pl.ds(column(place, slot // 2, slot % 2, n, low), total * HEAD)
        copies.append(
            [
                pltpu.make_async_copy(source.at[:, cols], buf.at[slot], sems.at[which, slot])
                for which, (source, buf) in enumerate(((keys, kbuf), (values, vbuf)))
            ]
        )
    for pair in copies:
        for copy in pair:
            copy.start()
    for slot in range(n):
        for copy in copies[slot]:
            copy.wait()
        places = [(chunk, head) for chunk, width in enumerate(widths) for head in range(width)]
        for first in range(0, total, 2):
            size = min(2, total - first)
            cols = slice(first * HEAD, (first + size) * HEAD)
            both = lax.dot_general(
                kbuf[slot, :, cols],
                vbuf[slot, :, cols],
                (((0,), (0,)), ((), ())),
                preferred_element_type=jnp.float32,
            )
            for index in range(size):
                chunk, head = places[first + index]
                out = outs[2 * chunk + slot % 2]
                part = slice(index * HEAD, (index + 1) * HEAD)
                out[slot // 2, head] = both[part, part].astype(out.dtype)


def local_states(place, keys, values, n, low, widths):
    rows, m, total = keys.shape[0], n // 2, sum(widths)
    buf = pltpu.VMEM((n, rows, total * HEAD), keys.dtype)
    shapes = [
        jax.ShapeDtypeStruct((m, width, HEAD, HEAD), kind)
        for width in widths
        for kind in (jnp.float32, jnp.bfloat16)
    ]
    return pl.pallas_call(
        functools.partial(local_body, n, low, widths),
        in_specs=[pl.BlockSpec(memory_space=pltpu.SMEM)] + [pl.BlockSpec(memory_space=pl.ANY)] * 2,
        out_specs=[pl.BlockSpec(memory_space=pltpu.VMEM)] * len(shapes),
        out_shape=shapes,
        scratch_shapes=[buf, buf, pltpu.SemaphoreType.DMA((2, n))],
        compiler_params=params(),
        cost_estimate=pl.CostEstimate(
            flops=2 * n * total * rows * HEAD * HEAD, bytes_accessed=4 * rows * n * total * HEAD, transcendentals=0
        ),
        name="local",
    )(place, keys, values)


def masked_scores(query, key):
    rows = query.shape[0]
    tiles = []
    for low in range(0, rows, TILE):
        high = min(low + TILE, rows)
        part = lax.dot_general(
            query[low:], key[low:high], (((1,), (1,)), ((), ())), preferred_element_type=jnp.float32
        )
        size = high - low
        spot = lax.broadcasted_iota(jnp.int32, (size, size), 0)
        other = lax.broadcasted_iota(jnp.int32, (size, size), 1)
        pieces = [jnp.where(other <= spot, part[:size], 0.0).astype(jnp.bfloat16)]
        if low:
            pieces.insert(0, jnp.zeros((low, size), jnp.bfloat16))
        if high < rows:
            pieces.append(part[size:].astype(jnp.bfloat16))
        tiles.append(jnp.concatenate(pieces, axis=0) if len(pieces) > 1 else pieces[0])
    return tiles


def attend_body(n, low, spans, place, queries, keys, values, gain, *refs):
    states, outs = refs[: 2 * len(spans)], refs[2 * len(spans) :][:n]
    qbuf, kbuf, vbuf, sown, soth, gbuf, held, sems, extra = refs[-9:]
    width = sum(size for _, size in spans)
    m = n // 2
    wide = width * HEAD
    spots = [lax.rem(place[0] + row, m) for row in range(m)]
    small, start = [(gain, gbuf)], 0
    for chunk, (skip, size) in enumerate(spans):
        for source, buf in ((states[2 * chunk], sown), (states[2 * chunk + 1], soth)):
            small.append((source.at[:, skip : skip + size], buf.at[:, start : start + size]))
        start += size
    small = [pltpu.make_async_copy(source, buf, extra.at[which]) for which, (source, buf) in enumerate(small)]
    copies = []
    for slot in range(n):
        cols = pl.ds(column(place, spots[slot // 2], slot % 2, n, low), wide)
        copies.append(
            [
                pltpu.make_async_copy(source.at[:, cols], buf.at[slot], sems.at[which, slot])
                for which, (source, buf) in enumerate(((queries, qbuf), (keys, kbuf), (values, vbuf)))
            ]
        )
    for slot in range(n):
        for copy in copies[slot]:
            copy.start()
        if slot == 1:
            for copy in small:
                copy.start()
    sends = [pltpu.make_async_copy(held.at[slot], outs[slot], sems.at[3, slot]) for slot in range(n)]
    group = max(1, 4 // width)
    for first in range(0, n, group):
        slots = range(first, min(first + group, n))
        for slot in slots:
            for copy in copies[slot]:
                copy.wait()
        heads = [(slot, head, slice(head * HEAD, (head + 1) * HEAD)) for slot in slots for head in range(width)]
        scores = [masked_scores(qbuf[slot, :, cols], kbuf[slot, :, cols]) for slot, _, cols in heads]
        if first == 0:
            for copy in small:
                copy.wait()
        attended = []
        for (slot, head, cols), tiles in zip(heads, scores):
            state = (sown if slot % 2 == 0 else soth)[spots[slot // 2], head]
            left = jnp.concatenate([*tiles, qbuf[slot, :, cols]], axis=1)
            right = jnp.concatenate([vbuf[slot, :, cols], state], axis=0)
            attended.append(jnp.dot(left, right, preferred_element_type=jnp.float32))
        for (slot, head, cols), value in zip(heads, attended):
            square = jnp.mean(value * value, axis=-1, keepdims=True)
            start = column(place, spots[slot // 2], slot % 2, n, low + head)
            mixed = value * lax.rsqrt(square + 1e-05) * gbuf[:, pl.ds(start, HEAD)]
            held[slot, :, cols] = mixed.astype(held.dtype)
        for slot in slots:
            sends[slot].start()
    for copy in sends:
        copy.wait()


def attend(place, queries, keys, values, gain, states, spans, n, low):
    rows, m = queries.shape[0], n // 2
    width = sum(size for _, size in spans)
    wide = width * HEAD
    tokens = pltpu.VMEM((n, rows, wide), jnp.bfloat16)
    state = pltpu.VMEM((m, width, HEAD, HEAD), jnp.bfloat16)
    return pl.pallas_call(
        functools.partial(attend_body, n, low, spans),
        in_specs=[pl.BlockSpec(memory_space=pltpu.SMEM)] + [pl.BlockSpec(memory_space=pl.ANY)] * (4 + 2 * len(states)),
        out_specs=[pl.BlockSpec(memory_space=pl.ANY)] * n,
        out_shape=[jax.ShapeDtypeStruct((rows, wide), jnp.bfloat16)] * n,
        scratch_shapes=[
            tokens,
            tokens,
            tokens,
            state,
            state,
            pltpu.VMEM((1, HEADS * HEAD), jnp.float32),
            tokens,
            pltpu.SemaphoreType.DMA((4, n)),
            pltpu.SemaphoreType.DMA((1 + 2 * len(states),)),
        ],
        compiler_params=params(),
        cost_estimate=pl.CostEstimate(
            flops=2 * n * width * rows * HEAD * (2 * rows + HEAD),
            bytes_accessed=8 * rows * n * wide,
            transcendentals=n * width * rows,
        ),
        name="attend",
    )(place, queries, keys, values, gain, *(array for pair in states for array in pair))


def put_body(n, low, place, *refs):
    parts, out, again, sems = refs[:n], refs[-3], refs[-2], refs[-1]
    m = n // 2
    rows, wide = parts[0].shape
    copies = []
    for shift in range(n):
        row = lax.rem(place[0] + m - shift // 2, m)
        col = place[1] if shift % 2 == 0 else 1 - place[1]
        start = pl.multiple_of((2 * row + col) * rows, rows)
        copies.append(
            pltpu.make_async_copy(
                parts[shift], out.at[pl.ds(start, rows), pl.ds(low * HEAD, wide)], sems.at[shift]
            )
        )
    for copy in copies:
        copy.start()
    for index in range(2):
        again[index] = place[index]
    for copy in copies:
        copy.wait()


def put(place, parts, out, n, low):
    rows, first = parts[0].shape[0], out is None
    anywhere = pl.BlockSpec(memory_space=pl.ANY)
    return pl.pallas_call(
        functools.partial(put_body, n, low),
        in_specs=[pl.BlockSpec(memory_space=pltpu.SMEM)] + [anywhere] * (n if first else n + 1),
        out_specs=[anywhere, pl.BlockSpec(memory_space=pltpu.SMEM)],
        out_shape=[
            jax.ShapeDtypeStruct((n * rows, HEADS // n * HEAD), jnp.bfloat16),
            jax.ShapeDtypeStruct((2,), jnp.int32),
        ],
        scratch_shapes=[pltpu.SemaphoreType.DMA((n,))],
        input_output_aliases={} if first else {n + 1: 0},
        compiler_params=params(),
        name="put",
    )(place, *parts, *(() if first else (out,)))


def split(widths, per_dest):
    chunks, low = [], 0
    for width in widths:
        if low < per_dest:
            width = min(width, per_dest - low)
            chunks.append((low, width))
            low += width
    return chunks


def inside(chunks, low, width):
    return [c for c, (start, _) in enumerate(chunks) if low <= start < low + width]


class Plan:
    def __init__(self, n, queries, keys, values, gain):
        self.n, self.m = n, n // 2
        me = lax.axis_index("seq")
        self.col = me % 2
        self.place = jnp.stack([me // 2, self.col]).astype(jnp.int32)
        self.arrays = queries, keys, values
        self.gain = gain.reshape(1, HEADS * HEAD)
        self.groups, self.parts, self.chunks = (split(widths, HEADS // n) for widths in (LOCAL, PREFIX, MIXED))
        self.made = {}

    def has(self, key):
        limit = {"message": self.m, "prefix": self.m, "sent": self.n - 1}.get(key[0], 0)
        chunks = {"group": self.groups, "mixed": self.chunks, "sent": self.chunks}.get(key[0], self.parts)
        return key[1] < len(chunks) and (len(key) < 3 or key[2] <= limit)

    def get(self, *key):
        if key not in self.made:
            self.made[key] = getattr(self, key[0])(*key[1:])
        return self.made[key]

    def hold(self, value, *key):
        others = []
        for other in ORDER.get(key, ()):
            if self.has(other):
                result = self.get(*other)
                others.append(result[1] if other[0] == "mixed" else result)
        return lax.optimization_barrier((value, *others))[0] if others else value

    def group(self, g):
        low, width = self.groups[g]
        widths = tuple(self.parts[c][1] for c in inside(self.parts, low, width))
        _, keys, values = self.arrays
        return local_states(self.hold(self.place, "group", g), keys, values, self.n, low, widths)

    def local(self, c):
        for g, group in enumerate(self.groups):
            members = inside(self.parts, *group)
            if c in members:
                spot = 2 * members.index(c)
                return self.get("group", g)[spot : spot + 2]

    def both(self, c):
        return self.get("local", c)[0] + self.get("prefix", c, 0).astype(jnp.float32)

    def total(self, c):
        parts = [self.get("prefix", c, s) for s in range(1, self.m)]
        return sum(parts[1:], parts[0]).astype(jnp.float32)

    def message(self, c, s):
        if s == 0:
            value = self.get("local", c)[1]
        elif s < self.m:
            value = self.get("both", c)
            if s > 1:
                value = self.get("prefix", c, s - 1).astype(jnp.float32) + value
        else:
            value = self.get("total", c) + jnp.where(self.col == 0, self.get("local", c)[0], 0.0)
        return self.hold(value.astype(jnp.bfloat16), "message", c, s)

    def prefix(self, c, s):
        if s in (0, self.m):
            pairs = [(d, d ^ 1) for d in range(self.n)]
        else:
            pairs = [(2 * (s - 1) + y, 2 * s + y) for y in range(2)]
        return lax.ppermute(self.get("message", c, s), "seq", pairs)

    def states(self, c):
        near = self.get("prefix", c, 0).astype(jnp.float32)
        own = (self.get("total", c) + jnp.where(self.col == 1, near, 0.0)).astype(jnp.bfloat16)
        return own, self.get("prefix", c, self.m)

    def mixed(self, c):
        low, width = self.chunks[c]
        place = self.get("put", c - 3)[1] if c > 2 else self.place
        place = self.hold(place, "mixed", c)
        states, spans = [], []
        for part, (start, size) in enumerate(self.parts):
            first, last = max(low, start), min(low + width, start + size)
            if first < last:
                states.append(self.get("states", part))
                spans.append((first - start, last - first))
        return attend(place, *self.arrays, self.gain, states, tuple(spans), self.n, low)

    def sent(self, c, k):
        pairs = [
            (2 * z + y, 2 * ((z + k // 2) % self.m) + (y + k) % 2) for z in range(self.m) for y in range(2)
        ]
        return lax.ppermute(self.hold(self.get("mixed", c)[k], "sent", c, k), "seq", pairs)

    def put(self, c):
        parts = [self.get("mixed", c)[0]] + [self.get("sent", c, k) for k in range(1, self.n)]
        out = self.get("put", c - 1)[0] if c else None
        return put(self.place, parts, out, self.n, self.chunks[c][0])


def per_device(n, *arrays):
    plan = Plan(n, *arrays)
    return plan.get("put", len(plan.chunks) - 1)[0]


def solution(mesh):
    tokens = P(("batch", "seq"), None)
    return jax.shard_map(
        functools.partial(per_device, mesh.shape["seq"]),
        mesh=mesh,
        in_specs=(tokens, tokens, tokens, P()),
        out_specs=P("batch", "seq"),
        check_vma=False,
    )
```

```python
import functools

import jax
import jax.numpy as jnp
from jax import lax
from jax.experimental import pallas as pl
from jax.experimental.pallas import tpu as pltpu
from jax.sharding import PartitionSpec as P

HEADS = 64
HEAD = 128
LOCAL = (2, 6)
PREFIX = (1, 1, 2, 2, 2)
MIXED = (2, 2, 2, 2)
TILE = 256
SPARE = 8 * 1024 * 1024
ORDER = {
    ("message", 2, 0): [("message", 0, 1), ("message", 1, 1)],
    ("message", 3, 0): [("message", 0, 1), ("message", 1, 1)],
    ("message", 4, 0): [("message", 0, 1), ("message", 1, 1)],
    ("mixed", 0): [("message", 2, 4), ("message", 3, 3), ("message", 4, 2)],
}


def params(buffers=0):
    return pltpu.CompilerParams(vmem_limit_bytes=buffers + SPARE)


def column(place, row, side, n, low):
    col = place[1] if side == 0 else 1 - place[1]
    return pl.multiple_of(((2 * row + col) * (HEADS // n) + low) * HEAD, HEAD)


def local_body(n, low, widths, place, keys, values, *refs):
    outs, (kbuf, vbuf, sems) = refs[:-3], refs[-3:]
    total = sum(widths)
    copies = []
    for slot in range(n):
        cols = pl.ds(column(place, slot // 2, slot % 2, n, low), total * HEAD)
        copies.append(
            [
                pltpu.make_async_copy(source.at[:, cols], buf.at[slot], sems.at[which, slot])
                for which, (source, buf) in enumerate(((keys, kbuf), (values, vbuf)))
            ]
        )
    for pair in copies:
        for copy in pair:
            copy.start()
    for slot in range(n):
        for copy in copies[slot]:
            copy.wait()
        places = [(chunk, head) for chunk, width in enumerate(widths) for head in range(width)]
        for first in range(0, total, 2):
            size = min(2, total - first)
            cols = slice(first * HEAD, (first + size) * HEAD)
            both = lax.dot_general(
                kbuf[slot, :, cols],
                vbuf[slot, :, cols],
                (((0,), (0,)), ((), ())),
                preferred_element_type=jnp.float32,
            )
            for index in range(size):
                chunk, head = places[first + index]
                out = outs[2 * chunk + slot % 2]
                part = slice(index * HEAD, (index + 1) * HEAD)
                out[slot // 2, head] = both[part, part].astype(out.dtype)


def local_states(place, keys, values, n, low, widths):
    rows, m, total = keys.shape[0], n // 2, sum(widths)
    buf = pltpu.VMEM((n, rows, total * HEAD), keys.dtype)
    shapes = [
        jax.ShapeDtypeStruct((m, width, HEAD, HEAD), kind)
        for width in widths
        for kind in (jnp.float32, jnp.bfloat16)
    ]
    return pl.pallas_call(
        functools.partial(local_body, n, low, widths),
        in_specs=[pl.BlockSpec(memory_space=pltpu.SMEM)] + [pl.BlockSpec(memory_space=pl.ANY)] * 2,
        out_specs=[pl.BlockSpec(memory_space=pltpu.VMEM)] * len(shapes),
        out_shape=shapes,
        scratch_shapes=[buf, buf, pltpu.SemaphoreType.DMA((2, n))],
        compiler_params=params(4 * n * rows * total * HEAD + 3 * n * total * HEAD * HEAD),
        cost_estimate=pl.CostEstimate(
            flops=2 * n * total * rows * HEAD * HEAD, bytes_accessed=4 * rows * n * total * HEAD, transcendentals=0
        ),
        name="local",
    )(place, keys, values)


def masked_scores(query, key):
    rows = query.shape[0]
    tiles = []
    for low in range(0, rows, TILE):
        high = min(low + TILE, rows)
        part = lax.dot_general(
            query[low:], key[low:high], (((1,), (1,)), ((), ())), preferred_element_type=jnp.float32
        )
        size = high - low
        spot = lax.broadcasted_iota(jnp.int32, (size, size), 0)
        other = lax.broadcasted_iota(jnp.int32, (size, size), 1)
        pieces = [jnp.where(other <= spot, part[:size], 0.0).astype(jnp.bfloat16)]
        if low:
            pieces.insert(0, jnp.zeros((low, size), jnp.bfloat16))
        if high < rows:
            pieces.append(part[size:].astype(jnp.bfloat16))
        tiles.append(jnp.concatenate(pieces, axis=0) if len(pieces) > 1 else pieces[0])
    return tiles


def attend_body(n, low, spans, place, queries, keys, values, gain, *refs):
    states, outs = refs[: 2 * len(spans)], refs[2 * len(spans) :][:n]
    qbuf, kbuf, vbuf, sown, soth, gbuf, held, sems, extra = refs[-9:]
    width = sum(size for _, size in spans)
    m = n // 2
    wide = width * HEAD
    spots = [lax.rem(place[0] + row, m) for row in range(m)]
    small, start = [(gain, gbuf)], 0
    for chunk, (skip, size) in enumerate(spans):
        for source, buf in ((states[2 * chunk], sown), (states[2 * chunk + 1], soth)):
            small.append((source.at[:, skip : skip + size], buf.at[:, start : start + size]))
        start += size
    small = [pltpu.make_async_copy(source, buf, extra.at[which]) for which, (source, buf) in enumerate(small)]
    copies = []
    for slot in range(n):
        cols = pl.ds(column(place, spots[slot // 2], slot % 2, n, low), wide)
        copies.append(
            [
                pltpu.make_async_copy(source.at[:, cols], buf.at[slot], sems.at[which, slot])
                for which, (source, buf) in enumerate(((queries, qbuf), (keys, kbuf), (values, vbuf)))
            ]
        )
    for slot in range(n):
        for copy in copies[slot]:
            copy.start()
        if slot == 1:
            for copy in small:
                copy.start()
    sends = [pltpu.make_async_copy(held.at[slot], outs[slot], sems.at[3, slot]) for slot in range(n)]
    group = max(1, 4 // width)
    for first in range(0, n, group):
        slots = range(first, min(first + group, n))
        for slot in slots:
            for copy in copies[slot]:
                copy.wait()
        heads = [(slot, head, slice(head * HEAD, (head + 1) * HEAD)) for slot in slots for head in range(width)]
        scores = [masked_scores(qbuf[slot, :, cols], kbuf[slot, :, cols]) for slot, _, cols in heads]
        if first == 0:
            for copy in small:
                copy.wait()
        attended = []
        for (slot, head, cols), tiles in zip(heads, scores):
            state = (sown if slot % 2 == 0 else soth)[spots[slot // 2], head]
            left = jnp.concatenate([*tiles, qbuf[slot, :, cols]], axis=1)
            right = jnp.concatenate([vbuf[slot, :, cols], state], axis=0)
            attended.append(jnp.dot(left, right, preferred_element_type=jnp.float32))
        for (slot, head, cols), value in zip(heads, attended):
            square = jnp.mean(value * value, axis=-1, keepdims=True)
            start = column(place, spots[slot // 2], slot % 2, n, low + head)
            mixed = value * lax.rsqrt(square + 1e-05) * gbuf[:, pl.ds(start, HEAD)]
            held[slot, :, cols] = mixed.astype(held.dtype)
        for slot in slots:
            sends[slot].start()
    for copy in sends:
        copy.wait()


def attend(place, queries, keys, values, gain, states, spans, n, low):
    rows, m = queries.shape[0], n // 2
    width = sum(size for _, size in spans)
    wide = width * HEAD
    tokens = pltpu.VMEM((n, rows, wide), jnp.bfloat16)
    state = pltpu.VMEM((m, width, HEAD, HEAD), jnp.bfloat16)
    return pl.pallas_call(
        functools.partial(attend_body, n, low, spans),
        in_specs=[pl.BlockSpec(memory_space=pltpu.SMEM)] + [pl.BlockSpec(memory_space=pl.ANY)] * (4 + 2 * len(states)),
        out_specs=[pl.BlockSpec(memory_space=pl.ANY)] * n,
        out_shape=[jax.ShapeDtypeStruct((rows, wide), jnp.bfloat16)] * n,
        scratch_shapes=[
            tokens,
            tokens,
            tokens,
            state,
            state,
            pltpu.VMEM((1, HEADS * HEAD), jnp.float32),
            tokens,
            pltpu.SemaphoreType.DMA((4, n)),
            pltpu.SemaphoreType.DMA((1 + 2 * len(states),)),
        ],
        compiler_params=params(8 * n * rows * wide + 2 * n * width * HEAD * HEAD + 4 * HEADS * HEAD),
        cost_estimate=pl.CostEstimate(
            flops=2 * n * width * rows * HEAD * (2 * rows + HEAD),
            bytes_accessed=8 * rows * n * wide,
            transcendentals=n * width * rows,
        ),
        name="attend",
    )(place, queries, keys, values, gain, *(array for pair in states for array in pair))


def put_body(n, low, place, *refs):
    parts, out, again, sems = refs[:n], refs[-3], refs[-2], refs[-1]
    m = n // 2
    rows, wide = parts[0].shape
    copies = []
    for shift in range(n):
        row = lax.rem(place[0] + m - shift // 2, m)
        col = place[1] if shift % 2 == 0 else 1 - place[1]
        start = pl.multiple_of((2 * row + col) * rows, rows)
        copies.append(
            pltpu.make_async_copy(
                parts[shift], out.at[pl.ds(start, rows), pl.ds(low * HEAD, wide)], sems.at[shift]
            )
        )
    for copy in copies:
        copy.start()
    for index in range(2):
        again[index] = place[index]
    for copy in copies:
        copy.wait()


def put(place, parts, out, n, low):
    rows, first = parts[0].shape[0], out is None
    anywhere = pl.BlockSpec(memory_space=pl.ANY)
    return pl.pallas_call(
        functools.partial(put_body, n, low),
        in_specs=[pl.BlockSpec(memory_space=pltpu.SMEM)] + [anywhere] * (n if first else n + 1),
        out_specs=[anywhere, pl.BlockSpec(memory_space=pltpu.SMEM)],
        out_shape=[
            jax.ShapeDtypeStruct((n * rows, HEADS // n * HEAD), jnp.bfloat16),
            jax.ShapeDtypeStruct((2,), jnp.int32),
        ],
        scratch_shapes=[pltpu.SemaphoreType.DMA((n,))],
        input_output_aliases={} if first else {n + 1: 0},
        compiler_params=params(),
        name="put",
    )(place, *parts, *(() if first else (out,)))


def split(widths, per_dest):
    chunks, low = [], 0
    for width in widths:
        if low < per_dest:
            width = min(width, per_dest - low)
            chunks.append((low, width))
            low += width
    return chunks


def inside(chunks, low, width):
    return [c for c, (start, _) in enumerate(chunks) if low <= start < low + width]


class Plan:
    def __init__(self, n, queries, keys, values, gain):
        self.n, self.m = n, n // 2
        me = lax.axis_index("seq")
        self.col = me % 2
        self.place = jnp.stack([me // 2, self.col]).astype(jnp.int32)
        self.arrays = queries, keys, values
        self.gain = gain.reshape(1, HEADS * HEAD)
        self.groups, self.parts, self.chunks = (split(widths, HEADS // n) for widths in (LOCAL, PREFIX, MIXED))
        self.made = {}

    def has(self, key):
        limit = {"message": self.m, "prefix": self.m, "sent": self.n - 1}.get(key[0], 0)
        chunks = {"group": self.groups, "mixed": self.chunks, "sent": self.chunks}.get(key[0], self.parts)
        return key[1] < len(chunks) and (len(key) < 3 or key[2] <= limit)

    def get(self, *key):
        if key not in self.made:
            self.made[key] = getattr(self, key[0])(*key[1:])
        return self.made[key]

    def hold(self, value, *key):
        others = []
        for other in ORDER.get(key, ()):
            if self.has(other):
                result = self.get(*other)
                others.append(result[1] if other[0] == "mixed" else result)
        return lax.optimization_barrier((value, *others))[0] if others else value

    def group(self, g):
        low, width = self.groups[g]
        widths = tuple(self.parts[c][1] for c in inside(self.parts, low, width))
        _, keys, values = self.arrays
        return local_states(self.hold(self.place, "group", g), keys, values, self.n, low, widths)

    def local(self, c):
        for g, group in enumerate(self.groups):
            members = inside(self.parts, *group)
            if c in members:
                spot = 2 * members.index(c)
                return self.get("group", g)[spot : spot + 2]

    def both(self, c):
        return self.get("local", c)[0] + self.get("prefix", c, 0).astype(jnp.float32)

    def total(self, c):
        parts = [self.get("prefix", c, s) for s in range(1, self.m)]
        return sum(parts[1:], parts[0]).astype(jnp.float32)

    def message(self, c, s):
        if s == 0:
            value = self.get("local", c)[1]
        elif s < self.m:
            value = self.get("both", c)
            if s > 1:
                value = self.get("prefix", c, s - 1).astype(jnp.float32) + value
        else:
            value = self.get("total", c) + jnp.where(self.col == 0, self.get("local", c)[0], 0.0)
        return self.hold(value.astype(jnp.bfloat16), "message", c, s)

    def prefix(self, c, s):
        if s in (0, self.m):
            pairs = [(d, d ^ 1) for d in range(self.n)]
        else:
            pairs = [(2 * (s - 1) + y, 2 * s + y) for y in range(2)]
        return lax.ppermute(self.get("message", c, s), "seq", pairs)

    def states(self, c):
        near = self.get("prefix", c, 0).astype(jnp.float32)
        own = (self.get("total", c) + jnp.where(self.col == 1, near, 0.0)).astype(jnp.bfloat16)
        return own, self.get("prefix", c, self.m)

    def mixed(self, c):
        low, width = self.chunks[c]
        place = self.get("put", c - 3)[1] if c > 2 else self.place
        place = self.hold(place, "mixed", c)
        states, spans = [], []
        for part, (start, size) in enumerate(self.parts):
            first, last = max(low, start), min(low + width, start + size)
            if first < last:
                states.append(self.get("states", part))
                spans.append((first - start, last - first))
        return attend(place, *self.arrays, self.gain, states, tuple(spans), self.n, low)

    def sent(self, c, k):
        pairs = [
            (2 * z + y, 2 * ((z + k // 2) % self.m) + (y + k) % 2) for z in range(self.m) for y in range(2)
        ]
        return lax.ppermute(self.hold(self.get("mixed", c)[k], "sent", c, k), "seq", pairs)

    def put(self, c):
        parts = [self.get("mixed", c)[0]] + [self.get("sent", c, k) for k in range(1, self.n)]
        out = self.get("put", c - 1)[0] if c else None
        return put(self.place, parts, out, self.n, self.chunks[c][0])


def per_device(n, *arrays):
    plan = Plan(n, *arrays)
    return plan.get("put", len(plan.chunks) - 1)[0]


def solution(mesh):
    tokens = P(("batch", "seq"), None)
    return jax.shard_map(
        functools.partial(per_device, mesh.shape["seq"]),
        mesh=mesh,
        in_specs=(tokens, tokens, tokens, P()),
        out_specs=P("batch", "seq"),
        check_vma=False,
    )
```

```python
import functools

import jax
import jax.numpy as jnp
from jax import lax
from jax.experimental import pallas as pl
from jax.experimental.pallas import tpu as pltpu
from jax.sharding import PartitionSpec as P

HEADS = 64
HEAD = 128
LOCAL = (2, 6)
PREFIX = (1, 1, 2, 2, 2)
MIXED = (2, 2, 2, 2)
TILE = 256
SPARE = 8 * 1024 * 1024
ORDER = {
    ("message", 1, 0): [("message", 0, 0)],
    ("message", 2, 0): [("message", 1, 0)],
    ("message", 3, 0): [("message", 2, 0)],
    ("message", 4, 0): [("message", 3, 0)],
    ("message", 1, 1): [("message", 0, 1)],
    ("message", 1, 2): [("message", 0, 2)],
    ("message", 1, 3): [("message", 0, 3)],
    ("message", 1, 4): [("message", 0, 4)],
    ("message", 2, 1): [("message", 1, 1)],
    ("message", 2, 2): [("message", 1, 2)],
    ("message", 2, 3): [("message", 1, 3)],
    ("message", 2, 4): [("message", 1, 4)],
    ("message", 3, 1): [("message", 2, 1)],
    ("message", 3, 2): [("message", 2, 2)],
    ("message", 3, 3): [("message", 2, 3)],
    ("message", 3, 4): [("message", 2, 4)],
    ("message", 4, 1): [("message", 3, 1)],
    ("message", 4, 2): [("message", 3, 2)],
    ("message", 4, 3): [("message", 3, 3)],
    ("message", 4, 4): [("message", 3, 4)],
    ("mixed", 0): [("message", 2, 4), ("message", 3, 3), ("message", 4, 2)],
}


def params(buffers=0):
    return pltpu.CompilerParams(vmem_limit_bytes=buffers + SPARE)


def column(place, row, side, n, low):
    col = place[1] if side == 0 else 1 - place[1]
    return pl.multiple_of(((2 * row + col) * (HEADS // n) + low) * HEAD, HEAD)


def local_body(n, low, widths, place, keys, values, *refs):
    outs, (kbuf, vbuf, sems) = refs[:-3], refs[-3:]
    total = sum(widths)
    copies = []
    for slot in range(n):
        cols = pl.ds(column(place, slot // 2, slot % 2, n, low), total * HEAD)
        copies.append(
            [
                pltpu.make_async_copy(source.at[:, cols], buf.at[slot], sems.at[which, slot])
                for which, (source, buf) in enumerate(((keys, kbuf), (values, vbuf)))
            ]
        )
    for pair in copies:
        for copy in pair:
            copy.start()
    for slot in range(n):
        for copy in copies[slot]:
            copy.wait()
        places = [(chunk, head) for chunk, width in enumerate(widths) for head in range(width)]
        for first in range(0, total, 2):
            size = min(2, total - first)
            cols = slice(first * HEAD, (first + size) * HEAD)
            both = lax.dot_general(
                kbuf[slot, :, cols],
                vbuf[slot, :, cols],
                (((0,), (0,)), ((), ())),
                preferred_element_type=jnp.float32,
            )
            for index in range(size):
                chunk, head = places[first + index]
                out = outs[2 * chunk + slot % 2]
                part = slice(index * HEAD, (index + 1) * HEAD)
                out[slot // 2, head] = both[part, part].astype(out.dtype)


def local_states(place, keys, values, n, low, widths):
    rows, m, total = keys.shape[0], n // 2, sum(widths)
    buf = pltpu.VMEM((n, rows, total * HEAD), keys.dtype)
    shapes = [
        jax.ShapeDtypeStruct((m, width, HEAD, HEAD), kind)
        for width in widths
        for kind in (jnp.float32, jnp.bfloat16)
    ]
    return pl.pallas_call(
        functools.partial(local_body, n, low, widths),
        in_specs=[pl.BlockSpec(memory_space=pltpu.SMEM)] + [pl.BlockSpec(memory_space=pltpu.HBM)] * 2,
        out_specs=[pl.BlockSpec(memory_space=pltpu.VMEM)] * len(shapes),
        out_shape=shapes,
        scratch_shapes=[buf, buf, pltpu.SemaphoreType.DMA((2, n))],
        compiler_params=params(4 * n * rows * total * HEAD + 3 * n * total * HEAD * HEAD),
        cost_estimate=pl.CostEstimate(
            flops=2 * n * total * rows * HEAD * HEAD, bytes_accessed=4 * rows * n * total * HEAD, transcendentals=0
        ),
        name="local",
    )(place, keys, values)


def masked_scores(query, key):
    rows = query.shape[0]
    tiles = []
    for low in range(0, rows, TILE):
        high = min(low + TILE, rows)
        part = lax.dot_general(
            query[low:], key[low:high], (((1,), (1,)), ((), ())), preferred_element_type=jnp.float32
        )
        size = high - low
        spot = lax.broadcasted_iota(jnp.int32, (size, size), 0)
        other = lax.broadcasted_iota(jnp.int32, (size, size), 1)
        pieces = [jnp.where(other <= spot, part[:size], 0.0).astype(jnp.bfloat16)]
        if low:
            pieces.insert(0, jnp.zeros((low, size), jnp.bfloat16))
        if high < rows:
            pieces.append(part[size:].astype(jnp.bfloat16))
        tiles.append(jnp.concatenate(pieces, axis=0) if len(pieces) > 1 else pieces[0])
    return tiles


def attend_body(n, low, spans, place, queries, keys, values, gain, *refs):
    states, outs = refs[: 2 * len(spans)], refs[2 * len(spans) :][:n]
    qbuf, kbuf, vbuf, sown, soth, gbuf, held, sems, extra = refs[-9:]
    width = sum(size for _, size in spans)
    m = n // 2
    wide = width * HEAD
    spots = [lax.rem(place[0] + row, m) for row in range(m)]
    small, start = [(gain, gbuf)], 0
    for chunk, (skip, size) in enumerate(spans):
        for source, buf in ((states[2 * chunk], sown), (states[2 * chunk + 1], soth)):
            small.append((source.at[:, skip : skip + size], buf.at[:, start : start + size]))
        start += size
    small = [pltpu.make_async_copy(source, buf, extra.at[which]) for which, (source, buf) in enumerate(small)]
    copies = []
    for slot in range(n):
        cols = pl.ds(column(place, spots[slot // 2], slot % 2, n, low), wide)
        copies.append(
            [
                pltpu.make_async_copy(source.at[:, cols], buf.at[slot], sems.at[which, slot])
                for which, (source, buf) in enumerate(((queries, qbuf), (keys, kbuf), (values, vbuf)))
            ]
        )
    for slot in range(n):
        for copy in copies[slot]:
            copy.start()
        if slot == 1:
            for copy in small:
                copy.start()
    sends = [pltpu.make_async_copy(held.at[slot], outs[slot], sems.at[3, slot]) for slot in range(n)]
    group = max(1, 4 // width)
    for first in range(0, n, group):
        slots = range(first, min(first + group, n))
        for slot in slots:
            for copy in copies[slot]:
                copy.wait()
        heads = [(slot, head, slice(head * HEAD, (head + 1) * HEAD)) for slot in slots for head in range(width)]
        scores = [masked_scores(qbuf[slot, :, cols], kbuf[slot, :, cols]) for slot, _, cols in heads]
        if first == 0:
            for copy in small:
                copy.wait()
        attended = []
        for (slot, head, cols), tiles in zip(heads, scores):
            state = (sown if slot % 2 == 0 else soth)[spots[slot // 2], head]
            left = jnp.concatenate([*tiles, qbuf[slot, :, cols]], axis=1)
            right = jnp.concatenate([vbuf[slot, :, cols], state], axis=0)
            attended.append(jnp.dot(left, right, preferred_element_type=jnp.float32))
        for (slot, head, cols), value in zip(heads, attended):
            square = jnp.mean(value * value, axis=-1, keepdims=True)
            start = column(place, spots[slot // 2], slot % 2, n, low + head)
            mixed = value * lax.rsqrt(square + 1e-05) * gbuf[:, pl.ds(start, HEAD)]
            held[slot, :, cols] = mixed.astype(held.dtype)
        for slot in slots:
            sends[slot].start()
    for copy in sends:
        copy.wait()


def attend(place, queries, keys, values, gain, states, spans, n, low):
    rows, m = queries.shape[0], n // 2
    width = sum(size for _, size in spans)
    wide = width * HEAD
    tokens = pltpu.VMEM((n, rows, wide), jnp.bfloat16)
    state = pltpu.VMEM((m, width, HEAD, HEAD), jnp.bfloat16)
    return pl.pallas_call(
        functools.partial(attend_body, n, low, spans),
        in_specs=[pl.BlockSpec(memory_space=pltpu.SMEM)]
        + [pl.BlockSpec(memory_space=pltpu.HBM)] * 3
        + [pl.BlockSpec(memory_space=pl.ANY)] * (1 + 2 * len(states)),
        out_specs=[pl.BlockSpec(memory_space=pltpu.HBM)] * n,
        out_shape=[jax.ShapeDtypeStruct((rows, wide), jnp.bfloat16)] * n,
        scratch_shapes=[
            tokens,
            tokens,
            tokens,
            state,
            state,
            pltpu.VMEM((1, HEADS * HEAD), jnp.float32),
            tokens,
            pltpu.SemaphoreType.DMA((4, n)),
            pltpu.SemaphoreType.DMA((1 + 2 * len(states),)),
        ],
        compiler_params=params(8 * n * rows * wide + 2 * n * width * HEAD * HEAD + 4 * HEADS * HEAD),
        cost_estimate=pl.CostEstimate(
            flops=2 * n * width * rows * HEAD * (2 * rows + HEAD),
            bytes_accessed=8 * rows * n * wide,
            transcendentals=n * width * rows,
        ),
        name="attend",
    )(place, queries, keys, values, gain, *(array for pair in states for array in pair))


def put_body(n, low, place, *refs):
    parts, out, again, sems = refs[:n], refs[-3], refs[-2], refs[-1]
    m = n // 2
    rows, wide = parts[0].shape
    copies = []
    for shift in range(n):
        row = lax.rem(place[0] + m - shift // 2, m)
        col = place[1] if shift % 2 == 0 else 1 - place[1]
        start = pl.multiple_of((2 * row + col) * rows, rows)
        copies.append(
            pltpu.make_async_copy(
                parts[shift], out.at[pl.ds(start, rows), pl.ds(low * HEAD, wide)], sems.at[shift]
            )
        )
    for copy in copies:
        copy.start()
    for index in range(2):
        again[index] = place[index]
    for copy in copies:
        copy.wait()


def put(place, parts, out, n, low):
    rows, first = parts[0].shape[0], out is None
    anywhere = pl.BlockSpec(memory_space=pltpu.HBM)
    return pl.pallas_call(
        functools.partial(put_body, n, low),
        in_specs=[pl.BlockSpec(memory_space=pltpu.SMEM)] + [anywhere] * (n if first else n + 1),
        out_specs=[anywhere, pl.BlockSpec(memory_space=pltpu.SMEM)],
        out_shape=[
            jax.ShapeDtypeStruct((n * rows, HEADS // n * HEAD), jnp.bfloat16),
            jax.ShapeDtypeStruct((2,), jnp.int32),
        ],
        scratch_shapes=[pltpu.SemaphoreType.DMA((n,))],
        input_output_aliases={} if first else {n + 1: 0},
        compiler_params=params(),
        name="put",
    )(place, *parts, *(() if first else (out,)))


def split(widths, per_dest):
    chunks, low = [], 0
    for width in widths:
        if low < per_dest:
            width = min(width, per_dest - low)
            chunks.append((low, width))
            low += width
    return chunks


def inside(chunks, low, width):
    return [c for c, (start, _) in enumerate(chunks) if low <= start < low + width]


class Plan:
    def __init__(self, n, queries, keys, values, gain):
        self.n, self.m = n, n // 2
        me = lax.axis_index("seq")
        self.col = me % 2
        self.place = jnp.stack([me // 2, self.col]).astype(jnp.int32)
        self.arrays = tuple(pltpu.with_memory_space_constraint(x, pltpu.HBM) for x in (queries, keys, values))
        self.gain = gain.reshape(1, HEADS * HEAD)
        self.groups, self.parts, self.chunks = (split(widths, HEADS // n) for widths in (LOCAL, PREFIX, MIXED))
        self.made = {}

    def has(self, key):
        limit = {"message": self.m, "prefix": self.m, "sent": self.n - 1}.get(key[0], 0)
        chunks = {"group": self.groups, "mixed": self.chunks, "sent": self.chunks}.get(key[0], self.parts)
        return key[1] < len(chunks) and (len(key) < 3 or key[2] <= limit)

    def get(self, *key):
        if key not in self.made:
            self.made[key] = getattr(self, key[0])(*key[1:])
        return self.made[key]

    def hold(self, value, *key):
        others = []
        for other in ORDER.get(key, ()):
            if self.has(other):
                result = self.get(*other)
                others.append(result[1] if other[0] == "mixed" else result)
        return lax.optimization_barrier((value, *others))[0] if others else value

    def group(self, g):
        low, width = self.groups[g]
        widths = tuple(self.parts[c][1] for c in inside(self.parts, low, width))
        _, keys, values = self.arrays
        return local_states(self.hold(self.place, "group", g), keys, values, self.n, low, widths)

    def local(self, c):
        for g, group in enumerate(self.groups):
            members = inside(self.parts, *group)
            if c in members:
                spot = 2 * members.index(c)
                return self.get("group", g)[spot : spot + 2]

    def both(self, c):
        return self.get("local", c)[0] + self.get("prefix", c, 0).astype(jnp.float32)

    def total(self, c):
        parts = [self.get("prefix", c, s) for s in range(1, self.m)]
        return sum(parts[1:], parts[0]).astype(jnp.float32)

    def message(self, c, s):
        if s == 0:
            value = self.get("local", c)[1]
        elif s < self.m:
            value = self.get("both", c)
            if s > 1:
                value = self.get("prefix", c, s - 1).astype(jnp.float32) + value
        else:
            value = self.get("total", c) + jnp.where(self.col == 0, self.get("local", c)[0], 0.0)
        return self.hold(value.astype(jnp.bfloat16), "message", c, s)

    def prefix(self, c, s):
        if s in (0, self.m):
            pairs = [(d, d ^ 1) for d in range(self.n)]
        else:
            pairs = [(2 * (s - 1) + y, 2 * s + y) for y in range(2)]
        return lax.ppermute(self.get("message", c, s), "seq", pairs)

    def states(self, c):
        near = self.get("prefix", c, 0).astype(jnp.float32)
        own = (self.get("total", c) + jnp.where(self.col == 1, near, 0.0)).astype(jnp.bfloat16)
        return own, self.get("prefix", c, self.m)

    def mixed(self, c):
        low, width = self.chunks[c]
        place = self.get("put", c - 3)[1] if c > 2 else self.place
        place = self.hold(place, "mixed", c)
        states, spans = [], []
        for part, (start, size) in enumerate(self.parts):
            first, last = max(low, start), min(low + width, start + size)
            if first < last:
                states.append(self.get("states", part))
                spans.append((first - start, last - first))
        return attend(place, *self.arrays, self.gain, states, tuple(spans), self.n, low)

    def sent(self, c, k):
        pairs = [
            (2 * z + y, 2 * ((z + k // 2) % self.m) + (y + k) % 2) for z in range(self.m) for y in range(2)
        ]
        return lax.ppermute(self.hold(self.get("mixed", c)[k], "sent", c, k), "seq", pairs)

    def put(self, c):
        parts = [self.get("mixed", c)[0]] + [self.get("sent", c, k) for k in range(1, self.n)]
        out = self.get("put", c - 1)[0] if c else None
        return put(self.place, parts, out, self.n, self.chunks[c][0])


def per_device(n, *arrays):
    plan = Plan(n, *arrays)
    return plan.get("put", len(plan.chunks) - 1)[0]


def solution(mesh):
    tokens = P(("batch", "seq"), None)
    return jax.shard_map(
        functools.partial(per_device, mesh.shape["seq"]),
        mesh=mesh,
        in_specs=(tokens, tokens, tokens, P()),
        out_specs=P("batch", "seq"),
        check_vma=False,
    )
```

```python
import functools

import jax
import jax.numpy as jnp
from jax import lax
from jax.experimental import pallas as pl
from jax.experimental.pallas import tpu as pltpu
from jax.sharding import PartitionSpec as P

HEADS = 64
HEAD = 128
LOCAL = (2, 6)
SWAP = (1, 1, 3, 3)
PREFIX = (1, 1, 3, 3)
MIXED = (2, 3, 3)
TILE = 256
SPARE = 8 * 1024 * 1024
ORDER = {
    ("message", 1, 1): [("message", 0, 1)],
    ("message", 1, 2): [("message", 0, 2)],
    ("message", 1, 3): [("message", 0, 3)],
    ("message", 1, 4): [("message", 0, 4)],
    ("message", 3, 1): [("message", 2, 1)],
    ("message", 3, 2): [("message", 2, 2)],
    ("message", 3, 3): [("message", 2, 3)],
    ("message", 3, 4): [("message", 2, 4)],
    ("message", 2, 1): [("message", 1, 2)],
    ("mixed", 0): [("message", 2, 2), ("message", 3, 1)],
}


def params(buffers=0):
    return pltpu.CompilerParams(vmem_limit_bytes=buffers + SPARE)


def column(place, row, side, n):
    col = place[1] if side == 0 else 1 - place[1]
    return pl.multiple_of(((2 * row + col) * (HEADS // n) + place[2]) * HEAD, HEAD)


def local_body(n, widths, swaps, place, low, keys, values, *refs):
    outs, (kbuf, vbuf, sems) = refs[:-3], refs[-3:]
    total = sum(widths)
    here = place[0], place[1], low[0]

    def copies(row, side):
        cols = pl.ds(column(here, row, side, n), total * HEAD)
        slot = 2 * row + side
        return [
            pltpu.make_async_copy(source.at[:, cols], buf.at[slot], sems.at[which, slot])
            for which, (source, buf) in enumerate(((keys, kbuf), (values, vbuf)))
        ]

    def fetch(row, carry):
        for side in range(2):
            for copy in copies(row, side):
                copy.start()
        return carry

    def work(row, carry):
        for side in range(2):
            for copy in copies(row, side):
                copy.wait()
        places = [
            [(out, head) for out, width in zip(arrays, sizes) for head in range(width)]
            for arrays, sizes in ((outs[: len(widths)], widths), (outs[len(widths) :], swaps))
        ]
        for side in range(2):
            for first in range(0, total, 2):
                size = min(2, total - first)
                cols = slice(first * HEAD, (first + size) * HEAD)
                both = lax.dot_general(
                    kbuf[2 * row + side, :, cols],
                    vbuf[2 * row + side, :, cols],
                    (((0,), (0,)), ((), ())),
                    preferred_element_type=jnp.float32,
                )
                for index in range(first, first + size):
                    part = slice((index - first) * HEAD, (index - first + 1) * HEAD)
                    out, head = places[side][index]
                    out[row, head] = both[part, part].astype(out.dtype)
        return carry

    lax.fori_loop(0, n // 2, fetch, 0)
    lax.fori_loop(0, n // 2, work, 0)


def local_states(place, keys, values, n, low, widths, swaps):
    rows, m, total = keys.shape[0], n // 2, sum(widths)
    buf = pltpu.VMEM((n, rows, total * HEAD), keys.dtype)
    shapes = [jax.ShapeDtypeStruct((m, width, HEAD, HEAD), jnp.float32) for width in widths]
    shapes += [jax.ShapeDtypeStruct((m, width, HEAD, HEAD), jnp.bfloat16) for width in swaps]
    return pl.pallas_call(
        functools.partial(local_body, n, widths, swaps),
        in_specs=[pl.BlockSpec(memory_space=pltpu.SMEM)] * 2 + [pl.BlockSpec(memory_space=pltpu.HBM)] * 2,
        out_specs=[pl.BlockSpec(memory_space=pltpu.VMEM)] * len(shapes),
        out_shape=shapes,
        scratch_shapes=[buf, buf, pltpu.SemaphoreType.DMA((2, n))],
        compiler_params=params(4 * n * rows * total * HEAD + 3 * n * total * HEAD * HEAD),
        cost_estimate=pl.CostEstimate(
            flops=2 * n * total * rows * HEAD * HEAD, bytes_accessed=4 * rows * n * total * HEAD, transcendentals=0
        ),
        name="local",
    )(place, jnp.full((1,), low, jnp.int32), keys, values)


def masked_scores(query, key):
    rows = query.shape[0]
    tiles = []
    for low in range(0, rows, TILE):
        high = min(low + TILE, rows)
        part = lax.dot_general(
            query[low:], key[low:high], (((1,), (1,)), ((), ())), preferred_element_type=jnp.float32
        )
        size = high - low
        spot = lax.broadcasted_iota(jnp.int32, (size, size), 0)
        other = lax.broadcasted_iota(jnp.int32, (size, size), 1)
        pieces = [jnp.where(other <= spot, part[:size], 0.0).astype(jnp.bfloat16)]
        if low:
            pieces.insert(0, jnp.zeros((low, size), jnp.bfloat16))
        if high < rows:
            pieces.append(part[size:].astype(jnp.bfloat16))
        tiles.append(jnp.concatenate(pieces, axis=0) if len(pieces) > 1 else pieces[0])
    return tiles


def attend_body(n, spans, place, low, queries, keys, values, gain, *refs):
    states, outs = refs[: 2 * len(spans)], refs[2 * len(spans) :][:n]
    qbuf, kbuf, vbuf, sown, soth, gbuf, held, sems, extra = refs[-9:]
    width = sum(size for _, size in spans)
    m, wide = n // 2, width * HEAD
    here = place[0], place[1], low[0]
    small, start = [(gain, gbuf)], 0
    for chunk, (skip, size) in enumerate(spans):
        for source, buf in ((states[2 * chunk], sown), (states[2 * chunk + 1], soth)):
            small.append((source.at[:, skip : skip + size], buf.at[:, start : start + size]))
        start += size
    small = [pltpu.make_async_copy(source, buf, extra.at[which]) for which, (source, buf) in enumerate(small)]

    def copies(step, side):
        cols = pl.ds(column(here, lax.rem(here[0] + step, m), side, n), wide)
        slot = 2 * step + side
        return [
            pltpu.make_async_copy(source.at[:, cols], buf.at[slot], sems.at[which, slot])
            for which, (source, buf) in enumerate(((queries, qbuf), (keys, kbuf), (values, vbuf)))
        ]

    def sends(step):
        return [
            pltpu.make_async_copy(held.at[slot], outs[slot], sems.at[3, slot])
            for slot in (2 * step, 2 * step + 1)
        ]

    def fetch(step, carry):
        for side in range(2):
            for copy in copies(step, side):
                copy.start()
        return carry

    def work(step, carry):
        for side in range(2):
            for copy in copies(step, side):
                copy.wait()
        row = lax.rem(here[0] + step, m)
        heads = [(side, head, slice(head * HEAD, (head + 1) * HEAD)) for side in range(2) for head in range(width)]
        scores = [masked_scores(qbuf[2 * step + side, :, cols], kbuf[2 * step + side, :, cols]) for side, _, cols in heads]
        attended = []
        for (side, head, cols), tiles in zip(heads, scores):
            slot = 2 * step + side
            state = (sown if side == 0 else soth)[row, head]
            left = jnp.concatenate([*tiles, qbuf[slot, :, cols]], axis=1)
            right = jnp.concatenate([vbuf[slot, :, cols], state], axis=0)
            attended.append(jnp.dot(left, right, preferred_element_type=jnp.float32))
        for (side, head, cols), value in zip(heads, attended):
            square = jnp.mean(value * value, axis=-1, keepdims=True)
            begin = pl.multiple_of(column(here, row, side, n) + head * HEAD, HEAD)
            mixed = value * lax.rsqrt(square + 1e-05) * gbuf[:, pl.ds(begin, HEAD)]
            held[2 * step + side, :, cols] = mixed.astype(held.dtype)
        for fixed in range(m):

            @pl.when(step == fixed)
            def _(fixed=fixed):
                for copy in sends(fixed):
                    copy.start()

        return carry

    lax.fori_loop(0, 1, fetch, 0)
    for copy in small:
        copy.start()
    lax.fori_loop(1, m, fetch, 0)
    for copy in small:
        copy.wait()
    lax.fori_loop(0, m, work, 0)
    for step in range(m):
        for copy in sends(step):
            copy.wait()


def attend(place, queries, keys, values, gain, states, spans, n, low):
    rows, m = queries.shape[0], n // 2
    width = sum(size for _, size in spans)
    wide = width * HEAD
    tokens = pltpu.VMEM((n, rows, wide), jnp.bfloat16)
    state = pltpu.VMEM((m, width, HEAD, HEAD), jnp.bfloat16)
    return pl.pallas_call(
        functools.partial(attend_body, n, spans),
        in_specs=[pl.BlockSpec(memory_space=pltpu.SMEM)] * 2
        + [pl.BlockSpec(memory_space=pltpu.HBM)] * 3
        + [pl.BlockSpec(memory_space=pl.ANY)] * (1 + 2 * len(states)),
        out_specs=[pl.BlockSpec(memory_space=pltpu.HBM)] * n,
        out_shape=[jax.ShapeDtypeStruct((rows, wide), jnp.bfloat16)] * n,
        scratch_shapes=[
            tokens,
            tokens,
            tokens,
            state,
            state,
            pltpu.VMEM((1, HEADS * HEAD), jnp.float32),
            tokens,
            pltpu.SemaphoreType.DMA((4, n)),
            pltpu.SemaphoreType.DMA((1 + 2 * len(states),)),
        ],
        compiler_params=params(8 * n * rows * wide + 2 * n * width * HEAD * HEAD + 4 * HEADS * HEAD),
        cost_estimate=pl.CostEstimate(
            flops=2 * n * width * rows * HEAD * (2 * rows + HEAD),
            bytes_accessed=8 * rows * n * wide,
            transcendentals=n * width * rows,
        ),
        name="attend",
    )(place, jnp.full((1,), low, jnp.int32), queries, keys, values, gain, *(array for pair in states for array in pair))


def put_body(n, place, low, *refs):
    parts, out, again, sems = refs[:n], refs[-3], refs[-2], refs[-1]
    m = n // 2
    rows, wide = parts[0].shape
    cols = pl.ds(pl.multiple_of(low[0] * HEAD, HEAD), wide)
    copies = []
    for shift in range(n):
        row = lax.rem(place[0] + m - shift // 2, m)
        col = place[1] if shift % 2 == 0 else 1 - place[1]
        start = pl.multiple_of((2 * row + col) * rows, rows)
        copies.append(
            pltpu.make_async_copy(parts[shift], out.at[pl.ds(start, rows), cols], sems.at[shift])
        )
    for copy in copies:
        copy.start()
    for index in range(2):
        again[index] = place[index]
    for copy in copies:
        copy.wait()


def put(place, parts, out, n, low):
    rows, first = parts[0].shape[0], out is None
    anywhere = pl.BlockSpec(memory_space=pltpu.HBM)
    return pl.pallas_call(
        functools.partial(put_body, n),
        in_specs=[pl.BlockSpec(memory_space=pltpu.SMEM)] * 2 + [anywhere] * (n if first else n + 1),
        out_specs=[anywhere, pl.BlockSpec(memory_space=pltpu.SMEM)],
        out_shape=[
            jax.ShapeDtypeStruct((n * rows, HEADS // n * HEAD), jnp.bfloat16),
            jax.ShapeDtypeStruct((2,), jnp.int32),
        ],
        scratch_shapes=[pltpu.SemaphoreType.DMA((n,))],
        input_output_aliases={} if first else {n + 2: 0},
        compiler_params=params(),
        name="put",
    )(place, jnp.full((1,), low, jnp.int32), *parts, *(() if first else (out,)))


def split(widths, per_dest):
    chunks, low = [], 0
    for width in widths:
        if low < per_dest:
            width = min(width, per_dest - low)
            chunks.append((low, width))
            low += width
    return chunks


def inside(chunks, low, width):
    return [c for c, (start, _) in enumerate(chunks) if low <= start < low + width]


class Plan:
    def __init__(self, n, queries, keys, values, gain):
        self.n, self.m = n, n // 2
        me = lax.axis_index("seq")
        self.col = me % 2
        self.place = jnp.stack([me // 2, self.col]).astype(jnp.int32)
        self.arrays = tuple(pltpu.with_memory_space_constraint(x, pltpu.HBM) for x in (queries, keys, values))
        self.gain = gain.reshape(1, HEADS * HEAD)
        self.groups, self.swaps, self.parts, self.chunks = (
            split(widths, HEADS // n) for widths in (LOCAL, SWAP, PREFIX, MIXED)
        )
        self.made = {}

    def has(self, key):
        limit = {"message": self.m, "prefix": self.m, "sent": self.n - 1}.get(key[0], 0)
        chunks = {"group": self.groups, "swap": self.swaps, "mixed": self.chunks, "sent": self.chunks}
        chunks = chunks.get(key[0], self.parts)
        return key[1] < len(chunks) and (len(key) < 3 or key[2] <= limit)

    def get(self, *key):
        if key not in self.made:
            self.made[key] = getattr(self, key[0])(*key[1:])
        return self.made[key]

    def hold(self, value, *key):
        others = []
        for other in ORDER.get(key, ()):
            if self.has(other):
                result = self.get(*other)
                while isinstance(result, (list, tuple)):
                    result = result[-1]
                others.append(result)
        return lax.optimization_barrier((value, *others))[0] if others else value

    def group(self, g):
        low, width = self.groups[g]
        widths = tuple(self.parts[c][1] for c in inside(self.parts, low, width))
        swaps = tuple(self.swaps[c][1] for c in inside(self.swaps, low, width))
        _, keys, values = self.arrays
        place = self.hold(self.place, "group", g)
        arrays = local_states(place, keys, values, self.n, low, widths, swaps)
        return arrays[: len(widths)], arrays[len(widths) :]

    def around(self, chunks, low):
        return next(c for c, (start, width) in enumerate(chunks) if start <= low < start + width)

    def swap(self, w):
        g = self.around(self.groups, self.swaps[w][0])
        spot = inside(self.swaps, *self.groups[g]).index(w)
        other = self.hold(self.get("group", g)[1][spot], "swap", w)
        return lax.ppermute(other, "seq", [(d, d ^ 1) for d in range(self.n)])

    def local(self, c):
        low, width = self.parts[c]
        g, w = self.around(self.groups, low), self.around(self.swaps, low)
        near = self.get("swap", w)[:, low - self.swaps[w][0] :][:, :width].astype(jnp.float32)
        return self.get("group", g)[0][inside(self.parts, *self.groups[g]).index(c)], near

    def total(self, c):
        parts = [self.get("prefix", c, s) for s in range(1, self.m)]
        return sum(parts[1:], parts[0]).astype(jnp.float32)

    def message(self, c, s):
        own, near = self.get("local", c)
        if s == self.m:
            value = self.get("total", c) + jnp.where(self.col == 0, own, 0.0)
        else:
            value = own + near
            if s > 1:
                value = self.get("prefix", c, s - 1).astype(jnp.float32) + value
        return self.hold(value.astype(jnp.bfloat16), "message", c, s)

    def prefix(self, c, s):
        if s == self.m:
            pairs = [(d, d ^ 1) for d in range(self.n)]
        else:
            pairs = [(2 * (s - 1) + y, 2 * s + y) for y in range(2)]
        return lax.ppermute(self.get("message", c, s), "seq", pairs)

    def states(self, c):
        _, near = self.get("local", c)
        own = (self.get("total", c) + jnp.where(self.col == 1, near, 0.0)).astype(jnp.bfloat16)
        return own, self.get("prefix", c, self.m)

    def mixed(self, c):
        low, width = self.chunks[c]
        place = self.get("put", c - 3)[1] if c > 2 else self.place
        place = self.hold(place, "mixed", c)
        states, spans = [], []
        for part, (start, size) in enumerate(self.parts):
            first, last = max(low, start), min(low + width, start + size)
            if first < last:
                states.append(self.get("states", part))
                spans.append((first - start, last - first))
        return attend(place, *self.arrays, self.gain, states, tuple(spans), self.n, low)

    def sent(self, c, k):
        pairs = [
            (2 * z + y, 2 * ((z + k // 2) % self.m) + (y + k) % 2) for z in range(self.m) for y in range(2)
        ]
        return lax.ppermute(self.hold(self.get("mixed", c)[k], "sent", c, k), "seq", pairs)

    def put(self, c):
        parts = [self.get("mixed", c)[0]] + [self.get("sent", c, k) for k in range(1, self.n)]
        out = self.get("put", c - 1)[0] if c else None
        return put(self.place, parts, out, self.n, self.chunks[c][0])


def per_device(n, *arrays):
    plan = Plan(n, *arrays)
    return plan.get("put", len(plan.chunks) - 1)[0]


def solution(mesh):
    tokens = P(("batch", "seq"), None)
    return jax.shard_map(
        functools.partial(per_device, mesh.shape["seq"]),
        mesh=mesh,
        in_specs=(tokens, tokens, tokens, P()),
        out_specs=P("batch", "seq"),
        check_vma=False,
    )
```

```python
import functools

import jax
import jax.numpy as jnp
from jax import lax
from jax.experimental import pallas as pl
from jax.experimental.pallas import tpu as pltpu
from jax.sharding import PartitionSpec as P

HEADS = 64
HEAD = 128
LOCAL = (2, 6)
SWAP = (2, 3, 3)
PREFIX = (2, 3, 3)
MIXED = (2, 3, 3)
TILE = 256
SPARE = 8 * 1024 * 1024
ORDER = {
    ("message", 0, 1): [("group", 1)],
    ("message", 1, 1): [("message", 0, 2)],
    ("message", 1, 2): [("message", 0, 3)],
    ("message", 1, 3): [("message", 0, 4)],
    ("message", 2, 1): [("message", 1, 2)],
    ("message", 2, 2): [("message", 1, 3)],
    ("message", 2, 3): [("message", 1, 4), ("mixed", 0)],
    ("mixed", 0): [("message", 1, 3), ("message", 2, 2)],
    ("message", 1, 4): [("mixed", 0)],
}


def params(buffers=0):
    return pltpu.CompilerParams(vmem_limit_bytes=buffers + SPARE)


def column(place, row, side, n):
    col = place[1] if side == 0 else 1 - place[1]
    return pl.multiple_of(((2 * row + col) * (HEADS // n) + place[2]) * HEAD, HEAD)


def local_body(n, widths, swaps, place, low, keys, values, *refs):
    outs, (kbuf, vbuf, sems) = refs[:-3], refs[-3:]
    total = sum(widths)
    here = place[0], place[1], low[0]

    def copies(row, side):
        cols = pl.ds(column(here, row, side, n), total * HEAD)
        slot = 2 * row + side
        return [
            pltpu.make_async_copy(source.at[:, cols], buf.at[slot], sems.at[which, slot])
            for which, (source, buf) in enumerate(((keys, kbuf), (values, vbuf)))
        ]

    def fetch(row, carry):
        for side in range(2):
            for copy in copies(row, side):
                copy.start()
        return carry

    def work(row, carry):
        for side in range(2):
            for copy in copies(row, side):
                copy.wait()
        places = [
            [(out, head) for out, width in zip(arrays, sizes) for head in range(width)]
            for arrays, sizes in ((outs[: len(widths)], widths), (outs[len(widths) :], swaps))
        ]
        for side in range(2):
            for first in range(0, total, 2):
                size = min(2, total - first)
                cols = slice(first * HEAD, (first + size) * HEAD)
                both = lax.dot_general(
                    kbuf[2 * row + side, :, cols],
                    vbuf[2 * row + side, :, cols],
                    (((0,), (0,)), ((), ())),
                    preferred_element_type=jnp.float32,
                )
                for index in range(first, first + size):
                    part = slice((index - first) * HEAD, (index - first + 1) * HEAD)
                    out, head = places[side][index]
                    out[row, head] = both[part, part].astype(out.dtype)
        return carry

    lax.fori_loop(0, n // 2, fetch, 0)
    lax.fori_loop(0, n // 2, work, 0)


def local_states(place, keys, values, n, low, widths, swaps):
    rows, m, total = keys.shape[0], n // 2, sum(widths)
    buf = pltpu.VMEM((n, rows, total * HEAD), keys.dtype)
    shapes = [jax.ShapeDtypeStruct((m, width, HEAD, HEAD), jnp.float32) for width in widths]
    shapes += [jax.ShapeDtypeStruct((m, width, HEAD, HEAD), jnp.bfloat16) for width in swaps]
    return pl.pallas_call(
        functools.partial(local_body, n, widths, swaps),
        in_specs=[pl.BlockSpec(memory_space=pltpu.SMEM)] * 2 + [pl.BlockSpec(memory_space=pltpu.HBM)] * 2,
        out_specs=[pl.BlockSpec(memory_space=pltpu.VMEM)] * len(shapes),
        out_shape=shapes,
        scratch_shapes=[buf, buf, pltpu.SemaphoreType.DMA((2, n))],
        compiler_params=params(4 * n * rows * total * HEAD + 3 * n * total * HEAD * HEAD),
        cost_estimate=pl.CostEstimate(
            flops=2 * n * total * rows * HEAD * HEAD, bytes_accessed=4 * rows * n * total * HEAD, transcendentals=0
        ),
        name="local",
    )(place, jnp.full((1,), low, jnp.int32), keys, values)


def masked_scores(query, key):
    rows = query.shape[0]
    tiles = []
    for low in range(0, rows, TILE):
        high = min(low + TILE, rows)
        part = lax.dot_general(
            query[low:], key[low:high], (((1,), (1,)), ((), ())), preferred_element_type=jnp.float32
        )
        size = high - low
        spot = lax.broadcasted_iota(jnp.int32, (size, size), 0)
        other = lax.broadcasted_iota(jnp.int32, (size, size), 1)
        pieces = [jnp.where(other <= spot, part[:size], 0.0).astype(jnp.bfloat16)]
        if low:
            pieces.insert(0, jnp.zeros((low, size), jnp.bfloat16))
        if high < rows:
            pieces.append(part[size:].astype(jnp.bfloat16))
        tiles.append(jnp.concatenate(pieces, axis=0) if len(pieces) > 1 else pieces[0])
    return tiles


def attend_body(n, spans, place, low, queries, keys, values, gain, *refs):
    states, outs = refs[: 2 * len(spans)], refs[2 * len(spans) :][:n]
    qbuf, kbuf, vbuf, sown, soth, gbuf, held, sems, extra = refs[-9:]
    width = sum(size for _, size in spans)
    m, wide = n // 2, width * HEAD
    here = place[0], place[1], low[0]
    small, start = [(gain, gbuf)], 0
    for chunk, (skip, size) in enumerate(spans):
        for source, buf in ((states[2 * chunk], sown), (states[2 * chunk + 1], soth)):
            small.append((source.at[:, skip : skip + size], buf.at[:, start : start + size]))
        start += size
    small = [pltpu.make_async_copy(source, buf, extra.at[which]) for which, (source, buf) in enumerate(small)]

    def copies(step, side):
        cols = pl.ds(column(here, lax.rem(here[0] + step, m), side, n), wide)
        slot = 2 * step + side
        return [
            pltpu.make_async_copy(source.at[:, cols], buf.at[slot], sems.at[which, slot])
            for which, (source, buf) in enumerate(((queries, qbuf), (keys, kbuf), (values, vbuf)))
        ]

    def sends(step):
        return [
            pltpu.make_async_copy(held.at[slot], outs[slot], sems.at[3, slot])
            for slot in (2 * step, 2 * step + 1)
        ]

    def fetch(step, carry):
        for side in range(2):
            for copy in copies(step, side):
                copy.start()
        return carry

    def work(step, carry):
        for side in range(2):
            for copy in copies(step, side):
                copy.wait()
        row = lax.rem(here[0] + step, m)
        heads = [(side, head, slice(head * HEAD, (head + 1) * HEAD)) for side in range(2) for head in range(width)]
        scores = [masked_scores(qbuf[2 * step + side, :, cols], kbuf[2 * step + side, :, cols]) for side, _, cols in heads]
        attended = []
        for (side, head, cols), tiles in zip(heads, scores):
            slot = 2 * step + side
            state = (sown if side == 0 else soth)[row, head]
            left = jnp.concatenate([*tiles, qbuf[slot, :, cols]], axis=1)
            right = jnp.concatenate([vbuf[slot, :, cols], state], axis=0)
            attended.append(jnp.dot(left, right, preferred_element_type=jnp.float32))
        for (side, head, cols), value in zip(heads, attended):
            square = jnp.mean(value * value, axis=-1, keepdims=True)
            begin = pl.multiple_of(column(here, row, side, n) + head * HEAD, HEAD)
            mixed = value * lax.rsqrt(square + 1e-05) * gbuf[:, pl.ds(begin, HEAD)]
            held[2 * step + side, :, cols] = mixed.astype(held.dtype)
        for fixed in range(m):

            @pl.when(step == fixed)
            def _(fixed=fixed):
                for copy in sends(fixed):
                    copy.start()

        return carry

    lax.fori_loop(0, 1, fetch, 0)
    for copy in small:
        copy.start()
    lax.fori_loop(1, m, fetch, 0)
    for copy in small:
        copy.wait()
    lax.fori_loop(0, m, work, 0)
    for step in range(m):
        for copy in sends(step):
            copy.wait()


def attend(place, queries, keys, values, gain, states, spans, n, low):
    rows, m = queries.shape[0], n // 2
    width = sum(size for _, size in spans)
    wide = width * HEAD
    tokens = pltpu.VMEM((n, rows, wide), jnp.bfloat16)
    state = pltpu.VMEM((m, width, HEAD, HEAD), jnp.bfloat16)
    return pl.pallas_call(
        functools.partial(attend_body, n, spans),
        in_specs=[pl.BlockSpec(memory_space=pltpu.SMEM)] * 2
        + [pl.BlockSpec(memory_space=pltpu.HBM)] * 3
        + [pl.BlockSpec(memory_space=pl.ANY)] * (1 + 2 * len(states)),
        out_specs=[pl.BlockSpec(memory_space=pltpu.HBM)] * n,
        out_shape=[jax.ShapeDtypeStruct((rows, wide), jnp.bfloat16)] * n,
        scratch_shapes=[
            tokens,
            tokens,
            tokens,
            state,
            state,
            pltpu.VMEM((1, HEADS * HEAD), jnp.float32),
            tokens,
            pltpu.SemaphoreType.DMA((4, n)),
            pltpu.SemaphoreType.DMA((1 + 2 * len(states),)),
        ],
        compiler_params=params(8 * n * rows * wide + 2 * n * width * HEAD * HEAD + 4 * HEADS * HEAD),
        cost_estimate=pl.CostEstimate(
            flops=2 * n * width * rows * HEAD * (2 * rows + HEAD),
            bytes_accessed=8 * rows * n * wide,
            transcendentals=n * width * rows,
        ),
        name="attend",
    )(place, jnp.full((1,), low, jnp.int32), queries, keys, values, gain, *(array for pair in states for array in pair))


def put_body(n, place, low, *refs):
    parts, out, again, sems = refs[:n], refs[-3], refs[-2], refs[-1]
    m = n // 2
    rows, wide = parts[0].shape
    cols = pl.ds(pl.multiple_of(low[0] * HEAD, HEAD), wide)
    copies = []
    for shift in range(n):
        row = lax.rem(place[0] + m - shift // 2, m)
        col = place[1] if shift % 2 == 0 else 1 - place[1]
        start = pl.multiple_of((2 * row + col) * rows, rows)
        copies.append(
            pltpu.make_async_copy(parts[shift], out.at[pl.ds(start, rows), cols], sems.at[shift])
        )
    for copy in copies:
        copy.start()
    for index in range(2):
        again[index] = place[index]
    for copy in copies:
        copy.wait()


def put(place, parts, out, n, low):
    rows, first = parts[0].shape[0], out is None
    anywhere = pl.BlockSpec(memory_space=pltpu.HBM)
    return pl.pallas_call(
        functools.partial(put_body, n),
        in_specs=[pl.BlockSpec(memory_space=pltpu.SMEM)] * 2 + [anywhere] * (n if first else n + 1),
        out_specs=[anywhere, pl.BlockSpec(memory_space=pltpu.SMEM)],
        out_shape=[
            jax.ShapeDtypeStruct((n * rows, HEADS // n * HEAD), jnp.bfloat16),
            jax.ShapeDtypeStruct((2,), jnp.int32),
        ],
        scratch_shapes=[pltpu.SemaphoreType.DMA((n,))],
        input_output_aliases={} if first else {n + 2: 0},
        compiler_params=params(),
        name="put",
    )(place, jnp.full((1,), low, jnp.int32), *parts, *(() if first else (out,)))


def split(widths, per_dest):
    chunks, low = [], 0
    for width in widths:
        if low < per_dest:
            width = min(width, per_dest - low)
            chunks.append((low, width))
            low += width
    return chunks


def inside(chunks, low, width):
    return [c for c, (start, _) in enumerate(chunks) if low <= start < low + width]


class Plan:
    def __init__(self, n, queries, keys, values, gain):
        self.n, self.m = n, n // 2
        me = lax.axis_index("seq")
        self.col = me % 2
        self.place = jnp.stack([me // 2, self.col]).astype(jnp.int32)
        self.arrays = tuple(pltpu.with_memory_space_constraint(x, pltpu.HBM) for x in (queries, keys, values))
        self.gain = gain.reshape(1, HEADS * HEAD)
        self.groups, self.swaps, self.parts, self.chunks = (
            split(widths, HEADS // n) for widths in (LOCAL, SWAP, PREFIX, MIXED)
        )
        self.made = {}

    def has(self, key):
        limit = {"message": self.m, "prefix": self.m, "sent": self.n - 1}.get(key[0], 0)
        chunks = {"group": self.groups, "swap": self.swaps, "mixed": self.chunks, "sent": self.chunks}
        chunks = chunks.get(key[0], self.parts)
        return key[1] < len(chunks) and (len(key) < 3 or key[2] <= limit)

    def get(self, *key):
        if key not in self.made:
            self.made[key] = getattr(self, key[0])(*key[1:])
        return self.made[key]

    def hold(self, value, *key):
        others = []
        for other in ORDER.get(key, ()):
            if self.has(other):
                result = self.get(*other)
                while isinstance(result, (list, tuple)):
                    result = result[-1]
                others.append(result)
        return lax.optimization_barrier((value, *others))[0] if others else value

    def group(self, g):
        low, width = self.groups[g]
        widths = tuple(self.parts[c][1] for c in inside(self.parts, low, width))
        swaps = tuple(self.swaps[c][1] for c in inside(self.swaps, low, width))
        _, keys, values = self.arrays
        place = self.hold(self.place, "group", g)
        arrays = local_states(place, keys, values, self.n, low, widths, swaps)
        return arrays[: len(widths)], arrays[len(widths) :]

    def around(self, chunks, low):
        return next(c for c, (start, width) in enumerate(chunks) if start <= low < start + width)

    def swap(self, w):
        g = self.around(self.groups, self.swaps[w][0])
        spot = inside(self.swaps, *self.groups[g]).index(w)
        other = self.hold(self.get("group", g)[1][spot], "swap", w)
        return lax.ppermute(other, "seq", [(d, d ^ 1) for d in range(self.n)])

    def local(self, c):
        low, width = self.parts[c]
        g, w = self.around(self.groups, low), self.around(self.swaps, low)
        near = self.get("swap", w)[:, low - self.swaps[w][0] :][:, :width].astype(jnp.float32)
        return self.get("group", g)[0][inside(self.parts, *self.groups[g]).index(c)], near

    def total(self, c):
        parts = [self.get("prefix", c, s) for s in range(1, self.m)]
        return sum(parts[1:], parts[0]).astype(jnp.float32)

    def message(self, c, s):
        own, near = self.get("local", c)
        if s == self.m:
            value = self.get("total", c) + jnp.where(self.col == 0, own, 0.0)
        else:
            value = own + near
            if s > 1:
                value = self.get("prefix", c, s - 1).astype(jnp.float32) + value
        return self.hold(value.astype(jnp.bfloat16), "message", c, s)

    def prefix(self, c, s):
        if s == self.m:
            pairs = [(d, d ^ 1) for d in range(self.n)]
        else:
            pairs = [(2 * (s - 1) + y, 2 * s + y) for y in range(2)]
        return lax.ppermute(self.get("message", c, s), "seq", pairs)

    def states(self, c):
        _, near = self.get("local", c)
        own = (self.get("total", c) + jnp.where(self.col == 1, near, 0.0)).astype(jnp.bfloat16)
        return own, self.get("prefix", c, self.m)

    def mixed(self, c):
        low, width = self.chunks[c]
        place = self.get("put", c - 3)[1] if c > 2 else self.place
        place = self.hold(place, "mixed", c)
        states, spans = [], []
        for part, (start, size) in enumerate(self.parts):
            first, last = max(low, start), min(low + width, start + size)
            if first < last:
                states.append(self.get("states", part))
                spans.append((first - start, last - first))
        return attend(place, *self.arrays, self.gain, states, tuple(spans), self.n, low)

    def sent(self, c, k):
        pairs = [
            (2 * z + y, 2 * ((z + k // 2) % self.m) + (y + k) % 2) for z in range(self.m) for y in range(2)
        ]
        return lax.ppermute(self.hold(self.get("mixed", c)[k], "sent", c, k), "seq", pairs)

    def put(self, c):
        parts = [self.get("mixed", c)[0]] + [self.get("sent", c, k) for k in range(1, self.n)]
        out = self.get("put", c - 1)[0] if c else None
        return put(self.place, parts, out, self.n, self.chunks[c][0])


def per_device(n, *arrays):
    plan = Plan(n, *arrays)
    return plan.get("put", len(plan.chunks) - 1)[0]


def solution(mesh):
    tokens = P(("batch", "seq"), None)
    return jax.shard_map(
        functools.partial(per_device, mesh.shape["seq"]),
        mesh=mesh,
        in_specs=(tokens, tokens, tokens, P()),
        out_specs=P("batch", "seq"),
        check_vma=False,
    )
```

```python
import functools

import jax
import jax.numpy as jnp
from jax import lax
from jax.experimental import pallas as pl
from jax.experimental.pallas import tpu as pltpu
from jax.sharding import PartitionSpec as P

HEADS = 64
HEAD = 128
LOCAL = (2, 6)
SWAP = (2, 3, 3)
PREFIX = (2, 3, 3)
MIXED = (2, 3, 3)
TILE = 256
SPARE = 8 * 1024 * 1024
ORDER = {
    ("message", 0, 1): [("group", 1)],
    ("message", 1, 1): [("message", 0, 2)],
    ("message", 1, 2): [("message", 0, 3)],
    ("message", 1, 3): [("message", 0, 4)],
    ("message", 2, 1): [("message", 1, 2)],
    ("message", 2, 2): [("message", 1, 3)],
    ("message", 2, 3): [("message", 1, 4), ("mixed", 0)],
    ("mixed", 0): [("message", 1, 3), ("message", 2, 2)],
    ("message", 1, 4): [("mixed", 0)],
}


def params(buffers=0):
    return pltpu.CompilerParams(vmem_limit_bytes=buffers + SPARE)


def column(place, row, side, n):
    col = place[1] if side == 0 else 1 - place[1]
    return pl.multiple_of(((2 * row + col) * (HEADS // n) + place[2]) * HEAD, HEAD)


def rows_together(m, width, most):
    return max(count for count in range(1, m + 1) if m % count == 0 and (count == 1 or 2 * width * count <= most))


def local_body(n, widths, swaps, place, low, keys, values, *refs):
    outs, (kbuf, vbuf, sems) = refs[:-3], refs[-3:]
    total = sum(widths)
    here = place[0], place[1], low[0]
    together = rows_together(n // 2, total, 16)

    def copies(row, side):
        cols = pl.ds(column(here, row, side, n), total * HEAD)
        slot = 2 * row + side
        return [
            pltpu.make_async_copy(source.at[:, cols], buf.at[slot], sems.at[which, slot])
            for which, (source, buf) in enumerate(((keys, kbuf), (values, vbuf)))
        ]

    def fetch(row, carry):
        for side in range(2):
            for copy in copies(row, side):
                copy.start()
        return carry

    def work(step, carry):
        slots = [(step * together + index, side) for index in range(together) for side in range(2)]
        for row, side in slots:
            for copy in copies(row, side):
                copy.wait()
        places = [
            [(out, head) for out, width in zip(arrays, sizes) for head in range(width)]
            for arrays, sizes in ((outs[: len(widths)], widths), (outs[len(widths) :], swaps))
        ]
        for row, side in slots:
            for first in range(0, total, 2):
                size = min(2, total - first)
                cols = slice(first * HEAD, (first + size) * HEAD)
                both = lax.dot_general(
                    kbuf[2 * row + side, :, cols],
                    vbuf[2 * row + side, :, cols],
                    (((0,), (0,)), ((), ())),
                    preferred_element_type=jnp.float32,
                )
                for index in range(first, first + size):
                    part = slice((index - first) * HEAD, (index - first + 1) * HEAD)
                    out, head = places[side][index]
                    out[row, head] = both[part, part].astype(out.dtype)
        return carry

    lax.fori_loop(0, n // 2, fetch, 0)
    lax.fori_loop(0, n // 2 // together, work, 0)


def local_states(place, keys, values, n, low, widths, swaps):
    rows, m, total = keys.shape[0], n // 2, sum(widths)
    buf = pltpu.VMEM((n, rows, total * HEAD), keys.dtype)
    shapes = [jax.ShapeDtypeStruct((m, width, HEAD, HEAD), jnp.float32) for width in widths]
    shapes += [jax.ShapeDtypeStruct((m, width, HEAD, HEAD), jnp.bfloat16) for width in swaps]
    return pl.pallas_call(
        functools.partial(local_body, n, widths, swaps),
        in_specs=[pl.BlockSpec(memory_space=pltpu.SMEM)] * 2 + [pl.BlockSpec(memory_space=pltpu.HBM)] * 2,
        out_specs=[pl.BlockSpec(memory_space=pltpu.VMEM)] * len(shapes),
        out_shape=shapes,
        scratch_shapes=[buf, buf, pltpu.SemaphoreType.DMA((2, n))],
        compiler_params=params(4 * n * rows * total * HEAD + 3 * n * total * HEAD * HEAD),
        cost_estimate=pl.CostEstimate(
            flops=2 * n * total * rows * HEAD * HEAD, bytes_accessed=4 * rows * n * total * HEAD, transcendentals=0
        ),
        name="local",
    )(place, jnp.full((1,), low, jnp.int32), keys, values)


def masked_scores(query, key):
    rows = query.shape[0]
    tiles = []
    for low in range(0, rows, TILE):
        high = min(low + TILE, rows)
        part = lax.dot_general(
            query[low:], key[low:high], (((1,), (1,)), ((), ())), preferred_element_type=jnp.float32
        )
        size = high - low
        spot = lax.broadcasted_iota(jnp.int32, (size, size), 0)
        other = lax.broadcasted_iota(jnp.int32, (size, size), 1)
        pieces = [jnp.where(other <= spot, part[:size], 0.0).astype(jnp.bfloat16)]
        if low:
            pieces.insert(0, jnp.zeros((low, size), jnp.bfloat16))
        if high < rows:
            pieces.append(part[size:].astype(jnp.bfloat16))
        tiles.append(jnp.concatenate(pieces, axis=0) if len(pieces) > 1 else pieces[0])
    return tiles


def attend_body(n, spans, place, low, queries, keys, values, gain, *refs):
    states, outs = refs[: 2 * len(spans)], refs[2 * len(spans) :][:n]
    qbuf, kbuf, vbuf, sown, soth, gbuf, held, sems, extra = refs[-9:]
    width = sum(size for _, size in spans)
    m, wide = n // 2, width * HEAD
    together = rows_together(m, width, 12)
    here = place[0], place[1], low[0]
    small, start = [(gain, gbuf)], 0
    for chunk, (skip, size) in enumerate(spans):
        for source, buf in ((states[2 * chunk], sown), (states[2 * chunk + 1], soth)):
            small.append((source.at[:, skip : skip + size], buf.at[:, start : start + size]))
        start += size
    small = [pltpu.make_async_copy(source, buf, extra.at[which]) for which, (source, buf) in enumerate(small)]

    def copies(step, side):
        cols = pl.ds(column(here, lax.rem(here[0] + step, m), side, n), wide)
        slot = 2 * step + side
        return [
            pltpu.make_async_copy(source.at[:, cols], buf.at[slot], sems.at[which, slot])
            for which, (source, buf) in enumerate(((queries, qbuf), (keys, kbuf), (values, vbuf)))
        ]

    def sends(step):
        return [
            pltpu.make_async_copy(held.at[slot], outs[slot], sems.at[3, slot])
            for slot in (2 * step, 2 * step + 1)
        ]

    def fetch(step, carry):
        for side in range(2):
            for copy in copies(step, side):
                copy.start()
        return carry

    def work(group, carry):
        steps = [group * together + index for index in range(together)]
        for step in steps:
            for side in range(2):
                for copy in copies(step, side):
                    copy.wait()
        heads = [
            (step, side, head, slice(head * HEAD, (head + 1) * HEAD))
            for step in steps
            for side in range(2)
            for head in range(width)
        ]
        scores = [
            masked_scores(qbuf[2 * step + side, :, cols], kbuf[2 * step + side, :, cols])
            for step, side, _, cols in heads
        ]
        attended = []
        for (step, side, head, cols), tiles in zip(heads, scores):
            slot = 2 * step + side
            state = (sown if side == 0 else soth)[lax.rem(here[0] + step, m), head]
            left = jnp.concatenate([*tiles, qbuf[slot, :, cols]], axis=1)
            right = jnp.concatenate([vbuf[slot, :, cols], state], axis=0)
            attended.append(jnp.dot(left, right, preferred_element_type=jnp.float32))
        for (step, side, head, cols), value in zip(heads, attended):
            square = jnp.mean(value * value, axis=-1, keepdims=True)
            begin = pl.multiple_of(column(here, lax.rem(here[0] + step, m), side, n) + head * HEAD, HEAD)
            mixed = value * lax.rsqrt(square + 1e-05) * gbuf[:, pl.ds(begin, HEAD)]
            held[2 * step + side, :, cols] = mixed.astype(held.dtype)
        for fixed in range(m // together):

            @pl.when(group == fixed)
            def _(fixed=fixed):
                for index in range(together):
                    for copy in sends(fixed * together + index):
                        copy.start()

        return carry

    lax.fori_loop(0, 1, fetch, 0)
    for copy in small:
        copy.start()
    lax.fori_loop(1, m, fetch, 0)
    for copy in small:
        copy.wait()
    lax.fori_loop(0, m // together, work, 0)
    for step in range(m):
        for copy in sends(step):
            copy.wait()


def attend(place, queries, keys, values, gain, states, spans, n, low):
    rows, m = queries.shape[0], n // 2
    width = sum(size for _, size in spans)
    wide = width * HEAD
    tokens = pltpu.VMEM((n, rows, wide), jnp.bfloat16)
    state = pltpu.VMEM((m, width, HEAD, HEAD), jnp.bfloat16)
    return pl.pallas_call(
        functools.partial(attend_body, n, spans),
        in_specs=[pl.BlockSpec(memory_space=pltpu.SMEM)] * 2
        + [pl.BlockSpec(memory_space=pltpu.HBM)] * 3
        + [pl.BlockSpec(memory_space=pl.ANY)] * (1 + 2 * len(states)),
        out_specs=[pl.BlockSpec(memory_space=pltpu.HBM)] * n,
        out_shape=[jax.ShapeDtypeStruct((rows, wide), jnp.bfloat16)] * n,
        scratch_shapes=[
            tokens,
            tokens,
            tokens,
            state,
            state,
            pltpu.VMEM((1, HEADS * HEAD), jnp.float32),
            tokens,
            pltpu.SemaphoreType.DMA((4, n)),
            pltpu.SemaphoreType.DMA((1 + 2 * len(states),)),
        ],
        compiler_params=params(8 * n * rows * wide + 2 * n * width * HEAD * HEAD + 4 * HEADS * HEAD),
        cost_estimate=pl.CostEstimate(
            flops=2 * n * width * rows * HEAD * (2 * rows + HEAD),
            bytes_accessed=8 * rows * n * wide,
            transcendentals=n * width * rows,
        ),
        name="attend",
    )(place, jnp.full((1,), low, jnp.int32), queries, keys, values, gain, *(array for pair in states for array in pair))


def put_body(n, place, low, *refs):
    parts, out, again, sems = refs[:n], refs[-3], refs[-2], refs[-1]
    m = n // 2
    rows, wide = parts[0].shape
    cols = pl.ds(pl.multiple_of(low[0] * HEAD, HEAD), wide)
    copies = []
    for shift in range(n):
        row = lax.rem(place[0] + m - shift // 2, m)
        col = place[1] if shift % 2 == 0 else 1 - place[1]
        start = pl.multiple_of((2 * row + col) * rows, rows)
        copies.append(
            pltpu.make_async_copy(parts[shift], out.at[pl.ds(start, rows), cols], sems.at[shift])
        )
    for copy in copies:
        copy.start()
    for index in range(2):
        again[index] = place[index]
    for copy in copies:
        copy.wait()


def put(place, parts, out, n, low):
    rows, first = parts[0].shape[0], out is None
    anywhere = pl.BlockSpec(memory_space=pltpu.HBM)
    return pl.pallas_call(
        functools.partial(put_body, n),
        in_specs=[pl.BlockSpec(memory_space=pltpu.SMEM)] * 2 + [anywhere] * (n if first else n + 1),
        out_specs=[anywhere, pl.BlockSpec(memory_space=pltpu.SMEM)],
        out_shape=[
            jax.ShapeDtypeStruct((n * rows, HEADS // n * HEAD), jnp.bfloat16),
            jax.ShapeDtypeStruct((2,), jnp.int32),
        ],
        scratch_shapes=[pltpu.SemaphoreType.DMA((n,))],
        input_output_aliases={} if first else {n + 2: 0},
        compiler_params=params(),
        name="put",
    )(place, jnp.full((1,), low, jnp.int32), *parts, *(() if first else (out,)))


def split(widths, per_dest):
    chunks, low = [], 0
    for width in widths:
        if low < per_dest:
            width = min(width, per_dest - low)
            chunks.append((low, width))
            low += width
    return chunks


def inside(chunks, low, width):
    return [c for c, (start, _) in enumerate(chunks) if low <= start < low + width]


class Plan:
    def __init__(self, n, queries, keys, values, gain):
        self.n, self.m = n, n // 2
        me = lax.axis_index("seq")
        self.col = me % 2
        self.place = jnp.stack([me // 2, self.col]).astype(jnp.int32)
        self.arrays = tuple(pltpu.with_memory_space_constraint(x, pltpu.HBM) for x in (queries, keys, values))
        self.gain = gain.reshape(1, HEADS * HEAD)
        self.groups, self.swaps, self.parts, self.chunks = (
            split(widths, HEADS // n) for widths in (LOCAL, SWAP, PREFIX, MIXED)
        )
        self.made = {}

    def has(self, key):
        limit = {"message": self.m, "prefix": self.m, "sent": self.n - 1}.get(key[0], 0)
        chunks = {"group": self.groups, "swap": self.swaps, "mixed": self.chunks, "sent": self.chunks}
        chunks = chunks.get(key[0], self.parts)
        return key[1] < len(chunks) and (len(key) < 3 or key[2] <= limit)

    def get(self, *key):
        if key not in self.made:
            self.made[key] = getattr(self, key[0])(*key[1:])
        return self.made[key]

    def hold(self, value, *key):
        others = []
        for other in ORDER.get(key, ()):
            if self.has(other):
                result = self.get(*other)
                while isinstance(result, (list, tuple)):
                    result = result[-1]
                others.append(result)
        return lax.optimization_barrier((value, *others))[0] if others else value

    def group(self, g):
        low, width = self.groups[g]
        widths = tuple(self.parts[c][1] for c in inside(self.parts, low, width))
        swaps = tuple(self.swaps[c][1] for c in inside(self.swaps, low, width))
        _, keys, values = self.arrays
        place = self.hold(self.place, "group", g)
        arrays = local_states(place, keys, values, self.n, low, widths, swaps)
        return arrays[: len(widths)], arrays[len(widths) :]

    def around(self, chunks, low):
        return next(c for c, (start, width) in enumerate(chunks) if start <= low < start + width)

    def swap(self, w):
        g = self.around(self.groups, self.swaps[w][0])
        spot = inside(self.swaps, *self.groups[g]).index(w)
        other = self.hold(self.get("group", g)[1][spot], "swap", w)
        return lax.ppermute(other, "seq", [(d, d ^ 1) for d in range(self.n)])

    def local(self, c):
        low, width = self.parts[c]
        g, w = self.around(self.groups, low), self.around(self.swaps, low)
        near = self.get("swap", w)[:, low - self.swaps[w][0] :][:, :width].astype(jnp.float32)
        return self.get("group", g)[0][inside(self.parts, *self.groups[g]).index(c)], near

    def total(self, c):
        parts = [self.get("prefix", c, s) for s in range(1, self.m)]
        return sum(parts[1:], parts[0]).astype(jnp.float32)

    def message(self, c, s):
        own, near = self.get("local", c)
        if s == self.m:
            value = self.get("total", c) + jnp.where(self.col == 0, own, 0.0)
        else:
            value = own + near
            if s > 1:
                value = self.get("prefix", c, s - 1).astype(jnp.float32) + value
        return self.hold(value.astype(jnp.bfloat16), "message", c, s)

    def prefix(self, c, s):
        if s == self.m:
            pairs = [(d, d ^ 1) for d in range(self.n)]
        else:
            pairs = [(2 * (s - 1) + y, 2 * s + y) for y in range(2)]
        return lax.ppermute(self.get("message", c, s), "seq", pairs)

    def states(self, c):
        _, near = self.get("local", c)
        own = (self.get("total", c) + jnp.where(self.col == 1, near, 0.0)).astype(jnp.bfloat16)
        return own, self.get("prefix", c, self.m)

    def mixed(self, c):
        low, width = self.chunks[c]
        place = self.get("put", c - 3)[1] if c > 2 else self.place
        place = self.hold(place, "mixed", c)
        states, spans = [], []
        for part, (start, size) in enumerate(self.parts):
            first, last = max(low, start), min(low + width, start + size)
            if first < last:
                states.append(self.get("states", part))
                spans.append((first - start, last - first))
        return attend(place, *self.arrays, self.gain, states, tuple(spans), self.n, low)

    def sent(self, c, k):
        pairs = [
            (2 * z + y, 2 * ((z + k // 2) % self.m) + (y + k) % 2) for z in range(self.m) for y in range(2)
        ]
        return lax.ppermute(self.hold(self.get("mixed", c)[k], "sent", c, k), "seq", pairs)

    def put(self, c):
        parts = [self.get("mixed", c)[0]] + [self.get("sent", c, k) for k in range(1, self.n)]
        out = self.get("put", c - 1)[0] if c else None
        return put(self.place, parts, out, self.n, self.chunks[c][0])


def per_device(n, *arrays):
    plan = Plan(n, *arrays)
    return plan.get("put", len(plan.chunks) - 1)[0]


def solution(mesh):
    tokens = P(("batch", "seq"), None)
    return jax.shard_map(
        functools.partial(per_device, mesh.shape["seq"]),
        mesh=mesh,
        in_specs=(tokens, tokens, tokens, P()),
        out_specs=P("batch", "seq"),
        check_vma=False,
    )
```

```python
import functools

import jax
import jax.numpy as jnp
from jax import lax
from jax.experimental import pallas as pl
from jax.experimental.pallas import tpu as pltpu
from jax.sharding import PartitionSpec as P

HEADS = 64
HEAD = 128
LOCAL = (2, 6)
SWAP = (2, 3, 3)
PREFIX = (2, 3, 3)
MIXED = (2, 3, 3)
TILE = 256
SPARE = 8 * 1024 * 1024
ORDER = {
    ("message", 0, 1): [("group", 1)],
    ("message", 1, 1): [("message", 0, 2)],
    ("message", 1, 2): [("message", 0, 3)],
    ("message", 1, 3): [("message", 0, 4), ("mixed", 0)],
    ("message", 2, 1): [("message", 1, 2)],
    ("message", 2, 2): [("message", 1, 3), ("mixed", 0)],
    ("message", 2, 3): [("message", 1, 4), ("sent", 0, 2)],
    ("mixed", 0): [("message", 1, 2), ("message", 2, 1)],
    ("message", 1, 4): [("sent", 0, 1)],
    ("mixed", 1): [("sent", 0, 1), ("sent", 0, 2), ("sent", 0, 3), ("sent", 0, 4)],
}


def params(buffers=0):
    return pltpu.CompilerParams(vmem_limit_bytes=buffers + SPARE)


def column(place, row, side, n):
    col = place[1] if side == 0 else 1 - place[1]
    return pl.multiple_of(((2 * row + col) * (HEADS // n) + place[2]) * HEAD, HEAD)


def rows_together(m, width, most):
    return max(count for count in range(1, m + 1) if m % count == 0 and (count == 1 or 2 * width * count <= most))


def local_body(n, widths, swaps, place, low, keys, values, *refs):
    outs, (kbuf, vbuf, sems) = refs[:-3], refs[-3:]
    total = sum(widths)
    here = place[0], place[1], low[0]
    together = rows_together(n // 2, total, 16)

    def copies(row, side):
        cols = pl.ds(column(here, row, side, n), total * HEAD)
        slot = 2 * row + side
        return [
            pltpu.make_async_copy(source.at[:, cols], buf.at[slot], sems.at[which, slot])
            for which, (source, buf) in enumerate(((keys, kbuf), (values, vbuf)))
        ]

    def fetch(row, carry):
        for side in range(2):
            for copy in copies(row, side):
                copy.start()
        return carry

    def work(step, carry):
        slots = [(step * together + index, side) for index in range(together) for side in range(2)]
        for row, side in slots:
            for copy in copies(row, side):
                copy.wait()
        places = [
            [(out, head) for out, width in zip(arrays, sizes) for head in range(width)]
            for arrays, sizes in ((outs[: len(widths)], widths), (outs[len(widths) :], swaps))
        ]
        for row, side in slots:
            for first in range(0, total, 2):
                size = min(2, total - first)
                cols = slice(first * HEAD, (first + size) * HEAD)
                both = lax.dot_general(
                    kbuf[2 * row + side, :, cols],
                    vbuf[2 * row + side, :, cols],
                    (((0,), (0,)), ((), ())),
                    preferred_element_type=jnp.float32,
                )
                for index in range(first, first + size):
                    part = slice((index - first) * HEAD, (index - first + 1) * HEAD)
                    out, head = places[side][index]
                    out[row, head] = both[part, part].astype(out.dtype)
        return carry

    lax.fori_loop(0, n // 2, fetch, 0)
    lax.fori_loop(0, n // 2 // together, work, 0)


def local_states(place, keys, values, n, low, widths, swaps):
    rows, m, total = keys.shape[0], n // 2, sum(widths)
    buf = pltpu.VMEM((n, rows, total * HEAD), keys.dtype)
    shapes = [jax.ShapeDtypeStruct((m, width, HEAD, HEAD), jnp.float32) for width in widths]
    shapes += [jax.ShapeDtypeStruct((m, width, HEAD, HEAD), jnp.bfloat16) for width in swaps]
    return pl.pallas_call(
        functools.partial(local_body, n, widths, swaps),
        in_specs=[pl.BlockSpec(memory_space=pltpu.SMEM)] * 2 + [pl.BlockSpec(memory_space=pltpu.HBM)] * 2,
        out_specs=[pl.BlockSpec(memory_space=pltpu.VMEM)] * len(shapes),
        out_shape=shapes,
        scratch_shapes=[buf, buf, pltpu.SemaphoreType.DMA((2, n))],
        compiler_params=params(4 * n * rows * total * HEAD + 3 * n * total * HEAD * HEAD),
        cost_estimate=pl.CostEstimate(
            flops=2 * n * total * rows * HEAD * HEAD, bytes_accessed=4 * rows * n * total * HEAD, transcendentals=0
        ),
        name="local",
    )(place, jnp.full((1,), low, jnp.int32), keys, values)


def masked_scores(query, key):
    rows = query.shape[0]
    tiles = []
    for low in range(0, rows, TILE):
        high = min(low + TILE, rows)
        part = lax.dot_general(
            query[low:], key[low:high], (((1,), (1,)), ((), ())), preferred_element_type=jnp.float32
        )
        size = high - low
        spot = lax.broadcasted_iota(jnp.int32, (size, size), 0)
        other = lax.broadcasted_iota(jnp.int32, (size, size), 1)
        pieces = [jnp.where(other <= spot, part[:size], 0.0).astype(jnp.bfloat16)]
        if low:
            pieces.insert(0, jnp.zeros((low, size), jnp.bfloat16))
        if high < rows:
            pieces.append(part[size:].astype(jnp.bfloat16))
        tiles.append(jnp.concatenate(pieces, axis=0) if len(pieces) > 1 else pieces[0])
    return tiles


def attend_body(n, spans, order, place, low, queries, keys, values, gain, *refs):
    states, outs = refs[: 2 * len(spans)], refs[2 * len(spans) :][:n]
    qbuf, kbuf, vbuf, sown, soth, gbuf, held, sems, extra = refs[-9:]
    width = sum(size for _, size in spans)
    m, wide = n // 2, width * HEAD
    together = rows_together(m, width, 12)
    here = place[0], place[1], low[0]
    small, start = [(gain, gbuf)], 0
    for chunk, (skip, size) in enumerate(spans):
        for source, buf in ((states[2 * chunk], sown), (states[2 * chunk + 1], soth)):
            small.append((source.at[:, skip : skip + size], buf.at[:, start : start + size]))
        start += size
    small = [pltpu.make_async_copy(source, buf, extra.at[which]) for which, (source, buf) in enumerate(small)]

    def copies(step, side):
        cols = pl.ds(column(here, lax.rem(here[0] + step, m), side, n), wide)
        slot = 2 * step + side
        return [
            pltpu.make_async_copy(source.at[:, cols], buf.at[slot], sems.at[which, slot])
            for which, (source, buf) in enumerate(((queries, qbuf), (keys, kbuf), (values, vbuf)))
        ]

    def sends(step):
        return [
            pltpu.make_async_copy(held.at[slot], outs[order.index(slot)], sems.at[3, slot])
            for slot in (2 * step, 2 * step + 1)
        ]

    def fetch(step, carry):
        for side in range(2):
            for copy in copies(step, side):
                copy.start()
        return carry

    def work(group, carry):
        steps = [group * together + index for index in range(together)]
        for step in steps:
            for side in range(2):
                for copy in copies(step, side):
                    copy.wait()
        heads = [
            (step, side, head, slice(head * HEAD, (head + 1) * HEAD))
            for step in steps
            for side in range(2)
            for head in range(width)
        ]
        scores = [
            masked_scores(qbuf[2 * step + side, :, cols], kbuf[2 * step + side, :, cols])
            for step, side, _, cols in heads
        ]
        attended = []
        for (step, side, head, cols), tiles in zip(heads, scores):
            slot = 2 * step + side
            state = (sown if side == 0 else soth)[lax.rem(here[0] + step, m), head]
            left = jnp.concatenate([*tiles, qbuf[slot, :, cols]], axis=1)
            right = jnp.concatenate([vbuf[slot, :, cols], state], axis=0)
            attended.append(jnp.dot(left, right, preferred_element_type=jnp.float32))
        for (step, side, head, cols), value in zip(heads, attended):
            square = jnp.mean(value * value, axis=-1, keepdims=True)
            begin = pl.multiple_of(column(here, lax.rem(here[0] + step, m), side, n) + head * HEAD, HEAD)
            mixed = value * lax.rsqrt(square + 1e-05) * gbuf[:, pl.ds(begin, HEAD)]
            held[2 * step + side, :, cols] = mixed.astype(held.dtype)
        for fixed in range(m // together):

            @pl.when(group == fixed)
            def _(fixed=fixed):
                for index in range(together):
                    for copy in sends(fixed * together + index):
                        copy.start()

        return carry

    lax.fori_loop(0, 1, fetch, 0)
    for copy in small:
        copy.start()
    lax.fori_loop(1, m, fetch, 0)
    for copy in small:
        copy.wait()
    lax.fori_loop(0, m // together, work, 0)
    for step in range(m):
        for copy in sends(step):
            copy.wait()


def attend(place, queries, keys, values, gain, states, spans, order, n, low):
    rows, m = queries.shape[0], n // 2
    width = sum(size for _, size in spans)
    wide = width * HEAD
    tokens = pltpu.VMEM((n, rows, wide), jnp.bfloat16)
    state = pltpu.VMEM((m, width, HEAD, HEAD), jnp.bfloat16)
    return pl.pallas_call(
        functools.partial(attend_body, n, spans, order),
        in_specs=[pl.BlockSpec(memory_space=pltpu.SMEM)] * 2
        + [pl.BlockSpec(memory_space=pltpu.HBM)] * 3
        + [pl.BlockSpec(memory_space=pl.ANY)] * (1 + 2 * len(states)),
        out_specs=[pl.BlockSpec(memory_space=pltpu.HBM)] * n,
        out_shape=[jax.ShapeDtypeStruct((rows, wide), jnp.bfloat16)] * n,
        scratch_shapes=[
            tokens,
            tokens,
            tokens,
            state,
            state,
            pltpu.VMEM((1, HEADS * HEAD), jnp.float32),
            tokens,
            pltpu.SemaphoreType.DMA((4, n)),
            pltpu.SemaphoreType.DMA((1 + 2 * len(states),)),
        ],
        compiler_params=params(8 * n * rows * wide + 2 * n * width * HEAD * HEAD + 4 * HEADS * HEAD),
        cost_estimate=pl.CostEstimate(
            flops=2 * n * width * rows * HEAD * (2 * rows + HEAD),
            bytes_accessed=8 * rows * n * wide,
            transcendentals=n * width * rows,
        ),
        name="attend",
    )(place, jnp.full((1,), low, jnp.int32), queries, keys, values, gain, *(array for pair in states for array in pair))


def put_body(n, order, place, low, *refs):
    parts, out, again, sems = refs[:n], refs[-3], refs[-2], refs[-1]
    m = n // 2
    rows, wide = parts[0].shape
    cols = pl.ds(pl.multiple_of(low[0] * HEAD, HEAD), wide)
    copies = []
    for index, shift in enumerate(order):
        row = lax.rem(place[0] + m - shift // 2, m)
        col = place[1] if shift % 2 == 0 else 1 - place[1]
        start = pl.multiple_of((2 * row + col) * rows, rows)
        copies.append(
            pltpu.make_async_copy(parts[index], out.at[pl.ds(start, rows), cols], sems.at[index])
        )
    for copy in copies:
        copy.start()
    for index in range(2):
        again[index] = place[index]
    for copy in copies:
        copy.wait()


def put(place, parts, out, order, n, low):
    rows, first = parts[0].shape[0], out is None
    anywhere = pl.BlockSpec(memory_space=pltpu.HBM)
    return pl.pallas_call(
        functools.partial(put_body, n, order),
        in_specs=[pl.BlockSpec(memory_space=pltpu.SMEM)] * 2 + [anywhere] * (n if first else n + 1),
        out_specs=[anywhere, pl.BlockSpec(memory_space=pltpu.SMEM)],
        out_shape=[
            jax.ShapeDtypeStruct((n * rows, HEADS // n * HEAD), jnp.bfloat16),
            jax.ShapeDtypeStruct((2,), jnp.int32),
        ],
        scratch_shapes=[pltpu.SemaphoreType.DMA((n,))],
        input_output_aliases={} if first else {n + 2: 0},
        compiler_params=params(),
        name="put",
    )(place, jnp.full((1,), low, jnp.int32), *parts, *(() if first else (out,)))


def split(widths, per_dest):
    chunks, low = [], 0
    for width in widths:
        if low < per_dest:
            width = min(width, per_dest - low)
            chunks.append((low, width))
            low += width
    return chunks


def inside(chunks, low, width):
    return [c for c, (start, _) in enumerate(chunks) if low <= start < low + width]


class Plan:
    def __init__(self, n, queries, keys, values, gain):
        self.n, self.m = n, n // 2
        me = lax.axis_index("seq")
        self.col = me % 2
        self.place = jnp.stack([me // 2, self.col]).astype(jnp.int32)
        self.arrays = tuple(pltpu.with_memory_space_constraint(x, pltpu.HBM) for x in (queries, keys, values))
        self.gain = gain.reshape(1, HEADS * HEAD)
        self.groups, self.swaps, self.parts, self.chunks = (
            split(widths, HEADS // n) for widths in (LOCAL, SWAP, PREFIX, MIXED)
        )
        self.shifts = sorted(range(1, n), key=lambda k: (-min(k // 2, self.m - k // 2), k))
        self.made = {}

    def has(self, key):
        limit = {"message": self.m, "prefix": self.m, "sent": self.n - 1}.get(key[0], 0)
        chunks = {"group": self.groups, "swap": self.swaps, "mixed": self.chunks, "sent": self.chunks}
        chunks = chunks.get(key[0], self.parts)
        return key[1] < len(chunks) and (len(key) < 3 or key[2] <= limit)

    def get(self, *key):
        if key not in self.made:
            self.made[key] = getattr(self, key[0])(*key[1:])
        return self.made[key]

    def hold(self, value, *key):
        others = []
        for other in ORDER.get(key, ()):
            if self.has(other):
                result = self.get(*other)
                while isinstance(result, (list, tuple)):
                    result = result[-1]
                others.append(result)
        return lax.optimization_barrier((value, *others))[0] if others else value

    def group(self, g):
        low, width = self.groups[g]
        widths = tuple(self.parts[c][1] for c in inside(self.parts, low, width))
        swaps = tuple(self.swaps[c][1] for c in inside(self.swaps, low, width))
        _, keys, values = self.arrays
        place = self.hold(self.place, "group", g)
        arrays = local_states(place, keys, values, self.n, low, widths, swaps)
        return arrays[: len(widths)], arrays[len(widths) :]

    def around(self, chunks, low):
        return next(c for c, (start, width) in enumerate(chunks) if start <= low < start + width)

    def swap(self, w):
        g = self.around(self.groups, self.swaps[w][0])
        spot = inside(self.swaps, *self.groups[g]).index(w)
        other = self.hold(self.get("group", g)[1][spot], "swap", w)
        return lax.ppermute(other, "seq", [(d, d ^ 1) for d in range(self.n)])

    def local(self, c):
        low, width = self.parts[c]
        g, w = self.around(self.groups, low), self.around(self.swaps, low)
        near = self.get("swap", w)[:, low - self.swaps[w][0] :][:, :width].astype(jnp.float32)
        return self.get("group", g)[0][inside(self.parts, *self.groups[g]).index(c)], near

    def total(self, c):
        parts = [self.get("prefix", c, s) for s in range(1, self.m)]
        return sum(parts[1:], parts[0]).astype(jnp.float32)

    def message(self, c, s):
        own, near = self.get("local", c)
        if s == self.m:
            value = self.get("total", c) + jnp.where(self.col == 0, own, 0.0)
        else:
            value = own + near
            if s > 1:
                value = self.get("prefix", c, s - 1).astype(jnp.float32) + value
        return self.hold(value.astype(jnp.bfloat16), "message", c, s)

    def prefix(self, c, s):
        if s == self.m:
            pairs = [(d, d ^ 1) for d in range(self.n)]
        else:
            pairs = [(2 * (s - 1) + y, 2 * s + y) for y in range(2)]
        return lax.ppermute(self.get("message", c, s), "seq", pairs)

    def states(self, c):
        _, near = self.get("local", c)
        own = (self.get("total", c) + jnp.where(self.col == 1, near, 0.0)).astype(jnp.bfloat16)
        return own, self.get("prefix", c, self.m)

    def mixed(self, c):
        low, width = self.chunks[c]
        place = self.get("put", c - 3)[1] if c > 2 else self.place
        place = self.hold(place, "mixed", c)
        states, spans = [], []
        for part, (start, size) in enumerate(self.parts):
            first, last = max(low, start), min(low + width, start + size)
            if first < last:
                states.append(self.get("states", part))
                spans.append((first - start, last - first))
        return attend(place, *self.arrays, self.gain, states, tuple(spans), (0, *self.shifts), self.n, low)

    def sent(self, c, k):
        shift = self.shifts[k - 1]
        pairs = [
            (2 * z + y, 2 * ((z + shift // 2) % self.m) + (y + shift) % 2) for z in range(self.m) for y in range(2)
        ]
        return lax.ppermute(self.hold(self.get("mixed", c)[k], "sent", c, k), "seq", pairs)

    def put(self, c):
        parts = [self.get("mixed", c)[0]] + [self.get("sent", c, k) for k in range(1, self.n)]
        out = self.get("put", c - 1)[0] if c else None
        return put(self.place, parts, out, (0, *self.shifts), self.n, self.chunks[c][0])


def per_device(n, *arrays):
    plan = Plan(n, *arrays)
    return plan.get("put", len(plan.chunks) - 1)[0]


def solution(mesh):
    tokens = P(("batch", "seq"), None)
    return jax.shard_map(
        functools.partial(per_device, mesh.shape["seq"]),
        mesh=mesh,
        in_specs=(tokens, tokens, tokens, P()),
        out_specs=P("batch", "seq"),
        check_vma=False,
    )
```

```python
import functools

import jax
import jax.numpy as jnp
from jax import lax
from jax.experimental import pallas as pl
from jax.experimental.pallas import tpu as pltpu
from jax.sharding import PartitionSpec as P

HEADS = 64
HEAD = 128
LOCAL = (2, 6)
SWAP = (2, 3, 3)
PREFIX = (2, 3, 3)
MIXED = (2, 3, 3)
TILE = 256
SPARE = 8 * 1024 * 1024
ORDER = {
    ("message", 0, 1): [("group", 1)],
    ("message", 1, 1): [("message", 0, 2)],
    ("message", 1, 2): [("message", 0, 3)],
    ("message", 1, 3): [("message", 0, 4)],
    ("message", 2, 1): [("message", 1, 2)],
    ("message", 2, 2): [("message", 1, 3)],
    ("message", 2, 3): [("message", 1, 4), ("mixed", 0)],
    ("mixed", 0): [("message", 1, 3), ("message", 2, 2)],
    ("message", 1, 4): [("mixed", 0)],
}


def params(buffers=0):
    return pltpu.CompilerParams(vmem_limit_bytes=buffers + SPARE)


def column(place, row, side, n):
    col = place[1] if side == 0 else 1 - place[1]
    return pl.multiple_of(((2 * row + col) * (HEADS // n) + place[2]) * HEAD, HEAD)


def rows_together(m, width, most):
    return max(count for count in range(1, m + 1) if m % count == 0 and (count == 1 or 2 * width * count <= most))


def local_body(n, widths, swaps, place, low, keys, values, *refs):
    outs, (kbuf, vbuf, sems) = refs[:-3], refs[-3:]
    total = sum(widths)
    here = place[0], place[1], low[0]
    together = rows_together(n // 2, total, 16)

    def copies(row, side):
        cols = pl.ds(column(here, row, side, n), total * HEAD)
        slot = 2 * row + side
        return [
            pltpu.make_async_copy(source.at[:, cols], buf.at[slot], sems.at[which, slot])
            for which, (source, buf) in enumerate(((keys, kbuf), (values, vbuf)))
        ]

    def fetch(row, carry):
        for side in range(2):
            for copy in copies(row, side):
                copy.start()
        return carry

    def work(step, carry):
        slots = [(step * together + index, side) for index in range(together) for side in range(2)]
        for row, side in slots:
            for copy in copies(row, side):
                copy.wait()
        places = [
            [(out, head) for out, width in zip(arrays, sizes) for head in range(width)]
            for arrays, sizes in ((outs[: len(widths)], widths), (outs[len(widths) :], swaps))
        ]
        for row, side in slots:
            for first in range(0, total, 2):
                size = min(2, total - first)
                cols = slice(first * HEAD, (first + size) * HEAD)
                both = lax.dot_general(
                    kbuf[2 * row + side, :, cols],
                    vbuf[2 * row + side, :, cols],
                    (((0,), (0,)), ((), ())),
                    preferred_element_type=jnp.float32,
                )
                for index in range(first, first + size):
                    part = slice((index - first) * HEAD, (index - first + 1) * HEAD)
                    out, head = places[side][index]
                    out[row, head] = both[part, part].astype(out.dtype)
        return carry

    lax.fori_loop(0, n // 2, fetch, 0)
    lax.fori_loop(0, n // 2 // together, work, 0)


def local_states(place, keys, values, n, low, widths, swaps):
    rows, m, total = keys.shape[0], n // 2, sum(widths)
    buf = pltpu.VMEM((n, rows, total * HEAD), keys.dtype)
    shapes = [jax.ShapeDtypeStruct((m, width, HEAD, HEAD), jnp.float32) for width in widths]
    shapes += [jax.ShapeDtypeStruct((m, width, HEAD, HEAD), jnp.bfloat16) for width in swaps]
    return pl.pallas_call(
        functools.partial(local_body, n, widths, swaps),
        in_specs=[pl.BlockSpec(memory_space=pltpu.SMEM)] * 2 + [pl.BlockSpec(memory_space=pltpu.HBM)] * 2,
        out_specs=[pl.BlockSpec(memory_space=pltpu.VMEM)] * len(shapes),
        out_shape=shapes,
        scratch_shapes=[buf, buf, pltpu.SemaphoreType.DMA((2, n))],
        compiler_params=params(4 * n * rows * total * HEAD + 3 * n * total * HEAD * HEAD),
        cost_estimate=pl.CostEstimate(
            flops=2 * n * total * rows * HEAD * HEAD, bytes_accessed=4 * rows * n * total * HEAD, transcendentals=0
        ),
        name="local",
    )(place, jnp.full((1,), low, jnp.int32), keys, values)


def masked_scores(query, key):
    rows = query.shape[0]
    tiles = []
    for low in range(0, rows, TILE):
        high = min(low + TILE, rows)
        part = lax.dot_general(
            query[low:], key[low:high], (((1,), (1,)), ((), ())), preferred_element_type=jnp.float32
        )
        size = high - low
        spot = lax.broadcasted_iota(jnp.int32, (size, size), 0)
        other = lax.broadcasted_iota(jnp.int32, (size, size), 1)
        pieces = [jnp.where(other <= spot, part[:size], 0.0).astype(jnp.bfloat16)]
        if low:
            pieces.insert(0, jnp.zeros((low, size), jnp.bfloat16))
        if high < rows:
            pieces.append(part[size:].astype(jnp.bfloat16))
        tiles.append(jnp.concatenate(pieces, axis=0) if len(pieces) > 1 else pieces[0])
    return tiles


def attend_body(n, spans, order, place, low, queries, keys, values, gain, *refs):
    states, outs = refs[: 2 * len(spans)], refs[2 * len(spans) :][:n]
    qbuf, kbuf, vbuf, sown, soth, gbuf, held, sems, extra = refs[-9:]
    width = sum(size for _, size in spans)
    m, wide = n // 2, width * HEAD
    together = rows_together(m, width, 12)
    here = place[0], place[1], low[0]
    small, start = [(gain, gbuf)], 0
    for chunk, (skip, size) in enumerate(spans):
        for source, buf in ((states[2 * chunk], sown), (states[2 * chunk + 1], soth)):
            small.append((source.at[:, skip : skip + size], buf.at[:, start : start + size]))
        start += size
    small = [pltpu.make_async_copy(source, buf, extra.at[which]) for which, (source, buf) in enumerate(small)]

    def copies(step, side):
        cols = pl.ds(column(here, lax.rem(here[0] + step, m), side, n), wide)
        slot = 2 * step + side
        return [
            pltpu.make_async_copy(source.at[:, cols], buf.at[slot], sems.at[which, slot])
            for which, (source, buf) in enumerate(((queries, qbuf), (keys, kbuf), (values, vbuf)))
        ]

    def sends(step):
        return [
            pltpu.make_async_copy(held.at[slot], outs[order.index(slot)], sems.at[3, slot])
            for slot in (2 * step, 2 * step + 1)
        ]

    def fetch(step, carry):
        for side in range(2):
            for copy in copies(step, side):
                copy.start()
        return carry

    def work(group, carry):
        steps = [group * together + index for index in range(together)]
        for step in steps:
            for side in range(2):
                for copy in copies(step, side):
                    copy.wait()
        heads = [
            (step, side, head, slice(head * HEAD, (head + 1) * HEAD))
            for step in steps
            for side in range(2)
            for head in range(width)
        ]
        scores = [
            masked_scores(qbuf[2 * step + side, :, cols], kbuf[2 * step + side, :, cols])
            for step, side, _, cols in heads
        ]
        attended = []
        for (step, side, head, cols), tiles in zip(heads, scores):
            slot = 2 * step + side
            state = (sown if side == 0 else soth)[lax.rem(here[0] + step, m), head]
            left = jnp.concatenate([*tiles, qbuf[slot, :, cols]], axis=1)
            right = jnp.concatenate([vbuf[slot, :, cols], state], axis=0)
            attended.append(jnp.dot(left, right, preferred_element_type=jnp.float32))
        for (step, side, head, cols), value in zip(heads, attended):
            square = jnp.mean(value * value, axis=-1, keepdims=True)
            begin = pl.multiple_of(column(here, lax.rem(here[0] + step, m), side, n) + head * HEAD, HEAD)
            mixed = value * lax.rsqrt(square + 1e-05) * gbuf[:, pl.ds(begin, HEAD)]
            held[2 * step + side, :, cols] = mixed.astype(held.dtype)
        for fixed in range(m // together):

            @pl.when(group == fixed)
            def _(fixed=fixed):
                for index in range(together):
                    for copy in sends(fixed * together + index):
                        copy.start()

        return carry

    lax.fori_loop(0, 1, fetch, 0)
    for copy in small:
        copy.start()
    lax.fori_loop(1, m, fetch, 0)
    for copy in small:
        copy.wait()
    lax.fori_loop(0, m // together, work, 0)
    for step in range(m):
        for copy in sends(step):
            copy.wait()


def attend(place, queries, keys, values, gain, states, spans, order, n, low):
    rows, m = queries.shape[0], n // 2
    width = sum(size for _, size in spans)
    wide = width * HEAD
    tokens = pltpu.VMEM((n, rows, wide), jnp.bfloat16)
    state = pltpu.VMEM((m, width, HEAD, HEAD), jnp.bfloat16)
    return pl.pallas_call(
        functools.partial(attend_body, n, spans, order),
        in_specs=[pl.BlockSpec(memory_space=pltpu.SMEM)] * 2
        + [pl.BlockSpec(memory_space=pltpu.HBM)] * 3
        + [pl.BlockSpec(memory_space=pl.ANY)] * (1 + 2 * len(states)),
        out_specs=[pl.BlockSpec(memory_space=pltpu.HBM)] * n,
        out_shape=[jax.ShapeDtypeStruct((rows, wide), jnp.bfloat16)] * n,
        scratch_shapes=[
            tokens,
            tokens,
            tokens,
            state,
            state,
            pltpu.VMEM((1, HEADS * HEAD), jnp.float32),
            tokens,
            pltpu.SemaphoreType.DMA((4, n)),
            pltpu.SemaphoreType.DMA((1 + 2 * len(states),)),
        ],
        compiler_params=params(8 * n * rows * wide + 2 * n * width * HEAD * HEAD + 4 * HEADS * HEAD),
        cost_estimate=pl.CostEstimate(
            flops=2 * n * width * rows * HEAD * (2 * rows + HEAD),
            bytes_accessed=8 * rows * n * wide,
            transcendentals=n * width * rows,
        ),
        name="attend",
    )(place, jnp.full((1,), low, jnp.int32), queries, keys, values, gain, *(array for pair in states for array in pair))


def put_body(n, order, place, low, *refs):
    parts, out, again, sems = refs[:n], refs[-3], refs[-2], refs[-1]
    m = n // 2
    rows, wide = parts[0].shape
    cols = pl.ds(pl.multiple_of(low[0] * HEAD, HEAD), wide)
    copies = []
    for index, shift in enumerate(order):
        row = lax.rem(place[0] + m - shift // 2, m)
        col = place[1] if shift % 2 == 0 else 1 - place[1]
        start = pl.multiple_of((2 * row + col) * rows, rows)
        copies.append(
            pltpu.make_async_copy(parts[index], out.at[pl.ds(start, rows), cols], sems.at[index])
        )
    for copy in copies:
        copy.start()
    for index in range(2):
        again[index] = place[index]
    for copy in copies:
        copy.wait()


def put(place, parts, out, order, n, low):
    rows, first = parts[0].shape[0], out is None
    anywhere = pl.BlockSpec(memory_space=pltpu.HBM)
    return pl.pallas_call(
        functools.partial(put_body, n, order),
        in_specs=[pl.BlockSpec(memory_space=pltpu.SMEM)] * 2 + [anywhere] * (n if first else n + 1),
        out_specs=[anywhere, pl.BlockSpec(memory_space=pltpu.SMEM)],
        out_shape=[
            jax.ShapeDtypeStruct((n * rows, HEADS // n * HEAD), jnp.bfloat16),
            jax.ShapeDtypeStruct((2,), jnp.int32),
        ],
        scratch_shapes=[pltpu.SemaphoreType.DMA((n,))],
        input_output_aliases={} if first else {n + 2: 0},
        compiler_params=params(),
        name="put",
    )(place, jnp.full((1,), low, jnp.int32), *parts, *(() if first else (out,)))


def split(widths, per_dest):
    chunks, low = [], 0
    for width in widths:
        if low < per_dest:
            width = min(width, per_dest - low)
            chunks.append((low, width))
            low += width
    return chunks


def inside(chunks, low, width):
    return [c for c, (start, _) in enumerate(chunks) if low <= start < low + width]


class Plan:
    def __init__(self, n, queries, keys, values, gain):
        self.n, self.m = n, n // 2
        me = lax.axis_index("seq")
        self.col = me % 2
        self.place = jnp.stack([me // 2, self.col]).astype(jnp.int32)
        self.arrays = tuple(pltpu.with_memory_space_constraint(x, pltpu.HBM) for x in (queries, keys, values))
        self.gain = gain.reshape(1, HEADS * HEAD)
        self.groups, self.swaps, self.parts, self.chunks = (
            split(widths, HEADS // n) for widths in (LOCAL, SWAP, PREFIX, MIXED)
        )
        self.shifts = sorted(range(1, n), key=lambda k: (-min(k // 2, self.m - k // 2), k))
        self.made = {}

    def has(self, key):
        limit = {"message": self.m, "prefix": self.m, "sent": self.n - 1}.get(key[0], 0)
        chunks = {"group": self.groups, "swap": self.swaps, "mixed": self.chunks, "sent": self.chunks}
        chunks = chunks.get(key[0], self.parts)
        return key[1] < len(chunks) and (len(key) < 3 or key[2] <= limit)

    def get(self, *key):
        if key not in self.made:
            self.made[key] = getattr(self, key[0])(*key[1:])
        return self.made[key]

    def hold(self, value, *key):
        others = []
        for other in ORDER.get(key, ()):
            if self.has(other):
                result = self.get(*other)
                while isinstance(result, (list, tuple)):
                    result = result[-1]
                others.append(result)
        return lax.optimization_barrier((value, *others))[0] if others else value

    def group(self, g):
        low, width = self.groups[g]
        widths = tuple(self.parts[c][1] for c in inside(self.parts, low, width))
        swaps = tuple(self.swaps[c][1] for c in inside(self.swaps, low, width))
        _, keys, values = self.arrays
        place = self.hold(self.place, "group", g)
        arrays = local_states(place, keys, values, self.n, low, widths, swaps)
        return arrays[: len(widths)], arrays[len(widths) :]

    def around(self, chunks, low):
        return next(c for c, (start, width) in enumerate(chunks) if start <= low < start + width)

    def swap(self, w):
        g = self.around(self.groups, self.swaps[w][0])
        spot = inside(self.swaps, *self.groups[g]).index(w)
        other = self.hold(self.get("group", g)[1][spot], "swap", w)
        return lax.ppermute(other, "seq", [(d, d ^ 1) for d in range(self.n)])

    def local(self, c):
        low, width = self.parts[c]
        g, w = self.around(self.groups, low), self.around(self.swaps, low)
        near = self.get("swap", w)[:, low - self.swaps[w][0] :][:, :width].astype(jnp.float32)
        return self.get("group", g)[0][inside(self.parts, *self.groups[g]).index(c)], near

    def total(self, c):
        parts = [self.get("prefix", c, s) for s in range(1, self.m)]
        return sum(parts[1:], parts[0]).astype(jnp.float32)

    def message(self, c, s):
        own, near = self.get("local", c)
        if s == self.m:
            value = self.get("total", c) + jnp.where(self.col == 0, own, 0.0)
        else:
            value = own + near
            if s > 1:
                value = self.get("prefix", c, s - 1).astype(jnp.float32) + value
        return self.hold(value.astype(jnp.bfloat16), "message", c, s)

    def prefix(self, c, s):
        if s == self.m:
            pairs = [(d, d ^ 1) for d in range(self.n)]
        else:
            pairs = [(2 * (s - 1) + y, 2 * s + y) for y in range(2)]
        return lax.ppermute(self.get("message", c, s), "seq", pairs)

    def states(self, c):
        _, near = self.get("local", c)
        own = (self.get("total", c) + jnp.where(self.col == 1, near, 0.0)).astype(jnp.bfloat16)
        return own, self.get("prefix", c, self.m)

    def mixed(self, c):
        low, width = self.chunks[c]
        place = self.get("put", c - 3)[1] if c > 2 else self.place
        place = self.hold(place, "mixed", c)
        states, spans = [], []
        for part, (start, size) in enumerate(self.parts):
            first, last = max(low, start), min(low + width, start + size)
            if first < last:
                states.append(self.get("states", part))
                spans.append((first - start, last - first))
        return attend(place, *self.arrays, self.gain, states, tuple(spans), (0, *self.shifts), self.n, low)

    def sent(self, c, k):
        shift = self.shifts[k - 1]
        pairs = [
            (2 * z + y, 2 * ((z + shift // 2) % self.m) + (y + shift) % 2) for z in range(self.m) for y in range(2)
        ]
        return lax.ppermute(self.hold(self.get("mixed", c)[k], "sent", c, k), "seq", pairs)

    def put(self, c):
        parts = [self.get("mixed", c)[0]] + [self.get("sent", c, k) for k in range(1, self.n)]
        out = self.get("put", c - 1)[0] if c else None
        return put(self.place, parts, out, (0, *self.shifts), self.n, self.chunks[c][0])


def per_device(n, *arrays):
    plan = Plan(n, *arrays)
    return plan.get("put", len(plan.chunks) - 1)[0]


def solution(mesh):
    tokens = P(("batch", "seq"), None)
    return jax.shard_map(
        functools.partial(per_device, mesh.shape["seq"]),
        mesh=mesh,
        in_specs=(tokens, tokens, tokens, P()),
        out_specs=P("batch", "seq"),
        check_vma=False,
    )
```

```python
import functools

import jax
import jax.numpy as jnp
from jax import lax
from jax.experimental import pallas as pl
from jax.experimental.pallas import tpu as pltpu
from jax.sharding import PartitionSpec as P

HEADS = 64
HEAD = 128
LOCAL = (1, 7)
SWAP = (1, 2, 2, 3)
PREFIX = (1, 2, 2, 3)
MIXED = (1, 2, 2, 3)
TILE = 256
SPARE = 8 * 1024 * 1024
ORDER = {
    ("message", 0, 1): [("group", 1)],
    ("message", 1, 1): [("message", 0, 2)],
    ("message", 1, 2): [("message", 0, 3)],
    ("message", 1, 3): [("message", 0, 4)],
    ("message", 2, 1): [("message", 1, 2)],
    ("message", 2, 2): [("message", 1, 3)],
    ("message", 2, 3): [("message", 1, 4)],
    ("message", 3, 1): [("message", 2, 2)],
    ("message", 3, 2): [("message", 2, 3)],
    ("message", 3, 3): [("message", 2, 4), ("mixed", 0)],
    ("mixed", 0): [("message", 1, 4), ("message", 2, 3), ("message", 3, 2)],
    ("message", 2, 4): [("mixed", 0)],
}


def params(buffers=0):
    return pltpu.CompilerParams(vmem_limit_bytes=buffers + SPARE)


def column(place, row, side, n):
    col = place[1] if side == 0 else 1 - place[1]
    return pl.multiple_of(((2 * row + col) * (HEADS // n) + place[2]) * HEAD, HEAD)


def rows_together(m, width, most):
    return max(count for count in range(1, m + 1) if m % count == 0 and (count == 1 or 2 * width * count <= most))


def local_body(n, widths, swaps, place, low, keys, values, *refs):
    outs, (kbuf, vbuf, sems) = refs[:-3], refs[-3:]
    total = sum(widths)
    here = place[0], place[1], low[0]
    together = rows_together(n // 2, total, 16)

    def copies(row, side):
        cols = pl.ds(column(here, row, side, n), total * HEAD)
        slot = 2 * row + side
        return [
            pltpu.make_async_copy(source.at[:, cols], buf.at[slot], sems.at[which, slot])
            for which, (source, buf) in enumerate(((keys, kbuf), (values, vbuf)))
        ]

    def fetch(row, carry):
        for side in range(2):
            for copy in copies(row, side):
                copy.start()
        return carry

    def work(step, carry):
        slots = [(step * together + index, side) for index in range(together) for side in range(2)]
        for row, side in slots:
            for copy in copies(row, side):
                copy.wait()
        places = [
            [(out, head) for out, width in zip(arrays, sizes) for head in range(width)]
            for arrays, sizes in ((outs[: len(widths)], widths), (outs[len(widths) :], swaps))
        ]
        for row, side in slots:
            for first in range(0, total, 2):
                size = min(2, total - first)
                cols = slice(first * HEAD, (first + size) * HEAD)
                both = lax.dot_general(
                    kbuf[2 * row + side, :, cols],
                    vbuf[2 * row + side, :, cols],
                    (((0,), (0,)), ((), ())),
                    preferred_element_type=jnp.float32,
                )
                for index in range(first, first + size):
                    part = slice((index - first) * HEAD, (index - first + 1) * HEAD)
                    out, head = places[side][index]
                    out[row, head] = both[part, part].astype(out.dtype)
        return carry

    lax.fori_loop(0, n // 2, fetch, 0)
    lax.fori_loop(0, n // 2 // together, work, 0)


def local_states(place, keys, values, n, low, widths, swaps):
    rows, m, total = keys.shape[0], n // 2, sum(widths)
    buf = pltpu.VMEM((n, rows, total * HEAD), keys.dtype)
    shapes = [jax.ShapeDtypeStruct((m, width, HEAD, HEAD), jnp.float32) for width in widths]
    shapes += [jax.ShapeDtypeStruct((m, width, HEAD, HEAD), jnp.bfloat16) for width in swaps]
    return pl.pallas_call(
        functools.partial(local_body, n, widths, swaps),
        in_specs=[pl.BlockSpec(memory_space=pltpu.SMEM)] * 2 + [pl.BlockSpec(memory_space=pltpu.HBM)] * 2,
        out_specs=[pl.BlockSpec(memory_space=pltpu.VMEM)] * len(shapes),
        out_shape=shapes,
        scratch_shapes=[buf, buf, pltpu.SemaphoreType.DMA((2, n))],
        compiler_params=params(4 * n * rows * total * HEAD + 3 * n * total * HEAD * HEAD),
        cost_estimate=pl.CostEstimate(
            flops=2 * n * total * rows * HEAD * HEAD, bytes_accessed=4 * rows * n * total * HEAD, transcendentals=0
        ),
        name="local",
    )(place, jnp.full((1,), low, jnp.int32), keys, values)


def masked_scores(query, key):
    rows = query.shape[0]
    tiles = []
    for low in range(0, rows, TILE):
        high = min(low + TILE, rows)
        part = lax.dot_general(
            query[low:], key[low:high], (((1,), (1,)), ((), ())), preferred_element_type=jnp.float32
        )
        size = high - low
        spot = lax.broadcasted_iota(jnp.int32, (size, size), 0)
        other = lax.broadcasted_iota(jnp.int32, (size, size), 1)
        pieces = [jnp.where(other <= spot, part[:size], 0.0).astype(jnp.bfloat16)]
        if low:
            pieces.insert(0, jnp.zeros((low, size), jnp.bfloat16))
        if high < rows:
            pieces.append(part[size:].astype(jnp.bfloat16))
        tiles.append(jnp.concatenate(pieces, axis=0) if len(pieces) > 1 else pieces[0])
    return tiles


def attend_body(n, spans, order, place, low, queries, keys, values, gain, *refs):
    states, outs = refs[: 2 * len(spans)], refs[2 * len(spans) :][:n]
    qbuf, kbuf, vbuf, sown, soth, gbuf, held, sems, extra = refs[-9:]
    width = sum(size for _, size in spans)
    m, wide = n // 2, width * HEAD
    together = rows_together(m, width, 12)
    here = place[0], place[1], low[0]
    small, start = [(gain, gbuf)], 0
    for chunk, (skip, size) in enumerate(spans):
        for source, buf in ((states[2 * chunk], sown), (states[2 * chunk + 1], soth)):
            small.append((source.at[:, skip : skip + size], buf.at[:, start : start + size]))
        start += size
    small = [pltpu.make_async_copy(source, buf, extra.at[which]) for which, (source, buf) in enumerate(small)]

    def copies(step, side):
        cols = pl.ds(column(here, lax.rem(here[0] + step, m), side, n), wide)
        slot = 2 * step + side
        return [
            pltpu.make_async_copy(source.at[:, cols], buf.at[slot], sems.at[which, slot])
            for which, (source, buf) in enumerate(((queries, qbuf), (keys, kbuf), (values, vbuf)))
        ]

    def sends(step):
        return [
            pltpu.make_async_copy(held.at[slot], outs[order.index(slot)], sems.at[3, slot])
            for slot in (2 * step, 2 * step + 1)
        ]

    def fetch(step, carry):
        for side in range(2):
            for copy in copies(step, side):
                copy.start()
        return carry

    def work(group, carry):
        steps = [group * together + index for index in range(together)]
        for step in steps:
            for side in range(2):
                for copy in copies(step, side):
                    copy.wait()
        heads = [
            (step, side, head, slice(head * HEAD, (head + 1) * HEAD))
            for step in steps
            for side in range(2)
            for head in range(width)
        ]
        scores = [
            masked_scores(qbuf[2 * step + side, :, cols], kbuf[2 * step + side, :, cols])
            for step, side, _, cols in heads
        ]
        attended = []
        for (step, side, head, cols), tiles in zip(heads, scores):
            slot = 2 * step + side
            state = (sown if side == 0 else soth)[lax.rem(here[0] + step, m), head]
            left = jnp.concatenate([*tiles, qbuf[slot, :, cols]], axis=1)
            right = jnp.concatenate([vbuf[slot, :, cols], state], axis=0)
            attended.append(jnp.dot(left, right, preferred_element_type=jnp.float32))
        for (step, side, head, cols), value in zip(heads, attended):
            square = jnp.mean(value * value, axis=-1, keepdims=True)
            begin = pl.multiple_of(column(here, lax.rem(here[0] + step, m), side, n) + head * HEAD, HEAD)
            mixed = value * lax.rsqrt(square + 1e-05) * gbuf[:, pl.ds(begin, HEAD)]
            held[2 * step + side, :, cols] = mixed.astype(held.dtype)
        for fixed in range(m // together):

            @pl.when(group == fixed)
            def _(fixed=fixed):
                for index in range(together):
                    for copy in sends(fixed * together + index):
                        copy.start()

        return carry

    lax.fori_loop(0, 1, fetch, 0)
    for copy in small:
        copy.start()
    lax.fori_loop(1, m, fetch, 0)
    for copy in small:
        copy.wait()
    lax.fori_loop(0, m // together, work, 0)
    for step in range(m):
        for copy in sends(step):
            copy.wait()


def attend(place, queries, keys, values, gain, states, spans, order, n, low):
    rows, m = queries.shape[0], n // 2
    width = sum(size for _, size in spans)
    wide = width * HEAD
    tokens = pltpu.VMEM((n, rows, wide), jnp.bfloat16)
    state = pltpu.VMEM((m, width, HEAD, HEAD), jnp.bfloat16)
    return pl.pallas_call(
        functools.partial(attend_body, n, spans, order),
        in_specs=[pl.BlockSpec(memory_space=pltpu.SMEM)] * 2
        + [pl.BlockSpec(memory_space=pltpu.HBM)] * 3
        + [pl.BlockSpec(memory_space=pl.ANY)] * (1 + 2 * len(states)),
        out_specs=[pl.BlockSpec(memory_space=pltpu.HBM)] * n,
        out_shape=[jax.ShapeDtypeStruct((rows, wide), jnp.bfloat16)] * n,
        scratch_shapes=[
            tokens,
            tokens,
            tokens,
            state,
            state,
            pltpu.VMEM((1, HEADS * HEAD), jnp.float32),
            tokens,
            pltpu.SemaphoreType.DMA((4, n)),
            pltpu.SemaphoreType.DMA((1 + 2 * len(states),)),
        ],
        compiler_params=params(8 * n * rows * wide + 2 * n * width * HEAD * HEAD + 4 * HEADS * HEAD),
        cost_estimate=pl.CostEstimate(
            flops=2 * n * width * rows * HEAD * (2 * rows + HEAD),
            bytes_accessed=8 * rows * n * wide,
            transcendentals=n * width * rows,
        ),
        name="attend",
    )(place, jnp.full((1,), low, jnp.int32), queries, keys, values, gain, *(array for pair in states for array in pair))


def put_body(n, order, place, low, *refs):
    parts, out, again, sems = refs[:n], refs[-3], refs[-2], refs[-1]
    m = n // 2
    rows, wide = parts[0].shape
    cols = pl.ds(pl.multiple_of(low[0] * HEAD, HEAD), wide)
    copies = []
    for index, shift in enumerate(order):
        row = lax.rem(place[0] + m - shift // 2, m)
        col = place[1] if shift % 2 == 0 else 1 - place[1]
        start = pl.multiple_of((2 * row + col) * rows, rows)
        copies.append(
            pltpu.make_async_copy(parts[index], out.at[pl.ds(start, rows), cols], sems.at[index])
        )
    for copy in copies:
        copy.start()
    for index in range(2):
        again[index] = place[index]
    for copy in copies:
        copy.wait()


def put(place, parts, out, order, n, low):
    rows, first = parts[0].shape[0], out is None
    anywhere = pl.BlockSpec(memory_space=pltpu.HBM)
    return pl.pallas_call(
        functools.partial(put_body, n, order),
        in_specs=[pl.BlockSpec(memory_space=pltpu.SMEM)] * 2 + [anywhere] * (n if first else n + 1),
        out_specs=[anywhere, pl.BlockSpec(memory_space=pltpu.SMEM)],
        out_shape=[
            jax.ShapeDtypeStruct((n * rows, HEADS // n * HEAD), jnp.bfloat16),
            jax.ShapeDtypeStruct((2,), jnp.int32),
        ],
        scratch_shapes=[pltpu.SemaphoreType.DMA((n,))],
        input_output_aliases={} if first else {n + 2: 0},
        compiler_params=params(),
        name="put",
    )(place, jnp.full((1,), low, jnp.int32), *parts, *(() if first else (out,)))


def split(widths, per_dest):
    chunks, low = [], 0
    for width in widths:
        if low < per_dest:
            width = min(width, per_dest - low)
            chunks.append((low, width))
            low += width
    return chunks


def inside(chunks, low, width):
    return [c for c, (start, _) in enumerate(chunks) if low <= start < low + width]


class Plan:
    def __init__(self, n, queries, keys, values, gain):
        self.n, self.m = n, n // 2
        me = lax.axis_index("seq")
        self.col = me % 2
        self.place = jnp.stack([me // 2, self.col]).astype(jnp.int32)
        self.arrays = tuple(pltpu.with_memory_space_constraint(x, pltpu.HBM) for x in (queries, keys, values))
        self.gain = gain.reshape(1, HEADS * HEAD)
        self.groups, self.swaps, self.parts, self.chunks = (
            split(widths, HEADS // n) for widths in (LOCAL, SWAP, PREFIX, MIXED)
        )
        self.shifts = sorted(range(1, n), key=lambda k: (-min(k // 2, self.m - k // 2), k))
        self.made = {}

    def has(self, key):
        limit = {"message": self.m, "prefix": self.m, "sent": self.n - 1}.get(key[0], 0)
        chunks = {"group": self.groups, "swap": self.swaps, "mixed": self.chunks, "sent": self.chunks}
        chunks = chunks.get(key[0], self.parts)
        return key[1] < len(chunks) and (len(key) < 3 or key[2] <= limit)

    def get(self, *key):
        if key not in self.made:
            self.made[key] = getattr(self, key[0])(*key[1:])
        return self.made[key]

    def hold(self, value, *key):
        others = []
        for other in ORDER.get(key, ()):
            if self.has(other):
                result = self.get(*other)
                while isinstance(result, (list, tuple)):
                    result = result[-1]
                others.append(result)
        return lax.optimization_barrier((value, *others))[0] if others else value

    def group(self, g):
        low, width = self.groups[g]
        widths = tuple(self.parts[c][1] for c in inside(self.parts, low, width))
        swaps = tuple(self.swaps[c][1] for c in inside(self.swaps, low, width))
        _, keys, values = self.arrays
        place = self.hold(self.place, "group", g)
        arrays = local_states(place, keys, values, self.n, low, widths, swaps)
        return arrays[: len(widths)], arrays[len(widths) :]

    def around(self, chunks, low):
        return next(c for c, (start, width) in enumerate(chunks) if start <= low < start + width)

    def swap(self, w):
        g = self.around(self.groups, self.swaps[w][0])
        spot = inside(self.swaps, *self.groups[g]).index(w)
        other = self.hold(self.get("group", g)[1][spot], "swap", w)
        return lax.ppermute(other, "seq", [(d, d ^ 1) for d in range(self.n)])

    def local(self, c):
        low, width = self.parts[c]
        g, w = self.around(self.groups, low), self.around(self.swaps, low)
        near = self.get("swap", w)[:, low - self.swaps[w][0] :][:, :width].astype(jnp.float32)
        return self.get("group", g)[0][inside(self.parts, *self.groups[g]).index(c)], near

    def total(self, c):
        parts = [self.get("prefix", c, s) for s in range(1, self.m)]
        return sum(parts[1:], parts[0]).astype(jnp.float32)

    def message(self, c, s):
        own, near = self.get("local", c)
        if s == self.m:
            value = self.get("total", c) + jnp.where(self.col == 0, own, 0.0)
        else:
            value = own + near
            if s > 1:
                value = self.get("prefix", c, s - 1).astype(jnp.float32) + value
        return self.hold(value.astype(jnp.bfloat16), "message", c, s)

    def prefix(self, c, s):
        if s == self.m:
            pairs = [(d, d ^ 1) for d in range(self.n)]
        else:
            pairs = [(2 * (s - 1) + y, 2 * s + y) for y in range(2)]
        return lax.ppermute(self.get("message", c, s), "seq", pairs)

    def states(self, c):
        _, near = self.get("local", c)
        own = (self.get("total", c) + jnp.where(self.col == 1, near, 0.0)).astype(jnp.bfloat16)
        return own, self.get("prefix", c, self.m)

    def mixed(self, c):
        low, width = self.chunks[c]
        place = self.get("put", c - 3)[1] if c > 2 else self.place
        place = self.hold(place, "mixed", c)
        states, spans = [], []
        for part, (start, size) in enumerate(self.parts):
            first, last = max(low, start), min(low + width, start + size)
            if first < last:
                states.append(self.get("states", part))
                spans.append((first - start, last - first))
        return attend(place, *self.arrays, self.gain, states, tuple(spans), (0, *self.shifts), self.n, low)

    def sent(self, c, k):
        shift = self.shifts[k - 1]
        pairs = [
            (2 * z + y, 2 * ((z + shift // 2) % self.m) + (y + shift) % 2) for z in range(self.m) for y in range(2)
        ]
        return lax.ppermute(self.hold(self.get("mixed", c)[k], "sent", c, k), "seq", pairs)

    def put(self, c):
        parts = [self.get("mixed", c)[0]] + [self.get("sent", c, k) for k in range(1, self.n)]
        out = self.get("put", c - 1)[0] if c else None
        return put(self.place, parts, out, (0, *self.shifts), self.n, self.chunks[c][0])


def per_device(n, *arrays):
    plan = Plan(n, *arrays)
    return plan.get("put", len(plan.chunks) - 1)[0]


def solution(mesh):
    tokens = P(("batch", "seq"), None)
    return jax.shard_map(
        functools.partial(per_device, mesh.shape["seq"]),
        mesh=mesh,
        in_specs=(tokens, tokens, tokens, P()),
        out_specs=P("batch", "seq"),
        check_vma=False,
    )
```

```python
import functools

import jax
import jax.numpy as jnp
from jax import lax
from jax.experimental import pallas as pl
from jax.experimental.pallas import tpu as pltpu
from jax.sharding import PartitionSpec as P

HEADS = 64
HEAD = 128
LOCAL = (2, 6)
SWAP = (2, 3, 3)
PREFIX = (2, 3, 3)
MIXED = (2, 3, 3)
TILE = 256
SPARE = 8 * 1024 * 1024
ORDER = {
    ("message", 0, 1): [("group", 1)],
    ("message", 1, 1): [("message", 0, 2)],
    ("message", 1, 2): [("message", 0, 3)],
    ("message", 1, 3): [("message", 0, 4)],
    ("message", 2, 1): [("message", 1, 2)],
    ("message", 2, 2): [("message", 1, 3)],
    ("message", 2, 3): [("message", 1, 4), ("mixed", 0)],
    ("mixed", 0): [("message", 1, 3), ("message", 2, 2)],
    ("message", 1, 4): [("mixed", 0)],
}


def params(buffers=0):
    return pltpu.CompilerParams(vmem_limit_bytes=buffers + SPARE)


def column(place, row, side, n):
    col = place[1] if side == 0 else 1 - place[1]
    return pl.multiple_of(((2 * row + col) * (HEADS // n) + place[2]) * HEAD, HEAD)


def rows_together(m, width, most):
    return max(count for count in range(1, m + 1) if m % count == 0 and (count == 1 or 2 * width * count <= most))


def local_body(n, widths, swaps, place, low, keys, values, *refs):
    outs, (kbuf, vbuf, sems) = refs[:-3], refs[-3:]
    total = sum(widths)
    here = place[0], place[1], low[0]
    together = rows_together(n // 2, total, 16)

    def copies(row, side):
        cols = pl.ds(column(here, row, side, n), total * HEAD)
        slot = 2 * row + side
        return [
            pltpu.make_async_copy(source.at[:, cols], buf.at[slot], sems.at[which, slot])
            for which, (source, buf) in enumerate(((keys, kbuf), (values, vbuf)))
        ]

    def fetch(row, carry):
        for side in range(2):
            for copy in copies(row, side):
                copy.start()
        return carry

    def work(step, carry):
        slots = [(step * together + index, side) for index in range(together) for side in range(2)]
        for row, side in slots:
            for copy in copies(row, side):
                copy.wait()
        places = [
            [(out, head) for out, width in zip(arrays, sizes) for head in range(width)]
            for arrays, sizes in ((outs[: len(widths)], widths), (outs[len(widths) :], swaps))
        ]
        for row, side in slots:
            for first in range(0, total, 2):
                size = min(2, total - first)
                cols = slice(first * HEAD, (first + size) * HEAD)
                both = lax.dot_general(
                    kbuf[2 * row + side, :, cols],
                    vbuf[2 * row + side, :, cols],
                    (((0,), (0,)), ((), ())),
                    preferred_element_type=jnp.float32,
                )
                for index in range(first, first + size):
                    part = slice((index - first) * HEAD, (index - first + 1) * HEAD)
                    out, head = places[side][index]
                    out[row, head] = both[part, part].astype(out.dtype)
        return carry

    lax.fori_loop(0, n // 2, fetch, 0)
    lax.fori_loop(0, n // 2 // together, work, 0)


def local_states(place, keys, values, n, low, widths, swaps):
    rows, m, total = keys.shape[0], n // 2, sum(widths)
    buf = pltpu.VMEM((n, rows, total * HEAD), keys.dtype)
    shapes = [jax.ShapeDtypeStruct((m, width, HEAD, HEAD), jnp.float32) for width in widths]
    shapes += [jax.ShapeDtypeStruct((m, width, HEAD, HEAD), jnp.bfloat16) for width in swaps]
    return pl.pallas_call(
        functools.partial(local_body, n, widths, swaps),
        in_specs=[pl.BlockSpec(memory_space=pltpu.SMEM)] * 2 + [pl.BlockSpec(memory_space=pltpu.HBM)] * 2,
        out_specs=[pl.BlockSpec(memory_space=pltpu.VMEM)] * len(shapes),
        out_shape=shapes,
        scratch_shapes=[buf, buf, pltpu.SemaphoreType.DMA((2, n))],
        compiler_params=params(4 * n * rows * total * HEAD + 3 * n * total * HEAD * HEAD),
        cost_estimate=pl.CostEstimate(
            flops=2 * n * total * rows * HEAD * HEAD, bytes_accessed=4 * rows * n * total * HEAD, transcendentals=0
        ),
        name="local",
    )(place, jnp.full((1,), low, jnp.int32), keys, values)


def masked_scores(query, key):
    rows = query.shape[0]
    tiles = []
    for low in range(0, rows, TILE):
        high = min(low + TILE, rows)
        part = lax.dot_general(
            query[low:], key[low:high], (((1,), (1,)), ((), ())), preferred_element_type=jnp.float32
        )
        size = high - low
        spot = lax.broadcasted_iota(jnp.int32, (size, size), 0)
        other = lax.broadcasted_iota(jnp.int32, (size, size), 1)
        pieces = [jnp.where(other <= spot, part[:size], 0.0).astype(jnp.bfloat16)]
        if low:
            pieces.insert(0, jnp.zeros((low, size), jnp.bfloat16))
        if high < rows:
            pieces.append(part[size:].astype(jnp.bfloat16))
        tiles.append(jnp.concatenate(pieces, axis=0) if len(pieces) > 1 else pieces[0])
    return tiles


def attend_body(n, spans, order, place, low, queries, keys, values, gain, *refs):
    states, outs = refs[: 2 * len(spans)], refs[2 * len(spans) :][:n]
    qbuf, kbuf, vbuf, sown, soth, gbuf, held, sems, extra = refs[-9:]
    width = sum(size for _, size in spans)
    m, wide = n // 2, width * HEAD
    together = rows_together(m, width, 12)
    here = place[0], place[1], low[0]
    small, start = [(gain, gbuf)], 0
    for chunk, (skip, size) in enumerate(spans):
        for source, buf in ((states[2 * chunk], sown), (states[2 * chunk + 1], soth)):
            small.append((source.at[:, skip : skip + size], buf.at[:, start : start + size]))
        start += size
    small = [pltpu.make_async_copy(source, buf, extra.at[which]) for which, (source, buf) in enumerate(small)]

    def copies(step, side):
        cols = pl.ds(column(here, lax.rem(here[0] + step, m), side, n), wide)
        slot = 2 * step + side
        return [
            pltpu.make_async_copy(source.at[:, cols], buf.at[slot, :, :wide], sems.at[which, slot])
            for which, (source, buf) in enumerate(((queries, qbuf), (keys, kbuf), (values, vbuf)))
        ]

    def sends(step):
        return [
            pltpu.make_async_copy(held.at[slot, :, :wide], outs[order.index(slot)], sems.at[3, slot])
            for slot in (2 * step, 2 * step + 1)
        ]

    def fetch(step, carry):
        for side in range(2):
            for copy in copies(step, side):
                copy.start()
        return carry

    def work(group, carry):
        steps = [group * together + index for index in range(together)]
        for step in steps:
            for side in range(2):
                for copy in copies(step, side):
                    copy.wait()
        heads = [
            (step, side, head, slice(head * HEAD, (head + 1) * HEAD))
            for step in steps
            for side in range(2)
            for head in range(width)
        ]
        scores = [
            masked_scores(qbuf[2 * step + side, :, cols], kbuf[2 * step + side, :, cols])
            for step, side, _, cols in heads
        ]
        attended = []
        for (step, side, head, cols), tiles in zip(heads, scores):
            slot = 2 * step + side
            state = (sown if side == 0 else soth)[lax.rem(here[0] + step, m), head]
            left = jnp.concatenate([*tiles, qbuf[slot, :, cols]], axis=1)
            right = jnp.concatenate([vbuf[slot, :, cols], state], axis=0)
            attended.append(jnp.dot(left, right, preferred_element_type=jnp.float32))
        for (step, side, head, cols), value in zip(heads, attended):
            square = jnp.mean(value * value, axis=-1, keepdims=True)
            begin = pl.multiple_of(column(here, lax.rem(here[0] + step, m), side, n) + head * HEAD, HEAD)
            mixed = value * lax.rsqrt(square + 1e-05) * gbuf[:, pl.ds(begin, HEAD)]
            held[2 * step + side, :, cols] = mixed.astype(held.dtype)
        for fixed in range(m // together):

            @pl.when(group == fixed)
            def _(fixed=fixed):
                for index in range(together):
                    for copy in sends(fixed * together + index):
                        copy.start()

        return carry

    lax.fori_loop(0, 1, fetch, 0)
    for copy in small:
        copy.start()
    lax.fori_loop(1, m, fetch, 0)
    for copy in small:
        copy.wait()
    lax.fori_loop(0, m // together, work, 0)
    for step in range(m):
        for copy in sends(step):
            copy.wait()


def attend(place, queries, keys, values, gain, states, spans, order, n, low):
    rows, m = queries.shape[0], n // 2
    width = sum(size for _, size in spans)
    wide = width * HEAD
    tokens = pltpu.VMEM((n, rows, (width + 1 - width % 2) * HEAD), jnp.bfloat16)
    state = pltpu.VMEM((m, width, HEAD, HEAD), jnp.bfloat16)
    return pl.pallas_call(
        functools.partial(attend_body, n, spans, order),
        in_specs=[pl.BlockSpec(memory_space=pltpu.SMEM)] * 2
        + [pl.BlockSpec(memory_space=pltpu.HBM)] * 3
        + [pl.BlockSpec(memory_space=pl.ANY)] * (1 + 2 * len(states)),
        out_specs=[pl.BlockSpec(memory_space=pltpu.HBM)] * n,
        out_shape=[jax.ShapeDtypeStruct((rows, wide), jnp.bfloat16)] * n,
        scratch_shapes=[
            tokens,
            tokens,
            tokens,
            state,
            state,
            pltpu.VMEM((1, HEADS * HEAD), jnp.float32),
            tokens,
            pltpu.SemaphoreType.DMA((4, n)),
            pltpu.SemaphoreType.DMA((1 + 2 * len(states),)),
        ],
        compiler_params=params(8 * n * rows * (wide + HEAD) + 2 * n * width * HEAD * HEAD + 4 * HEADS * HEAD),
        cost_estimate=pl.CostEstimate(
            flops=2 * n * width * rows * HEAD * (2 * rows + HEAD),
            bytes_accessed=8 * rows * n * wide,
            transcendentals=n * width * rows,
        ),
        name="attend",
    )(place, jnp.full((1,), low, jnp.int32), queries, keys, values, gain, *(array for pair in states for array in pair))


def put_body(n, order, place, low, *refs):
    parts, out, again, sems = refs[:n], refs[-3], refs[-2], refs[-1]
    m = n // 2
    rows, wide = parts[0].shape
    cols = pl.ds(pl.multiple_of(low[0] * HEAD, HEAD), wide)
    copies = []
    for index, shift in enumerate(order):
        row = lax.rem(place[0] + m - shift // 2, m)
        col = place[1] if shift % 2 == 0 else 1 - place[1]
        start = pl.multiple_of((2 * row + col) * rows, rows)
        copies.append(
            pltpu.make_async_copy(parts[index], out.at[pl.ds(start, rows), cols], sems.at[index])
        )
    for copy in copies:
        copy.start()
    for index in range(2):
        again[index] = place[index]
    for copy in copies:
        copy.wait()


def put(place, parts, out, order, n, low):
    rows, first = parts[0].shape[0], out is None
    anywhere = pl.BlockSpec(memory_space=pltpu.HBM)
    return pl.pallas_call(
        functools.partial(put_body, n, order),
        in_specs=[pl.BlockSpec(memory_space=pltpu.SMEM)] * 2 + [anywhere] * (n if first else n + 1),
        out_specs=[anywhere, pl.BlockSpec(memory_space=pltpu.SMEM)],
        out_shape=[
            jax.ShapeDtypeStruct((n * rows, HEADS // n * HEAD), jnp.bfloat16),
            jax.ShapeDtypeStruct((2,), jnp.int32),
        ],
        scratch_shapes=[pltpu.SemaphoreType.DMA((n,))],
        input_output_aliases={} if first else {n + 2: 0},
        compiler_params=params(),
        name="put",
    )(place, jnp.full((1,), low, jnp.int32), *parts, *(() if first else (out,)))


def split(widths, per_dest):
    chunks, low = [], 0
    for width in widths:
        if low < per_dest:
            width = min(width, per_dest - low)
            chunks.append((low, width))
            low += width
    return chunks


def inside(chunks, low, width):
    return [c for c, (start, _) in enumerate(chunks) if low <= start < low + width]


class Plan:
    def __init__(self, n, queries, keys, values, gain):
        self.n, self.m = n, n // 2
        me = lax.axis_index("seq")
        self.col = me % 2
        self.place = jnp.stack([me // 2, self.col]).astype(jnp.int32)
        self.arrays = tuple(pltpu.with_memory_space_constraint(x, pltpu.HBM) for x in (queries, keys, values))
        self.gain = gain.reshape(1, HEADS * HEAD)
        self.groups, self.swaps, self.parts, self.chunks = (
            split(widths, HEADS // n) for widths in (LOCAL, SWAP, PREFIX, MIXED)
        )
        self.shifts = sorted(range(1, n), key=lambda k: (-min(k // 2, self.m - k // 2), k))
        self.made = {}

    def has(self, key):
        limit = {"message": self.m, "prefix": self.m, "sent": self.n - 1}.get(key[0], 0)
        chunks = {"group": self.groups, "swap": self.swaps, "mixed": self.chunks, "sent": self.chunks}
        chunks = chunks.get(key[0], self.parts)
        return key[1] < len(chunks) and (len(key) < 3 or key[2] <= limit)

    def get(self, *key):
        if key not in self.made:
            self.made[key] = getattr(self, key[0])(*key[1:])
        return self.made[key]

    def hold(self, value, *key):
        others = []
        for other in ORDER.get(key, ()):
            if self.has(other):
                result = self.get(*other)
                while isinstance(result, (list, tuple)):
                    result = result[-1]
                others.append(result)
        return lax.optimization_barrier((value, *others))[0] if others else value

    def group(self, g):
        low, width = self.groups[g]
        widths = tuple(self.parts[c][1] for c in inside(self.parts, low, width))
        swaps = tuple(self.swaps[c][1] for c in inside(self.swaps, low, width))
        _, keys, values = self.arrays
        place = self.hold(self.place, "group", g)
        arrays = local_states(place, keys, values, self.n, low, widths, swaps)
        return arrays[: len(widths)], arrays[len(widths) :]

    def around(self, chunks, low):
        return next(c for c, (start, width) in enumerate(chunks) if start <= low < start + width)

    def swap(self, w):
        g = self.around(self.groups, self.swaps[w][0])
        spot = inside(self.swaps, *self.groups[g]).index(w)
        other = self.hold(self.get("group", g)[1][spot], "swap", w)
        return lax.ppermute(other, "seq", [(d, d ^ 1) for d in range(self.n)])

    def local(self, c):
        low, width = self.parts[c]
        g, w = self.around(self.groups, low), self.around(self.swaps, low)
        near = self.get("swap", w)[:, low - self.swaps[w][0] :][:, :width].astype(jnp.float32)
        return self.get("group", g)[0][inside(self.parts, *self.groups[g]).index(c)], near

    def total(self, c):
        parts = [self.get("prefix", c, s) for s in range(1, self.m)]
        return sum(parts[1:], parts[0]).astype(jnp.float32)

    def message(self, c, s):
        own, near = self.get("local", c)
        if s == self.m:
            value = self.get("total", c) + jnp.where(self.col == 0, own, 0.0)
        else:
            value = own + near
            if s > 1:
                value = self.get("prefix", c, s - 1).astype(jnp.float32) + value
        return self.hold(value.astype(jnp.bfloat16), "message", c, s)

    def prefix(self, c, s):
        if s == self.m:
            pairs = [(d, d ^ 1) for d in range(self.n)]
        else:
            pairs = [(2 * (s - 1) + y, 2 * s + y) for y in range(2)]
        return lax.ppermute(self.get("message", c, s), "seq", pairs)

    def states(self, c):
        _, near = self.get("local", c)
        own = (self.get("total", c) + jnp.where(self.col == 1, near, 0.0)).astype(jnp.bfloat16)
        return own, self.get("prefix", c, self.m)

    def mixed(self, c):
        low, width = self.chunks[c]
        place = self.get("put", c - 3)[1] if c > 2 else self.place
        place = self.hold(place, "mixed", c)
        states, spans = [], []
        for part, (start, size) in enumerate(self.parts):
            first, last = max(low, start), min(low + width, start + size)
            if first < last:
                states.append(self.get("states", part))
                spans.append((first - start, last - first))
        return attend(place, *self.arrays, self.gain, states, tuple(spans), (0, *self.shifts), self.n, low)

    def sent(self, c, k):
        shift = self.shifts[k - 1]
        pairs = [
            (2 * z + y, 2 * ((z + shift // 2) % self.m) + (y + shift) % 2) for z in range(self.m) for y in range(2)
        ]
        return lax.ppermute(self.hold(self.get("mixed", c)[k], "sent", c, k), "seq", pairs)

    def put(self, c):
        parts = [self.get("mixed", c)[0]] + [self.get("sent", c, k) for k in range(1, self.n)]
        out = self.get("put", c - 1)[0] if c else None
        return put(self.place, parts, out, (0, *self.shifts), self.n, self.chunks[c][0])


def per_device(n, *arrays):
    plan = Plan(n, *arrays)
    return plan.get("put", len(plan.chunks) - 1)[0]


def solution(mesh):
    tokens = P(("batch", "seq"), None)
    return jax.shard_map(
        functools.partial(per_device, mesh.shape["seq"]),
        mesh=mesh,
        in_specs=(tokens, tokens, tokens, P()),
        out_specs=P("batch", "seq"),
        check_vma=False,
    )
```

```python
import functools

import jax
import jax.numpy as jnp
from jax import lax
from jax.experimental import pallas as pl
from jax.experimental.pallas import tpu as pltpu
from jax.sharding import PartitionSpec as P

HEADS = 64
HEAD = 128
LOCAL = (2, 6)
SWAP = (2, 3, 3)
PREFIX = (2, 3, 3)
MIXED = (2, 3, 3)
TILE = 256
SPARE = 8 * 1024 * 1024
ORDER = {
    ("message", 0, 1): [("group", 1)],
    ("message", 1, 1): [("message", 0, 2)],
    ("message", 1, 2): [("message", 0, 3)],
    ("message", 1, 3): [("message", 0, 4)],
    ("message", 2, 1): [("message", 1, 2)],
    ("message", 2, 2): [("message", 1, 3)],
    ("message", 2, 3): [("message", 1, 4), ("mixed", 0)],
    ("mixed", 0): [("message", 1, 3), ("message", 2, 2)],
    ("message", 1, 4): [("mixed", 0)],
}


def params(buffers=0):
    return pltpu.CompilerParams(vmem_limit_bytes=buffers + SPARE)


def column(place, row, side, n):
    col = place[1] if side == 0 else 1 - place[1]
    return pl.multiple_of(((2 * row + col) * (HEADS // n) + place[2]) * HEAD, HEAD)


def odd(tiles):
    return tiles + 1 - tiles % 2


def rows_together(m, width, most):
    return max(count for count in range(1, m + 1) if m % count == 0 and (count == 1 or 2 * width * count <= most))


def local_body(n, widths, swaps, place, low, keys, values, *refs):
    outs, (kbuf, vbuf, sems) = refs[:-3], refs[-3:]
    total = sum(widths)
    here = place[0], place[1], low[0]
    together = rows_together(n // 2, total, 16)

    def copies(row, side):
        cols = pl.ds(column(here, row, side, n), total * HEAD)
        slot = 2 * row + side
        return [
            pltpu.make_async_copy(source.at[:, cols], buf.at[slot, :, : total * HEAD], sems.at[which, slot])
            for which, (source, buf) in enumerate(((keys, kbuf), (values, vbuf)))
        ]

    def fetch(row, carry):
        for side in range(2):
            for copy in copies(row, side):
                copy.start()
        return carry

    def work(step, carry):
        slots = [(step * together + index, side) for index in range(together) for side in range(2)]
        for row, side in slots:
            for copy in copies(row, side):
                copy.wait()
        places = [
            [(out, head) for out, width in zip(arrays, sizes) for head in range(width)]
            for arrays, sizes in ((outs[: len(widths)], widths), (outs[len(widths) :], swaps))
        ]
        for row, side in slots:
            for first in range(0, total, 2):
                size = min(2, total - first)
                cols = slice(first * HEAD, (first + size) * HEAD)
                both = lax.dot_general(
                    kbuf[2 * row + side, :, cols],
                    vbuf[2 * row + side, :, cols],
                    (((0,), (0,)), ((), ())),
                    preferred_element_type=jnp.float32,
                )
                for index in range(first, first + size):
                    part = slice((index - first) * HEAD, (index - first + 1) * HEAD)
                    out, head = places[side][index]
                    out[row, head] = both[part, part].astype(out.dtype)
        return carry

    lax.fori_loop(0, n // 2, fetch, 0)
    lax.fori_loop(0, n // 2 // together, work, 0)


def local_states(place, keys, values, n, low, widths, swaps):
    rows, m, total = keys.shape[0], n // 2, sum(widths)
    buf = pltpu.VMEM((n, rows, odd(total) * HEAD), keys.dtype)
    shapes = [jax.ShapeDtypeStruct((m, width, HEAD, HEAD), jnp.float32) for width in widths]
    shapes += [jax.ShapeDtypeStruct((m, width, HEAD, HEAD), jnp.bfloat16) for width in swaps]
    return pl.pallas_call(
        functools.partial(local_body, n, widths, swaps),
        in_specs=[pl.BlockSpec(memory_space=pltpu.SMEM)] * 2 + [pl.BlockSpec(memory_space=pltpu.HBM)] * 2,
        out_specs=[pl.BlockSpec(memory_space=pltpu.VMEM)] * len(shapes),
        out_shape=shapes,
        scratch_shapes=[buf, buf, pltpu.SemaphoreType.DMA((2, n))],
        compiler_params=params(4 * n * rows * odd(total) * HEAD + 3 * n * total * HEAD * HEAD),
        cost_estimate=pl.CostEstimate(
            flops=2 * n * total * rows * HEAD * HEAD, bytes_accessed=4 * rows * n * total * HEAD, transcendentals=0
        ),
        name="local",
    )(place, jnp.full((1,), low, jnp.int32), keys, values)


def masked_scores(query, key):
    rows = query.shape[0]
    tiles = []
    for low in range(0, rows, TILE):
        high = min(low + TILE, rows)
        part = lax.dot_general(
            query[low:], key[low:high], (((1,), (1,)), ((), ())), preferred_element_type=jnp.float32
        )
        size = high - low
        spot = lax.broadcasted_iota(jnp.int32, (size, size), 0)
        other = lax.broadcasted_iota(jnp.int32, (size, size), 1)
        pieces = [jnp.where(other <= spot, part[:size], 0.0).astype(jnp.bfloat16)]
        if low:
            pieces.insert(0, jnp.zeros((low, size), jnp.bfloat16))
        if high < rows:
            pieces.append(part[size:].astype(jnp.bfloat16))
        tiles.append(jnp.concatenate(pieces, axis=0) if len(pieces) > 1 else pieces[0])
    return tiles


def attend_body(n, spans, order, place, low, queries, keys, values, gain, *refs):
    states, outs = refs[: 2 * len(spans)], refs[2 * len(spans) :][:n]
    qbuf, kbuf, vbuf, sown, soth, gbuf, held, sems, extra = refs[-9:]
    width = sum(size for _, size in spans)
    m, wide = n // 2, width * HEAD
    together = rows_together(m, width, 12)
    here = place[0], place[1], low[0]
    small, start = [(gain, gbuf)], 0
    for chunk, (skip, size) in enumerate(spans):
        for source, buf in ((states[2 * chunk], sown), (states[2 * chunk + 1], soth)):
            small.append((source.at[:, skip : skip + size], buf.at[:, start : start + size]))
        start += size
    small = [pltpu.make_async_copy(source, buf, extra.at[which]) for which, (source, buf) in enumerate(small)]

    def copies(step, side):
        cols = pl.ds(column(here, lax.rem(here[0] + step, m), side, n), wide)
        slot = 2 * step + side
        return [
            pltpu.make_async_copy(source.at[:, cols], buf.at[slot, :, :wide], sems.at[which, slot])
            for which, (source, buf) in enumerate(((queries, qbuf), (keys, kbuf), (values, vbuf)))
        ]

    def sends(step):
        return [
            pltpu.make_async_copy(held.at[slot, :, :wide], outs[order.index(slot)], sems.at[3, slot])
            for slot in (2 * step, 2 * step + 1)
        ]

    def fetch(step, carry):
        for side in range(2):
            for copy in copies(step, side):
                copy.start()
        return carry

    def work(group, carry):
        steps = [group * together + index for index in range(together)]
        for step in steps:
            for side in range(2):
                for copy in copies(step, side):
                    copy.wait()
        heads = [
            (step, side, head, slice(head * HEAD, (head + 1) * HEAD))
            for step in steps
            for side in range(2)
            for head in range(width)
        ]
        scores = [
            masked_scores(qbuf[2 * step + side, :, cols], kbuf[2 * step + side, :, cols])
            for step, side, _, cols in heads
        ]
        attended = []
        for (step, side, head, cols), tiles in zip(heads, scores):
            slot = 2 * step + side
            state = (sown if side == 0 else soth)[lax.rem(here[0] + step, m), head]
            left = jnp.concatenate([*tiles, qbuf[slot, :, cols]], axis=1)
            right = jnp.concatenate([vbuf[slot, :, cols], state], axis=0)
            attended.append(jnp.dot(left, right, preferred_element_type=jnp.float32))
        for (step, side, head, cols), value in zip(heads, attended):
            square = jnp.mean(value * value, axis=-1, keepdims=True)
            begin = pl.multiple_of(column(here, lax.rem(here[0] + step, m), side, n) + head * HEAD, HEAD)
            mixed = value * lax.rsqrt(square + 1e-05) * gbuf[:, pl.ds(begin, HEAD)]
            held[2 * step + side, :, cols] = mixed.astype(held.dtype)
        for fixed in range(m // together):

            @pl.when(group == fixed)
            def _(fixed=fixed):
                for index in range(together):
                    for copy in sends(fixed * together + index):
                        copy.start()

        return carry

    lax.fori_loop(0, 1, fetch, 0)
    for copy in small:
        copy.start()
    lax.fori_loop(1, m, fetch, 0)
    for copy in small:
        copy.wait()
    lax.fori_loop(0, m // together, work, 0)
    for step in range(m):
        for copy in sends(step):
            copy.wait()


def attend(place, queries, keys, values, gain, states, spans, order, n, low):
    rows, m = queries.shape[0], n // 2
    width = sum(size for _, size in spans)
    wide = width * HEAD
    tokens = pltpu.VMEM((n, rows, odd(width) * HEAD), jnp.bfloat16)
    state = pltpu.VMEM((m, width, HEAD, HEAD), jnp.bfloat16)
    return pl.pallas_call(
        functools.partial(attend_body, n, spans, order),
        in_specs=[pl.BlockSpec(memory_space=pltpu.SMEM)] * 2
        + [pl.BlockSpec(memory_space=pltpu.HBM)] * 3
        + [pl.BlockSpec(memory_space=pl.ANY)] * (1 + 2 * len(states)),
        out_specs=[pl.BlockSpec(memory_space=pltpu.HBM)] * n,
        out_shape=[jax.ShapeDtypeStruct((rows, wide), jnp.bfloat16)] * n,
        scratch_shapes=[
            tokens,
            tokens,
            tokens,
            state,
            state,
            pltpu.VMEM((1, HEADS * HEAD), jnp.float32),
            tokens,
            pltpu.SemaphoreType.DMA((4, n)),
            pltpu.SemaphoreType.DMA((1 + 2 * len(states),)),
        ],
        compiler_params=params(8 * n * rows * odd(width) * HEAD + 2 * n * width * HEAD * HEAD + 4 * HEADS * HEAD),
        cost_estimate=pl.CostEstimate(
            flops=2 * n * width * rows * HEAD * (2 * rows + HEAD),
            bytes_accessed=8 * rows * n * wide,
            transcendentals=n * width * rows,
        ),
        name="attend",
    )(place, jnp.full((1,), low, jnp.int32), queries, keys, values, gain, *(array for pair in states for array in pair))


def put_body(n, order, place, low, *refs):
    parts, out, again, sems = refs[: len(order)], refs[-3], refs[-2], refs[-1]
    m = n // 2
    rows, wide = parts[0].shape
    cols = pl.ds(pl.multiple_of(low[0] * HEAD, HEAD), wide)
    copies = []
    for index, shift in enumerate(order):
        row = lax.rem(place[0] + m - shift // 2, m)
        col = place[1] if shift % 2 == 0 else 1 - place[1]
        start = pl.multiple_of((2 * row + col) * rows, rows)
        copies.append(
            pltpu.make_async_copy(parts[index], out.at[pl.ds(start, rows), cols], sems.at[index])
        )
    for copy in copies:
        copy.start()
    for index in range(2):
        again[index] = place[index]
    for copy in copies:
        copy.wait()


def put(place, parts, out, order, n, low):
    rows, first = parts[0].shape[0], out is None
    anywhere = pl.BlockSpec(memory_space=pltpu.HBM)
    return pl.pallas_call(
        functools.partial(put_body, n, order),
        in_specs=[pl.BlockSpec(memory_space=pltpu.SMEM)] * 2 + [anywhere] * (len(parts) + (not first)),
        out_specs=[anywhere, pl.BlockSpec(memory_space=pltpu.SMEM)],
        out_shape=[
            jax.ShapeDtypeStruct((n * rows, HEADS // n * HEAD), jnp.bfloat16),
            jax.ShapeDtypeStruct((2,), jnp.int32),
        ],
        scratch_shapes=[pltpu.SemaphoreType.DMA((len(parts),))],
        input_output_aliases={} if first else {len(parts) + 2: 0},
        compiler_params=params(),
        name="put",
    )(place, jnp.full((1,), low, jnp.int32), *parts, *(() if first else (out,)))


def split(widths, per_dest):
    chunks, low = [], 0
    for width in widths:
        if low < per_dest:
            width = min(width, per_dest - low)
            chunks.append((low, width))
            low += width
    return chunks


def inside(chunks, low, width):
    return [c for c, (start, _) in enumerate(chunks) if low <= start < low + width]


class Plan:
    def __init__(self, n, queries, keys, values, gain):
        self.n, self.m = n, n // 2
        me = lax.axis_index("seq")
        self.col = me % 2
        self.place = jnp.stack([me // 2, self.col]).astype(jnp.int32)
        self.arrays = tuple(pltpu.with_memory_space_constraint(x, pltpu.HBM) for x in (queries, keys, values))
        self.gain = gain.reshape(1, HEADS * HEAD)
        self.groups, self.swaps, self.parts, self.chunks = (
            split(widths, HEADS // n) for widths in (LOCAL, SWAP, PREFIX, MIXED)
        )
        self.shifts = sorted(range(1, n), key=lambda k: (-min(k // 2, self.m - k // 2), k))
        self.made = {}

    def has(self, key):
        limit = {"message": self.m, "prefix": self.m, "sent": self.n - 1}.get(key[0], 0)
        chunks = {"group": self.groups, "swap": self.swaps, "mixed": self.chunks, "sent": self.chunks}
        chunks = chunks.get(key[0], self.parts)
        return key[1] < len(chunks) and (len(key) < 3 or key[2] <= limit)

    def get(self, *key):
        if key not in self.made:
            self.made[key] = getattr(self, key[0])(*key[1:])
        return self.made[key]

    def hold(self, value, *key):
        others = []
        for other in ORDER.get(key, ()):
            if self.has(other):
                result = self.get(*other)
                while isinstance(result, (list, tuple)):
                    result = result[-1]
                others.append(result)
        return lax.optimization_barrier((value, *others))[0] if others else value

    def group(self, g):
        low, width = self.groups[g]
        widths = tuple(self.parts[c][1] for c in inside(self.parts, low, width))
        swaps = tuple(self.swaps[c][1] for c in inside(self.swaps, low, width))
        _, keys, values = self.arrays
        place = self.hold(self.place, "group", g)
        arrays = local_states(place, keys, values, self.n, low, widths, swaps)
        return arrays[: len(widths)], arrays[len(widths) :]

    def around(self, chunks, low):
        return next(c for c, (start, width) in enumerate(chunks) if start <= low < start + width)

    def swap(self, w):
        g = self.around(self.groups, self.swaps[w][0])
        spot = inside(self.swaps, *self.groups[g]).index(w)
        other = self.hold(self.get("group", g)[1][spot], "swap", w)
        return lax.ppermute(other, "seq", [(d, d ^ 1) for d in range(self.n)])

    def local(self, c):
        low, width = self.parts[c]
        g, w = self.around(self.groups, low), self.around(self.swaps, low)
        near = self.get("swap", w)[:, low - self.swaps[w][0] :][:, :width].astype(jnp.float32)
        return self.get("group", g)[0][inside(self.parts, *self.groups[g]).index(c)], near

    def total(self, c):
        parts = [self.get("prefix", c, s) for s in range(1, self.m)]
        return sum(parts[1:], parts[0]).astype(jnp.float32)

    def message(self, c, s):
        own, near = self.get("local", c)
        if s == self.m:
            value = self.get("total", c) + jnp.where(self.col == 0, own, 0.0)
        else:
            value = own + near
            if s > 1:
                value = self.get("prefix", c, s - 1).astype(jnp.float32) + value
        return self.hold(value.astype(jnp.bfloat16), "message", c, s)

    def prefix(self, c, s):
        if s == self.m:
            pairs = [(d, d ^ 1) for d in range(self.n)]
        else:
            pairs = [(2 * (s - 1) + y, 2 * s + y) for y in range(2)]
        return lax.ppermute(self.get("message", c, s), "seq", pairs)

    def states(self, c):
        _, near = self.get("local", c)
        own = (self.get("total", c) + jnp.where(self.col == 1, near, 0.0)).astype(jnp.bfloat16)
        return own, self.get("prefix", c, self.m)

    def mixed(self, c):
        low, width = self.chunks[c]
        place = self.get("put", c - 3)[1] if c > 2 else self.place
        place = self.hold(place, "mixed", c)
        states, spans = [], []
        for part, (start, size) in enumerate(self.parts):
            first, last = max(low, start), min(low + width, start + size)
            if first < last:
                states.append(self.get("states", part))
                spans.append((first - start, last - first))
        return attend(place, *self.arrays, self.gain, states, tuple(spans), (0, *self.shifts), self.n, low)

    def sent(self, c, k):
        shift = self.shifts[k - 1]
        pairs = [
            (2 * z + y, 2 * ((z + shift // 2) % self.m) + (y + shift) % 2) for z in range(self.m) for y in range(2)
        ]
        return lax.ppermute(self.hold(self.get("mixed", c)[k], "sent", c, k), "seq", pairs)

    def put(self, c):
        parts = [self.get("mixed", c)[0]] + [self.get("sent", c, k) for k in range(1, self.n)]
        out, order, low = self.get("put", c - 1)[0] if c else None, (0, *self.shifts), self.chunks[c][0]
        if c == len(self.chunks) - 1:
            late = self.n // 2 + 1
            out, _ = put(self.place, parts[:late], out, order[:late], self.n, low)
            parts, order = parts[late:], order[late:]
        return put(self.place, parts, out, order, self.n, low)


def per_device(n, *arrays):
    plan = Plan(n, *arrays)
    return plan.get("put", len(plan.chunks) - 1)[0]


def solution(mesh):
    tokens = P(("batch", "seq"), None)
    return jax.shard_map(
        functools.partial(per_device, mesh.shape["seq"]),
        mesh=mesh,
        in_specs=(tokens, tokens, tokens, P()),
        out_specs=P("batch", "seq"),
        check_vma=False,
    )
```

```python
import functools

import jax
import jax.numpy as jnp
from jax import lax
from jax.experimental import pallas as pl
from jax.experimental.pallas import tpu as pltpu
from jax.sharding import PartitionSpec as P

HEADS = 64
HEAD = 128
LOCAL = (2, 6)
SWAP = (2, 3, 3)
PREFIX = (2, 3, 3)
MIXED = (2, 3, 3)
TILE = 256
SPARE = 8 * 1024 * 1024
ORDER = {
    ("message", 0, 1): [("group", 1)],
    ("message", 1, 1): [("message", 0, 2)],
    ("message", 1, 2): [("message", 0, 3)],
    ("message", 1, 3): [("message", 0, 4)],
    ("message", 2, 1): [("message", 1, 2)],
    ("message", 2, 2): [("message", 1, 3)],
    ("message", 2, 3): [("message", 1, 4), ("mixed", 0)],
    ("mixed", 0): [("message", 1, 3), ("message", 2, 2)],
    ("message", 1, 4): [("mixed", 0)],
}


def params(buffers=0):
    return pltpu.CompilerParams(vmem_limit_bytes=buffers + SPARE)


def column(place, row, side, n):
    col = place[1] if side == 0 else 1 - place[1]
    return pl.multiple_of(((2 * row + col) * (HEADS // n) + place[2]) * HEAD, HEAD)


def odd(tiles):
    return tiles + 1 - tiles % 2


def rows_together(m, width, most):
    return max(count for count in range(1, m + 1) if m % count == 0 and (count == 1 or 2 * width * count <= most))


def local_body(n, widths, swaps, ahead, place, low, keys, values, queries, *refs):
    outs, (kbuf, vbuf, sems, early) = refs[:-4], refs[-4:]
    total = sum(widths)
    here = place[0], place[1], low[0]
    together = rows_together(n // 2, total, 8)

    def copies(row, side):
        cols = pl.ds(column(here, row, side, n), total * HEAD)
        slot = 2 * row + side
        return [
            pltpu.make_async_copy(source.at[:, cols], buf.at[slot, :, : total * HEAD], sems.at[which, slot])
            for which, (source, buf) in enumerate(((keys, kbuf), (values, vbuf)))
        ]

    def copies_ahead(row, side):
        wide = ahead[1] * HEAD
        cols = pl.ds(column((place[0], place[1], ahead[0]), row, side, n), wide)
        slot = 2 * row + side
        return [
            pltpu.make_async_copy(source.at[:, cols], out.at[slot, :, :wide], early.at[which, slot])
            for which, (source, out) in enumerate(zip((queries, keys, values), outs[-3:]))
        ]

    def fetch(row, carry):
        for side in range(2):
            for copy in copies(row, side):
                copy.start()
        return carry

    def start_ahead(row, carry):
        for side in range(2):
            for copy in copies_ahead(row, side):
                copy.start()
        return carry

    def wait_ahead(row, carry):
        for side in range(2):
            for copy in copies_ahead(row, side):
                copy.wait()
        return carry

    def work(step, carry):
        slots = [(step * together + index, side) for index in range(together) for side in range(2)]
        for row, side in slots:
            for copy in copies(row, side):
                copy.wait()
        places = [
            [(out, head) for out, width in zip(arrays, sizes) for head in range(width)]
            for arrays, sizes in ((outs[: len(widths)], widths), (outs[len(widths) :][: len(swaps)], swaps))
        ]
        for row, side in slots:
            for first in range(0, total, 2):
                size = min(2, total - first)
                cols = slice(first * HEAD, (first + size) * HEAD)
                both = lax.dot_general(
                    kbuf[2 * row + side, :, cols],
                    vbuf[2 * row + side, :, cols],
                    (((0,), (0,)), ((), ())),
                    preferred_element_type=jnp.float32,
                )
                for index in range(first, first + size):
                    part = slice((index - first) * HEAD, (index - first + 1) * HEAD)
                    out, head = places[side][index]
                    out[row, head] = both[part, part].astype(out.dtype)
        return carry

    lax.fori_loop(0, n // 2, fetch, 0)
    if ahead:
        lax.fori_loop(0, n // 2, start_ahead, 0)
    lax.fori_loop(0, n // 2 // together, work, 0)
    if ahead:
        lax.fori_loop(0, n // 2, wait_ahead, 0)


def local_states(place, queries, keys, values, n, low, widths, swaps, ahead):
    rows, m, total = keys.shape[0], n // 2, sum(widths)
    buf = pltpu.VMEM((n, rows, odd(total) * HEAD), keys.dtype)
    shapes = [jax.ShapeDtypeStruct((m, width, HEAD, HEAD), jnp.float32) for width in widths]
    shapes += [jax.ShapeDtypeStruct((m, width, HEAD, HEAD), jnp.bfloat16) for width in swaps]
    spare = 0
    if ahead:
        shapes += [jax.ShapeDtypeStruct((n, rows, odd(ahead[1]) * HEAD), jnp.bfloat16)] * 3
        spare = 6 * n * rows * odd(ahead[1]) * HEAD
    return pl.pallas_call(
        functools.partial(local_body, n, widths, swaps, ahead),
        in_specs=[pl.BlockSpec(memory_space=pltpu.SMEM)] * 2 + [pl.BlockSpec(memory_space=pltpu.HBM)] * 3,
        out_specs=[pl.BlockSpec(memory_space=pltpu.VMEM)] * len(shapes),
        out_shape=shapes,
        scratch_shapes=[buf, buf, pltpu.SemaphoreType.DMA((2, n)), pltpu.SemaphoreType.DMA((3, n))],
        compiler_params=params(4 * n * rows * odd(total) * HEAD + 3 * n * total * HEAD * HEAD + spare),
        cost_estimate=pl.CostEstimate(
            flops=2 * n * total * rows * HEAD * HEAD, bytes_accessed=4 * rows * n * total * HEAD, transcendentals=0
        ),
        name="local",
    )(place, jnp.full((1,), low, jnp.int32), keys, values, queries)


def masked_scores(query, key):
    rows = query.shape[0]
    tiles = []
    for low in range(0, rows, TILE):
        high = min(low + TILE, rows)
        part = lax.dot_general(
            query[low:], key[low:high], (((1,), (1,)), ((), ())), preferred_element_type=jnp.float32
        )
        size = high - low
        spot = lax.broadcasted_iota(jnp.int32, (size, size), 0)
        other = lax.broadcasted_iota(jnp.int32, (size, size), 1)
        pieces = [jnp.where(other <= spot, part[:size], 0.0).astype(jnp.bfloat16)]
        if low:
            pieces.insert(0, jnp.zeros((low, size), jnp.bfloat16))
        if high < rows:
            pieces.append(part[size:].astype(jnp.bfloat16))
        tiles.append(jnp.concatenate(pieces, axis=0) if len(pieces) > 1 else pieces[0])
    return tiles


def attend_body(n, spans, order, early, place, low, queries, keys, values, gain, *refs):
    states, outs = refs[: 2 * len(spans)], refs[2 * len(spans) :][:n]
    sown, soth, gbuf, held, sems, extra = refs[-6:]
    qbuf, kbuf, vbuf = (queries, keys, values) if early else refs[-9:-6]
    width = sum(size for _, size in spans)
    m, wide = n // 2, width * HEAD
    together = rows_together(m, width, 8 if early else 6)
    here = place[0], place[1], low[0]
    small, start = [(gain, gbuf)], 0
    for chunk, (skip, size) in enumerate(spans):
        for source, buf in ((states[2 * chunk], sown), (states[2 * chunk + 1], soth)):
            small.append((source.at[:, skip : skip + size], buf.at[:, start : start + size]))
        start += size
    small = [pltpu.make_async_copy(source, buf, extra.at[which]) for which, (source, buf) in enumerate(small)]

    def copies(step, side):
        cols = pl.ds(column(here, lax.rem(here[0] + step, m), side, n), wide)
        slot = 2 * step + side
        return [
            pltpu.make_async_copy(source.at[:, cols], buf.at[slot, :, :wide], sems.at[which, slot])
            for which, (source, buf) in enumerate(((queries, qbuf), (keys, kbuf), (values, vbuf)))
        ]

    def source_slot(step, side):
        return 2 * (lax.rem(here[0] + step, m) if early else step) + side

    def sends(step):
        return [
            pltpu.make_async_copy(held.at[slot, :, :wide], outs[order.index(slot)], sems.at[3, slot])
            for slot in (2 * step, 2 * step + 1)
        ]

    def fetch(step, carry):
        for side in range(2):
            for copy in copies(step, side):
                copy.start()
        return carry

    def work(group, carry):
        steps = [group * together + index for index in range(together)]
        for step in steps:
            for side in range(0 if early else 2):
                for copy in copies(step, side):
                    copy.wait()
        heads = [
            (step, side, head, slice(head * HEAD, (head + 1) * HEAD))
            for step in steps
            for side in range(2)
            for head in range(width)
        ]
        scores = [
            masked_scores(qbuf[source_slot(step, side), :, cols], kbuf[source_slot(step, side), :, cols])
            for step, side, _, cols in heads
        ]
        attended = []
        for (step, side, head, cols), tiles in zip(heads, scores):
            slot = source_slot(step, side)
            state = (sown if side == 0 else soth)[lax.rem(here[0] + step, m), head]
            left = jnp.concatenate([*tiles, qbuf[slot, :, cols]], axis=1)
            right = jnp.concatenate([vbuf[slot, :, cols], state], axis=0)
            attended.append(jnp.dot(left, right, preferred_element_type=jnp.float32))
        for (step, side, head, cols), value in zip(heads, attended):
            square = jnp.mean(value * value, axis=-1, keepdims=True)
            begin = pl.multiple_of(column(here, lax.rem(here[0] + step, m), side, n) + head * HEAD, HEAD)
            mixed = value * lax.rsqrt(square + 1e-05) * gbuf[:, pl.ds(begin, HEAD)]
            held[2 * step + side, :, cols] = mixed.astype(held.dtype)
        for fixed in range(m // together):

            @pl.when(group == fixed)
            def _(fixed=fixed):
                for index in range(together):
                    for copy in sends(fixed * together + index):
                        copy.start()

        return carry

    if not early:
        lax.fori_loop(0, 1, fetch, 0)
    for copy in small:
        copy.start()
    if not early:
        lax.fori_loop(1, m, fetch, 0)
    for copy in small:
        copy.wait()
    lax.fori_loop(0, m // together, work, 0)
    for step in range(m):
        for copy in sends(step):
            copy.wait()


def attend(place, queries, keys, values, gain, states, spans, order, n, low, early):
    rows, m = queries.shape[1 if early else 0], n // 2
    width = sum(size for _, size in spans)
    wide = width * HEAD
    tokens = pltpu.VMEM((n, rows, odd(width) * HEAD), jnp.bfloat16)
    state = pltpu.VMEM((m, width, HEAD, HEAD), jnp.bfloat16)
    return pl.pallas_call(
        functools.partial(attend_body, n, spans, order, early),
        in_specs=[pl.BlockSpec(memory_space=pltpu.SMEM)] * 2
        + [pl.BlockSpec(memory_space=pltpu.VMEM if early else pltpu.HBM)] * 3
        + [pl.BlockSpec(memory_space=pl.ANY)] * (1 + 2 * len(states)),
        out_specs=[pl.BlockSpec(memory_space=pltpu.HBM)] * n,
        out_shape=[jax.ShapeDtypeStruct((rows, wide), jnp.bfloat16)] * n,
        scratch_shapes=[tokens] * (0 if early else 3)
        + [
            state,
            state,
            pltpu.VMEM((1, HEADS * HEAD), jnp.float32),
            tokens,
            pltpu.SemaphoreType.DMA((4, n)),
            pltpu.SemaphoreType.DMA((1 + 2 * len(states),)),
        ],
        compiler_params=params(8 * n * rows * odd(width) * HEAD + 2 * n * width * HEAD * HEAD + 4 * HEADS * HEAD),
        cost_estimate=pl.CostEstimate(
            flops=2 * n * width * rows * HEAD * (2 * rows + HEAD),
            bytes_accessed=8 * rows * n * wide,
            transcendentals=n * width * rows,
        ),
        name="attend",
    )(place, jnp.full((1,), low, jnp.int32), queries, keys, values, gain, *(array for pair in states for array in pair))


def put_body(n, order, place, low, *refs):
    parts, out, again, sems = refs[: len(order)], refs[-3], refs[-2], refs[-1]
    m = n // 2
    rows, wide = parts[0].shape
    cols = pl.ds(pl.multiple_of(low[0] * HEAD, HEAD), wide)
    copies = []
    for index, shift in enumerate(order):
        row = lax.rem(place[0] + m - shift // 2, m)
        col = place[1] if shift % 2 == 0 else 1 - place[1]
        start = pl.multiple_of((2 * row + col) * rows, rows)
        copies.append(
            pltpu.make_async_copy(parts[index], out.at[pl.ds(start, rows), cols], sems.at[index])
        )
    for copy in copies:
        copy.start()
    for index in range(2):
        again[index] = place[index]
    for copy in copies:
        copy.wait()


def put(place, parts, out, order, n, low):
    rows, first = parts[0].shape[0], out is None
    anywhere = pl.BlockSpec(memory_space=pltpu.HBM)
    return pl.pallas_call(
        functools.partial(put_body, n, order),
        in_specs=[pl.BlockSpec(memory_space=pltpu.SMEM)] * 2 + [anywhere] * (len(parts) + (not first)),
        out_specs=[anywhere, pl.BlockSpec(memory_space=pltpu.SMEM)],
        out_shape=[
            jax.ShapeDtypeStruct((n * rows, HEADS // n * HEAD), jnp.bfloat16),
            jax.ShapeDtypeStruct((2,), jnp.int32),
        ],
        scratch_shapes=[pltpu.SemaphoreType.DMA((len(parts),))],
        input_output_aliases={} if first else {len(parts) + 2: 0},
        compiler_params=params(),
        name="put",
    )(place, jnp.full((1,), low, jnp.int32), *parts, *(() if first else (out,)))


def split(widths, per_dest):
    chunks, low = [], 0
    for width in widths:
        if low < per_dest:
            width = min(width, per_dest - low)
            chunks.append((low, width))
            low += width
    return chunks


def inside(chunks, low, width):
    return [c for c, (start, _) in enumerate(chunks) if low <= start < low + width]


class Plan:
    def __init__(self, n, queries, keys, values, gain):
        self.n, self.m = n, n // 2
        me = lax.axis_index("seq")
        self.col = me % 2
        self.place = jnp.stack([me // 2, self.col]).astype(jnp.int32)
        self.arrays = tuple(pltpu.with_memory_space_constraint(x, pltpu.HBM) for x in (queries, keys, values))
        self.gain = gain.reshape(1, HEADS * HEAD)
        self.groups, self.swaps, self.parts, self.chunks = (
            split(widths, HEADS // n) for widths in (LOCAL, SWAP, PREFIX, MIXED)
        )
        self.shifts = sorted(range(1, n), key=lambda k: (-min(k // 2, self.m - k // 2), k))
        self.made = {}

    def has(self, key):
        limit = {"message": self.m, "prefix": self.m, "sent": self.n - 1}.get(key[0], 0)
        chunks = {"group": self.groups, "swap": self.swaps, "mixed": self.chunks, "sent": self.chunks}
        chunks = chunks.get(key[0], self.parts)
        return key[1] < len(chunks) and (len(key) < 3 or key[2] <= limit)

    def get(self, *key):
        if key not in self.made:
            self.made[key] = getattr(self, key[0])(*key[1:])
        return self.made[key]

    def hold(self, value, *key):
        others = []
        for other in ORDER.get(key, ()):
            if self.has(other):
                result = self.get(*other)
                while isinstance(result, (list, tuple)):
                    result = result[-1]
                others.append(result)
        return lax.optimization_barrier((value, *others))[0] if others else value

    def group(self, g):
        low, width = self.groups[g]
        widths = tuple(self.parts[c][1] for c in inside(self.parts, low, width))
        swaps = tuple(self.swaps[c][1] for c in inside(self.swaps, low, width))
        place = self.hold(self.place, "group", g)
        ahead = self.chunks[0] if g == 1 else None
        arrays = local_states(place, *self.arrays, self.n, low, widths, swaps, ahead)
        both = len(widths) + len(swaps)
        return arrays[: len(widths)], arrays[len(widths) : both], *((arrays[both:],) if ahead else ())

    def around(self, chunks, low):
        return next(c for c, (start, width) in enumerate(chunks) if start <= low < start + width)

    def swap(self, w):
        g = self.around(self.groups, self.swaps[w][0])
        spot = inside(self.swaps, *self.groups[g]).index(w)
        other = self.hold(self.get("group", g)[1][spot], "swap", w)
        return lax.ppermute(other, "seq", [(d, d ^ 1) for d in range(self.n)])

    def local(self, c):
        low, width = self.parts[c]
        g, w = self.around(self.groups, low), self.around(self.swaps, low)
        near = self.get("swap", w)[:, low - self.swaps[w][0] :][:, :width].astype(jnp.float32)
        return self.get("group", g)[0][inside(self.parts, *self.groups[g]).index(c)], near

    def total(self, c):
        parts = [self.get("prefix", c, s) for s in range(1, self.m)]
        return sum(parts[1:], parts[0]).astype(jnp.float32)

    def message(self, c, s):
        own, near = self.get("local", c)
        if s == self.m:
            value = self.get("total", c) + jnp.where(self.col == 0, own, 0.0)
        else:
            value = own + near
            if s > 1:
                value = self.get("prefix", c, s - 1).astype(jnp.float32) + value
        return self.hold(value.astype(jnp.bfloat16), "message", c, s)

    def prefix(self, c, s):
        if s == self.m:
            pairs = [(d, d ^ 1) for d in range(self.n)]
        else:
            pairs = [(2 * (s - 1) + y, 2 * s + y) for y in range(2)]
        return lax.ppermute(self.get("message", c, s), "seq", pairs)

    def states(self, c):
        _, near = self.get("local", c)
        own = (self.get("total", c) + jnp.where(self.col == 1, near, 0.0)).astype(jnp.bfloat16)
        return own, self.get("prefix", c, self.m)

    def mixed(self, c):
        low, width = self.chunks[c]
        place = self.get("put", c - 3)[1] if c > 2 else self.place
        place = self.hold(place, "mixed", c)
        states, spans = [], []
        for part, (start, size) in enumerate(self.parts):
            first, last = max(low, start), min(low + width, start + size)
            if first < last:
                states.append(self.get("states", part))
                spans.append((first - start, last - first))
        early = c == 0 and len(self.groups) > 1
        arrays = self.get("group", 1)[2] if early else self.arrays
        return attend(place, *arrays, self.gain, states, tuple(spans), (0, *self.shifts), self.n, low, early)

    def sent(self, c, k):
        shift = self.shifts[k - 1]
        pairs = [
            (2 * z + y, 2 * ((z + shift // 2) % self.m) + (y + shift) % 2) for z in range(self.m) for y in range(2)
        ]
        return lax.ppermute(self.hold(self.get("mixed", c)[k], "sent", c, k), "seq", pairs)

    def put(self, c):
        parts = [self.get("mixed", c)[0]] + [self.get("sent", c, k) for k in range(1, self.n)]
        out, order, low = self.get("put", c - 1)[0] if c else None, (0, *self.shifts), self.chunks[c][0]
        if c == len(self.chunks) - 1:
            late = self.n // 2 + 1
            out, _ = put(self.place, parts[:late], out, order[:late], self.n, low)
            parts, order = parts[late:], order[late:]
        return put(self.place, parts, out, order, self.n, low)


def per_device(n, *arrays):
    plan = Plan(n, *arrays)
    return plan.get("put", len(plan.chunks) - 1)[0]


def solution(mesh):
    tokens = P(("batch", "seq"), None)
    return jax.shard_map(
        functools.partial(per_device, mesh.shape["seq"]),
        mesh=mesh,
        in_specs=(tokens, tokens, tokens, P()),
        out_specs=P("batch", "seq"),
        check_vma=False,
    )
```

```python
import functools

import jax
import jax.numpy as jnp
from jax import lax
from jax.experimental import pallas as pl
from jax.experimental.pallas import tpu as pltpu
from jax.sharding import PartitionSpec as P

HEADS = 64
HEAD = 128
LOCAL = (2, 6)
SWAP = (2, 3, 3)
PREFIX = (2, 3, 3)
MIXED = (2, 3, 3)
TILE = 256
SPARE = 8 * 1024 * 1024
ORDER = {
    ("message", 0, 1): [("group", 1)],
    ("message", 1, 1): [("message", 0, 2)],
    ("message", 1, 2): [("message", 0, 3)],
    ("message", 1, 3): [("message", 0, 4)],
    ("message", 2, 1): [("message", 1, 2)],
    ("message", 2, 2): [("message", 1, 3)],
    ("message", 2, 3): [("message", 1, 4), ("mixed", 0)],
    ("mixed", 0): [("message", 1, 3), ("message", 2, 2)],
    ("message", 1, 4): [("mixed", 0)],
}


def params(buffers=0):
    return pltpu.CompilerParams(vmem_limit_bytes=buffers + SPARE)


def column(place, row, side, n):
    col = place[1] if side == 0 else 1 - place[1]
    return pl.multiple_of(((2 * row + col) * (HEADS // n) + place[2]) * HEAD, HEAD)


def odd(tiles):
    return tiles + 1 - tiles % 2


def rows_together(m, width, most):
    return max(count for count in range(1, m + 1) if m % count == 0 and (count == 1 or 2 * width * count <= most))


def local_body(n, widths, swaps, ahead, place, low, keys, values, queries, *refs):
    outs, (kbuf, vbuf, sems, early) = refs[:-4], refs[-4:]
    total = sum(widths)
    here = place[0], place[1], low[0]
    together = rows_together(n // 2, total, 8)

    def copies(row, side):
        cols = pl.ds(column(here, row, side, n), total * HEAD)
        slot = 2 * row + side
        return [
            pltpu.make_async_copy(source.at[:, cols], buf.at[slot, :, : total * HEAD], sems.at[which, slot])
            for which, (source, buf) in enumerate(((keys, kbuf), (values, vbuf)))
        ]

    def copies_ahead(row, side):
        wide = ahead[1] * HEAD
        cols = pl.ds(column((place[0], place[1], ahead[0]), row, side, n), wide)
        slot = 2 * row + side
        return [
            pltpu.make_async_copy(source.at[:, cols], out.at[slot, :, :wide], early.at[which, slot])
            for which, (source, out) in enumerate(zip((queries, keys, values), outs[-3:]))
        ]

    def fetch(row, carry):
        for side in range(2):
            for copy in copies(row, side):
                copy.start()
        return carry

    def start_ahead(row, carry):
        for side in range(2):
            for copy in copies_ahead(row, side):
                copy.start()
        return carry

    def wait_ahead(row, carry):
        for side in range(2):
            for copy in copies_ahead(row, side):
                copy.wait()
        return carry

    def work(step, carry):
        slots = [(step * together + index, side) for index in range(together) for side in range(2)]
        for row, side in slots:
            for copy in copies(row, side):
                copy.wait()
        places = [
            [(out, head) for out, width in zip(arrays, sizes) for head in range(width)]
            for arrays, sizes in ((outs[: len(widths)], widths), (outs[len(widths) :][: len(swaps)], swaps))
        ]
        for row, side in slots:
            for first in range(0, total, 2):
                size = min(2, total - first)
                cols = slice(first * HEAD, (first + size) * HEAD)
                both = lax.dot_general(
                    kbuf[2 * row + side, :, cols],
                    vbuf[2 * row + side, :, cols],
                    (((0,), (0,)), ((), ())),
                    preferred_element_type=jnp.float32,
                )
                for index in range(first, first + size):
                    part = slice((index - first) * HEAD, (index - first + 1) * HEAD)
                    out, head = places[side][index]
                    out[row, head] = both[part, part].astype(out.dtype)
        return carry

    lax.fori_loop(0, n // 2, fetch, 0)
    if ahead:
        lax.fori_loop(0, n // 2, start_ahead, 0)
    lax.fori_loop(0, n // 2 // together, work, 0)
    if ahead:
        lax.fori_loop(0, n // 2, wait_ahead, 0)


def local_states(place, queries, keys, values, n, low, widths, swaps, ahead):
    rows, m, total = keys.shape[0], n // 2, sum(widths)
    buf = pltpu.VMEM((n, rows, odd(total) * HEAD), keys.dtype)
    shapes = [jax.ShapeDtypeStruct((m, width, HEAD, HEAD), jnp.float32) for width in widths]
    shapes += [jax.ShapeDtypeStruct((m, width, HEAD, HEAD), jnp.bfloat16) for width in swaps]
    spare = 0
    if ahead:
        shapes += [jax.ShapeDtypeStruct((n, rows, odd(ahead[1]) * HEAD), jnp.bfloat16)] * 3
        spare = 6 * n * rows * odd(ahead[1]) * HEAD
    return pl.pallas_call(
        functools.partial(local_body, n, widths, swaps, ahead),
        in_specs=[pl.BlockSpec(memory_space=pltpu.SMEM)] * 2 + [pl.BlockSpec(memory_space=pltpu.HBM)] * 3,
        out_specs=[pl.BlockSpec(memory_space=pltpu.VMEM)] * len(shapes),
        out_shape=shapes,
        scratch_shapes=[buf, buf, pltpu.SemaphoreType.DMA((2, n)), pltpu.SemaphoreType.DMA((3, n))],
        compiler_params=params(4 * n * rows * odd(total) * HEAD + 3 * n * total * HEAD * HEAD + spare),
        cost_estimate=pl.CostEstimate(
            flops=2 * n * total * rows * HEAD * HEAD, bytes_accessed=4 * rows * n * total * HEAD, transcendentals=0
        ),
        name="local",
    )(place, jnp.full((1,), low, jnp.int32), keys, values, queries)


def masked_scores(query, key):
    rows = query.shape[0]
    tiles = []
    for low in range(0, rows, TILE):
        high = min(low + TILE, rows)
        part = lax.dot_general(
            query[low:], key[low:high], (((1,), (1,)), ((), ())), preferred_element_type=jnp.float32
        )
        size = high - low
        spot = lax.broadcasted_iota(jnp.int32, (size, size), 0)
        other = lax.broadcasted_iota(jnp.int32, (size, size), 1)
        pieces = [jnp.where(other <= spot, part[:size], 0.0).astype(jnp.bfloat16)]
        if low:
            pieces.insert(0, jnp.zeros((low, size), jnp.bfloat16))
        if high < rows:
            pieces.append(part[size:].astype(jnp.bfloat16))
        tiles.append(jnp.concatenate(pieces, axis=0) if len(pieces) > 1 else pieces[0])
    return tiles


def attend_body(n, spans, order, early, place, low, queries, keys, values, gain, *refs):
    states, outs = refs[: 2 * len(spans)], refs[2 * len(spans) :][:n]
    sown, soth, gbuf, held, sems, extra = refs[-6:]
    qbuf, kbuf, vbuf = (queries, keys, values) if early else refs[-9:-6]
    width = sum(size for _, size in spans)
    m, wide = n // 2, width * HEAD
    together = rows_together(m, width, 8 if early else 6)
    here = place[0], place[1], low[0]
    small, start = [(gain, gbuf)], 0
    for chunk, (skip, size) in enumerate(spans):
        for source, buf in ((states[2 * chunk], sown), (states[2 * chunk + 1], soth)):
            small.append((source.at[:, skip : skip + size], buf.at[:, start : start + size]))
        start += size
    small = [pltpu.make_async_copy(source, buf, extra.at[which]) for which, (source, buf) in enumerate(small)]

    def copies(step, side):
        cols = pl.ds(column(here, lax.rem(here[0] + step, m), side, n), wide)
        slot = 2 * step + side
        return [
            pltpu.make_async_copy(source.at[:, cols], buf.at[slot, :, :wide], sems.at[which, slot])
            for which, (source, buf) in enumerate(((queries, qbuf), (keys, kbuf), (values, vbuf)))
        ]

    def source_slot(step, side):
        return 2 * (lax.rem(here[0] + step, m) if early else step) + side

    def sends(step):
        return [
            pltpu.make_async_copy(held.at[slot, :, :wide], outs[order.index(slot)], sems.at[3, slot])
            for slot in (2 * step, 2 * step + 1)
        ]

    def fetch(step, carry):
        for side in range(2):
            for copy in copies(step, side):
                copy.start()
        return carry

    def work(group, carry):
        steps = [group * together + index for index in range(together)]
        for step in steps:
            for side in range(0 if early else 2):
                for copy in copies(step, side):
                    copy.wait()
        heads = [
            (step, side, head, slice(head * HEAD, (head + 1) * HEAD))
            for step in steps
            for side in range(2)
            for head in range(width)
        ]
        scores = [
            masked_scores(qbuf[source_slot(step, side), :, cols], kbuf[source_slot(step, side), :, cols])
            for step, side, _, cols in heads
        ]
        attended = []
        for (step, side, head, cols), tiles in zip(heads, scores):
            slot = source_slot(step, side)
            state = (sown if side == 0 else soth)[lax.rem(here[0] + step, m), head]
            left = jnp.concatenate([*tiles, qbuf[slot, :, cols]], axis=1)
            right = jnp.concatenate([vbuf[slot, :, cols], state], axis=0)
            attended.append(jnp.dot(left, right, preferred_element_type=jnp.float32))
        for (step, side, head, cols), value in zip(heads, attended):
            square = jnp.mean(value * value, axis=-1, keepdims=True)
            begin = pl.multiple_of(column(here, lax.rem(here[0] + step, m), side, n) + head * HEAD, HEAD)
            mixed = value * lax.rsqrt(square + 1e-05) * gbuf[:, pl.ds(begin, HEAD)]
            held[2 * step + side, :, cols] = mixed.astype(held.dtype)
        for fixed in range(m // together):

            @pl.when(group == fixed)
            def _(fixed=fixed):
                for index in range(together):
                    for copy in sends(fixed * together + index):
                        copy.start()

        return carry

    if not early:
        lax.fori_loop(0, 1, fetch, 0)
    for copy in small:
        copy.start()
    if not early:
        lax.fori_loop(1, m, fetch, 0)
    for copy in small:
        copy.wait()
    lax.fori_loop(0, m // together, work, 0)
    for step in range(m):
        for copy in sends(step):
            copy.wait()


def attend(place, queries, keys, values, gain, states, spans, order, n, low, early):
    rows, m = queries.shape[1 if early else 0], n // 2
    width = sum(size for _, size in spans)
    wide = width * HEAD
    tokens = pltpu.VMEM((n, rows, odd(width) * HEAD), jnp.bfloat16)
    state = pltpu.VMEM((m, width, HEAD, HEAD), jnp.bfloat16)
    return pl.pallas_call(
        functools.partial(attend_body, n, spans, order, early),
        in_specs=[pl.BlockSpec(memory_space=pltpu.SMEM)] * 2
        + [pl.BlockSpec(memory_space=pltpu.VMEM if early else pltpu.HBM)] * 3
        + [pl.BlockSpec(memory_space=pl.ANY)] * (1 + 2 * len(states)),
        out_specs=[pl.BlockSpec(memory_space=pltpu.HBM)] * n,
        out_shape=[jax.ShapeDtypeStruct((rows, wide), jnp.bfloat16)] * n,
        scratch_shapes=[tokens] * (0 if early else 3)
        + [
            state,
            state,
            pltpu.VMEM((1, HEADS * HEAD), jnp.float32),
            tokens,
            pltpu.SemaphoreType.DMA((4, n)),
            pltpu.SemaphoreType.DMA((1 + 2 * len(states),)),
        ],
        compiler_params=params(8 * n * rows * odd(width) * HEAD + 2 * n * width * HEAD * HEAD + 4 * HEADS * HEAD),
        cost_estimate=pl.CostEstimate(
            flops=2 * n * width * rows * HEAD * (2 * rows + HEAD),
            bytes_accessed=8 * rows * n * wide,
            transcendentals=n * width * rows,
        ),
        name="attend",
    )(place, jnp.full((1,), low, jnp.int32), queries, keys, values, gain, *(array for pair in states for array in pair))


def put_body(n, order, place, low, *refs):
    parts, out, again, sems = refs[: len(order)], refs[-3], refs[-2], refs[-1]
    m = n // 2
    rows, wide = parts[0].shape
    cols = pl.ds(pl.multiple_of(low[0] * HEAD, HEAD), wide)
    copies = []
    for index, shift in enumerate(order):
        row = lax.rem(place[0] + m - shift // 2, m)
        col = place[1] if shift % 2 == 0 else 1 - place[1]
        start = pl.multiple_of((2 * row + col) * rows, rows)
        copies.append(
            pltpu.make_async_copy(parts[index], out.at[pl.ds(start, rows), cols], sems.at[index])
        )
    for copy in copies:
        copy.start()
    for index in range(2):
        again[index] = place[index]
    for copy in copies:
        copy.wait()


def put(place, parts, out, order, n, low):
    rows, first = parts[0].shape[0], out is None
    anywhere = pl.BlockSpec(memory_space=pltpu.HBM)
    return pl.pallas_call(
        functools.partial(put_body, n, order),
        in_specs=[pl.BlockSpec(memory_space=pltpu.SMEM)] * 2 + [anywhere] * (len(parts) + (not first)),
        out_specs=[anywhere, pl.BlockSpec(memory_space=pltpu.SMEM)],
        out_shape=[
            jax.ShapeDtypeStruct((n * rows, HEADS // n * HEAD), jnp.bfloat16),
            jax.ShapeDtypeStruct((2,), jnp.int32),
        ],
        scratch_shapes=[pltpu.SemaphoreType.DMA((len(parts),))],
        input_output_aliases={} if first else {len(parts) + 2: 0},
        compiler_params=params(),
        name="put",
    )(place, jnp.full((1,), low, jnp.int32), *parts, *(() if first else (out,)))


def split(widths, per_dest):
    chunks, low = [], 0
    for width in widths:
        if low < per_dest:
            width = min(width, per_dest - low)
            chunks.append((low, width))
            low += width
    return chunks


def inside(chunks, low, width):
    return [c for c, (start, _) in enumerate(chunks) if low <= start < low + width]


class Plan:
    def __init__(self, n, queries, keys, values, gain):
        self.n, self.m = n, n // 2
        me = lax.axis_index("seq")
        self.col = me % 2
        self.place = jnp.stack([me // 2, self.col]).astype(jnp.int32)
        self.arrays = tuple(pltpu.with_memory_space_constraint(x, pltpu.HBM) for x in (queries, keys, values))
        self.gain = gain.reshape(1, HEADS * HEAD)
        self.groups, self.swaps, self.parts, self.chunks = (
            split(widths, HEADS // n) for widths in (LOCAL, SWAP, PREFIX, MIXED)
        )
        self.shifts = sorted(range(1, n), key=lambda k: (-min(k // 2, self.m - k // 2), k))
        self.made = {}

    def has(self, key):
        limit = {"message": self.m, "prefix": self.m, "sent": self.n - 1}.get(key[0], 0)
        chunks = {"group": self.groups, "swap": self.swaps, "mixed": self.chunks, "sent": self.chunks}
        chunks = chunks.get(key[0], self.parts)
        return key[1] < len(chunks) and (len(key) < 3 or key[2] <= limit)

    def get(self, *key):
        if key not in self.made:
            self.made[key] = getattr(self, key[0])(*key[1:])
        return self.made[key]

    def hold(self, value, *key):
        others = []
        for other in ORDER.get(key, ()):
            if self.has(other):
                result = self.get(*other)
                while isinstance(result, (list, tuple)):
                    result = result[-1]
                others.append(result)
        return lax.optimization_barrier((value, *others))[0] if others else value

    def group(self, g):
        low, width = self.groups[g]
        widths = tuple(self.parts[c][1] for c in inside(self.parts, low, width))
        swaps = tuple(self.swaps[c][1] for c in inside(self.swaps, low, width))
        place = self.hold(self.place, "group", g)
        ahead = self.chunks[0] if g == 1 else None
        arrays = local_states(place, *self.arrays, self.n, low, widths, swaps, ahead)
        both = len(widths) + len(swaps)
        return arrays[: len(widths)], arrays[len(widths) : both], *((arrays[both:],) if ahead else ())

    def around(self, chunks, low):
        return next(c for c, (start, width) in enumerate(chunks) if start <= low < start + width)

    def swap(self, w):
        g = self.around(self.groups, self.swaps[w][0])
        spot = inside(self.swaps, *self.groups[g]).index(w)
        other = self.hold(self.get("group", g)[1][spot], "swap", w)
        return lax.ppermute(other, "seq", [(d, d ^ 1) for d in range(self.n)])

    def local(self, c):
        low, width = self.parts[c]
        g, w = self.around(self.groups, low), self.around(self.swaps, low)
        near = self.get("swap", w)[:, low - self.swaps[w][0] :][:, :width].astype(jnp.float32)
        return self.get("group", g)[0][inside(self.parts, *self.groups[g]).index(c)], near

    def total(self, c):
        parts = [self.get("prefix", c, s) for s in range(1, self.m)]
        return sum(parts[1:], parts[0]).astype(jnp.float32)

    def message(self, c, s):
        own, near = self.get("local", c)
        if s == self.m:
            value = self.get("total", c) + jnp.where(self.col == 0, own, 0.0)
        else:
            value = own + near
            if s > 1:
                value = self.get("prefix", c, s - 1).astype(jnp.float32) + value
        return self.hold(value.astype(jnp.bfloat16), "message", c, s)

    def prefix(self, c, s):
        if s == self.m:
            pairs = [(d, d ^ 1) for d in range(self.n)]
        else:
            pairs = [(2 * (s - 1) + y, 2 * s + y) for y in range(2)]
        return lax.ppermute(self.get("message", c, s), "seq", pairs)

    def states(self, c):
        _, near = self.get("local", c)
        own = (self.get("total", c) + jnp.where(self.col == 1, near, 0.0)).astype(jnp.bfloat16)
        return own, self.get("prefix", c, self.m)

    def mixed(self, c):
        low, width = self.chunks[c]
        place = self.get("put", c - 3)[1] if c > 2 else self.place
        place = self.hold(place, "mixed", c)
        states, spans = [], []
        for part, (start, size) in enumerate(self.parts):
            first, last = max(low, start), min(low + width, start + size)
            if first < last:
                states.append(self.get("states", part))
                spans.append((first - start, last - first))
        early = c == 0 and len(self.groups) > 1
        arrays = self.arrays
        if early:
            arrays = [pltpu.with_memory_space_constraint(x, pltpu.VMEM) for x in self.get("group", 1)[2]]
        return attend(place, *arrays, self.gain, states, tuple(spans), (0, *self.shifts), self.n, low, early)

    def sent(self, c, k):
        shift = self.shifts[k - 1]
        pairs = [
            (2 * z + y, 2 * ((z + shift // 2) % self.m) + (y + shift) % 2) for z in range(self.m) for y in range(2)
        ]
        return lax.ppermute(self.hold(self.get("mixed", c)[k], "sent", c, k), "seq", pairs)

    def put(self, c):
        parts = [self.get("mixed", c)[0]] + [self.get("sent", c, k) for k in range(1, self.n)]
        out, order, low = self.get("put", c - 1)[0] if c else None, (0, *self.shifts), self.chunks[c][0]
        if c == len(self.chunks) - 1:
            late = self.n // 2 + 1
            out, _ = put(self.place, parts[:late], out, order[:late], self.n, low)
            parts, order = parts[late:], order[late:]
        return put(self.place, parts, out, order, self.n, low)


def per_device(n, *arrays):
    plan = Plan(n, *arrays)
    return plan.get("put", len(plan.chunks) - 1)[0]


def solution(mesh):
    tokens = P(("batch", "seq"), None)
    return jax.shard_map(
        functools.partial(per_device, mesh.shape["seq"]),
        mesh=mesh,
        in_specs=(tokens, tokens, tokens, P()),
        out_specs=P("batch", "seq"),
        check_vma=False,
    )
```

```python
import functools

import jax
import jax.numpy as jnp
from jax import lax
from jax.experimental import pallas as pl
from jax.experimental.pallas import tpu as pltpu
from jax.sharding import PartitionSpec as P

HEADS = 64
HEAD = 128
LOCAL = (2, 6)
SWAP = (2, 3, 3)
PREFIX = (2, 3, 3)
MIXED = (2, 3, 3)
TILE = 256
SPARE = 8 * 1024 * 1024
ORDER = {
    ("message", 0, 1): [("group", 1)],
    ("message", 1, 1): [("message", 0, 2)],
    ("message", 1, 2): [("message", 0, 3)],
    ("message", 1, 3): [("message", 0, 4)],
    ("message", 2, 1): [("message", 1, 2)],
    ("message", 2, 2): [("message", 1, 3)],
    ("message", 2, 3): [("message", 1, 4), ("mixed", 0)],
    ("mixed", 0): [("message", 1, 3), ("message", 2, 2)],
    ("message", 1, 4): [("mixed", 0)],
}


def params(buffers=0):
    return pltpu.CompilerParams(vmem_limit_bytes=buffers + SPARE)


def column(place, row, side, n):
    col = place[1] if side == 0 else 1 - place[1]
    return pl.multiple_of(((2 * row + col) * (HEADS // n) + place[2]) * HEAD, HEAD)


def odd(tiles):
    return tiles + 1 - tiles % 2


def rows_together(m, width, most):
    return max(count for count in range(1, m + 1) if m % count == 0 and (count == 1 or 2 * width * count <= most))


def local_body(n, widths, swaps, place, low, keys, values, *refs):
    outs, (kbuf, vbuf, sems) = refs[:-3], refs[-3:]
    total = sum(widths)
    here = place[0], place[1], low[0]
    together = rows_together(n // 2, total, 16)

    def copies(row, side):
        cols = pl.ds(column(here, row, side, n), total * HEAD)
        slot = 2 * row + side
        return [
            pltpu.make_async_copy(source.at[:, cols], buf.at[slot, :, : total * HEAD], sems.at[which, slot])
            for which, (source, buf) in enumerate(((keys, kbuf), (values, vbuf)))
        ]

    def fetch(row, carry):
        for side in range(2):
            for copy in copies(row, side):
                copy.start()
        return carry

    def work(step, carry):
        slots = [(step * together + index, side) for index in range(together) for side in range(2)]
        for row, side in slots:
            for copy in copies(row, side):
                copy.wait()
        places = [
            [(out, head) for out, width in zip(arrays, sizes) for head in range(width)]
            for arrays, sizes in ((outs[: len(widths)], widths), (outs[len(widths) :], swaps))
        ]
        for row, side in slots:
            for first in range(0, total, 2):
                size = min(2, total - first)
                cols = slice(first * HEAD, (first + size) * HEAD)
                both = lax.dot_general(
                    kbuf[2 * row + side, :, cols],
                    vbuf[2 * row + side, :, cols],
                    (((0,), (0,)), ((), ())),
                    preferred_element_type=jnp.float32,
                )
                for index in range(first, first + size):
                    part = slice((index - first) * HEAD, (index - first + 1) * HEAD)
                    out, head = places[side][index]
                    out[row, head] = both[part, part].astype(out.dtype)
        return carry

    lax.fori_loop(0, n // 2, fetch, 0)
    lax.fori_loop(0, n // 2 // together, work, 0)


def local_states(place, keys, values, n, low, widths, swaps):
    rows, m, total = keys.shape[0], n // 2, sum(widths)
    buf = pltpu.VMEM((n, rows, odd(total) * HEAD), keys.dtype)
    shapes = [jax.ShapeDtypeStruct((m, width, HEAD, HEAD), jnp.float32) for width in widths]
    shapes += [jax.ShapeDtypeStruct((m, width, HEAD, HEAD), jnp.bfloat16) for width in swaps]
    return pl.pallas_call(
        functools.partial(local_body, n, widths, swaps),
        in_specs=[pl.BlockSpec(memory_space=pltpu.SMEM)] * 2 + [pl.BlockSpec(memory_space=pltpu.HBM)] * 2,
        out_specs=[pl.BlockSpec(memory_space=pltpu.VMEM)] * len(shapes),
        out_shape=shapes,
        scratch_shapes=[buf, buf, pltpu.SemaphoreType.DMA((2, n))],
        compiler_params=params(4 * n * rows * odd(total) * HEAD + 3 * n * total * HEAD * HEAD),
        cost_estimate=pl.CostEstimate(
            flops=2 * n * total * rows * HEAD * HEAD, bytes_accessed=4 * rows * n * total * HEAD, transcendentals=0
        ),
        name="local",
    )(place, jnp.full((1,), low, jnp.int32), keys, values)


def masked_scores(query, key):
    rows = query.shape[0]
    tiles = []
    for low in range(0, rows, TILE):
        high = min(low + TILE, rows)
        part = lax.dot_general(
            query[low:], key[low:high], (((1,), (1,)), ((), ())), preferred_element_type=jnp.float32
        )
        size = high - low
        spot = lax.broadcasted_iota(jnp.int32, (size, size), 0)
        other = lax.broadcasted_iota(jnp.int32, (size, size), 1)
        pieces = [jnp.where(other <= spot, part[:size], 0.0).astype(jnp.bfloat16)]
        if low:
            pieces.insert(0, jnp.zeros((low, size), jnp.bfloat16))
        if high < rows:
            pieces.append(part[size:].astype(jnp.bfloat16))
        tiles.append(jnp.concatenate(pieces, axis=0) if len(pieces) > 1 else pieces[0])
    return tiles


def attend_body(n, spans, order, place, low, queries, keys, values, gain, *refs):
    states, outs = refs[: 2 * len(spans)], refs[2 * len(spans) :][:n]
    qbuf, kbuf, vbuf, sown, soth, gbuf, held, sems, extra = refs[-9:]
    width = sum(size for _, size in spans)
    m, wide = n // 2, width * HEAD
    together = rows_together(m, width, 6)
    here = place[0], place[1], low[0]
    small, start = [(gain, gbuf)], 0
    for chunk, (skip, size) in enumerate(spans):
        for source, buf in ((states[2 * chunk], sown), (states[2 * chunk + 1], soth)):
            small.append((source.at[:, skip : skip + size], buf.at[:, start : start + size]))
        start += size
    small = [pltpu.make_async_copy(source, buf, extra.at[which]) for which, (source, buf) in enumerate(small)]

    def copies(step, side):
        cols = pl.ds(column(here, lax.rem(here[0] + step, m), side, n), wide)
        slot = 2 * step + side
        return [
            pltpu.make_async_copy(source.at[:, cols], buf.at[slot, :, :wide], sems.at[which, slot])
            for which, (source, buf) in enumerate(((queries, qbuf), (keys, kbuf), (values, vbuf)))
        ]

    def sends(step):
        return [
            pltpu.make_async_copy(held.at[slot, :, :wide], outs[order.index(slot)], sems.at[3, slot])
            for slot in (2 * step, 2 * step + 1)
        ]

    def fetch(step, carry):
        for side in range(2):
            for copy in copies(step, side):
                copy.start()
        return carry

    def work(group, carry):
        steps = [group * together + index for index in range(together)]
        for step in steps:
            for side in range(2):
                for copy in copies(step, side):
                    copy.wait()
        heads = [
            (step, side, head, slice(head * HEAD, (head + 1) * HEAD))
            for step in steps
            for side in range(2)
            for head in range(width)
        ]
        scores = [
            masked_scores(qbuf[2 * step + side, :, cols], kbuf[2 * step + side, :, cols])
            for step, side, _, cols in heads
        ]
        attended = []
        for (step, side, head, cols), tiles in zip(heads, scores):
            slot = 2 * step + side
            state = (sown if side == 0 else soth)[lax.rem(here[0] + step, m), head]
            left = jnp.concatenate([*tiles, qbuf[slot, :, cols]], axis=1)
            right = jnp.concatenate([vbuf[slot, :, cols], state], axis=0)
            attended.append(jnp.dot(left, right, preferred_element_type=jnp.float32))
        for (step, side, head, cols), value in zip(heads, attended):
            square = jnp.mean(value * value, axis=-1, keepdims=True)
            begin = pl.multiple_of(column(here, lax.rem(here[0] + step, m), side, n) + head * HEAD, HEAD)
            mixed = value * lax.rsqrt(square + 1e-05) * gbuf[:, pl.ds(begin, HEAD)]
            held[2 * step + side, :, cols] = mixed.astype(held.dtype)
        for fixed in range(m // together):

            @pl.when(group == fixed)
            def _(fixed=fixed):
                for index in range(together):
                    for copy in sends(fixed * together + index):
                        copy.start()

        return carry

    lax.fori_loop(0, 1, fetch, 0)
    for copy in small:
        copy.start()
    lax.fori_loop(1, m, fetch, 0)
    for copy in small:
        copy.wait()
    lax.fori_loop(0, m // together, work, 0)
    for step in range(m):
        for copy in sends(step):
            copy.wait()


def attend(place, queries, keys, values, gain, states, spans, order, n, low):
    rows, m = queries.shape[0], n // 2
    width = sum(size for _, size in spans)
    wide = width * HEAD
    tokens = pltpu.VMEM((n, rows, odd(width) * HEAD), jnp.bfloat16)
    state = pltpu.VMEM((m, width, HEAD, HEAD), jnp.bfloat16)
    return pl.pallas_call(
        functools.partial(attend_body, n, spans, order),
        in_specs=[pl.BlockSpec(memory_space=pltpu.SMEM)] * 2
        + [pl.BlockSpec(memory_space=pltpu.HBM)] * 3
        + [pl.BlockSpec(memory_space=pl.ANY)] * (1 + 2 * len(states)),
        out_specs=[pl.BlockSpec(memory_space=pltpu.HBM)] * n,
        out_shape=[jax.ShapeDtypeStruct((rows, wide), jnp.bfloat16)] * n,
        scratch_shapes=[
            tokens,
            tokens,
            tokens,
            state,
            state,
            pltpu.VMEM((1, HEADS * HEAD), jnp.float32),
            tokens,
            pltpu.SemaphoreType.DMA((4, n)),
            pltpu.SemaphoreType.DMA((1 + 2 * len(states),)),
        ],
        compiler_params=params(8 * n * rows * odd(width) * HEAD + 2 * n * width * HEAD * HEAD + 4 * HEADS * HEAD),
        cost_estimate=pl.CostEstimate(
            flops=2 * n * width * rows * HEAD * (2 * rows + HEAD),
            bytes_accessed=8 * rows * n * wide,
            transcendentals=n * width * rows,
        ),
        name="attend",
    )(place, jnp.full((1,), low, jnp.int32), queries, keys, values, gain, *(array for pair in states for array in pair))


def put_body(n, order, place, low, *refs):
    parts, out, again, sems = refs[: len(order)], refs[-3], refs[-2], refs[-1]
    m = n // 2
    rows, wide = parts[0].shape
    cols = pl.ds(pl.multiple_of(low[0] * HEAD, HEAD), wide)
    copies = []
    for index, shift in enumerate(order):
        row = lax.rem(place[0] + m - shift // 2, m)
        col = place[1] if shift % 2 == 0 else 1 - place[1]
        start = pl.multiple_of((2 * row + col) * rows, rows)
        copies.append(
            pltpu.make_async_copy(parts[index], out.at[pl.ds(start, rows), cols], sems.at[index])
        )
    for copy in copies:
        copy.start()
    for index in range(2):
        again[index] = place[index]
    for copy in copies:
        copy.wait()


def put(place, parts, out, order, n, low):
    rows, first = parts[0].shape[0], out is None
    anywhere = pl.BlockSpec(memory_space=pltpu.HBM)
    return pl.pallas_call(
        functools.partial(put_body, n, order),
        in_specs=[pl.BlockSpec(memory_space=pltpu.SMEM)] * 2 + [anywhere] * (len(parts) + (not first)),
        out_specs=[anywhere, pl.BlockSpec(memory_space=pltpu.SMEM)],
        out_shape=[
            jax.ShapeDtypeStruct((n * rows, HEADS // n * HEAD), jnp.bfloat16),
            jax.ShapeDtypeStruct((2,), jnp.int32),
        ],
        scratch_shapes=[pltpu.SemaphoreType.DMA((len(parts),))],
        input_output_aliases={} if first else {len(parts) + 2: 0},
        compiler_params=params(),
        name="put",
    )(place, jnp.full((1,), low, jnp.int32), *parts, *(() if first else (out,)))


def split(widths, per_dest):
    chunks, low = [], 0
    for width in widths:
        if low < per_dest:
            width = min(width, per_dest - low)
            chunks.append((low, width))
            low += width
    return chunks


def inside(chunks, low, width):
    return [c for c, (start, _) in enumerate(chunks) if low <= start < low + width]


class Plan:
    def __init__(self, n, queries, keys, values, gain):
        self.n, self.m = n, n // 2
        me = lax.axis_index("seq")
        self.col = me % 2
        self.place = jnp.stack([me // 2, self.col]).astype(jnp.int32)
        self.arrays = tuple(pltpu.with_memory_space_constraint(x, pltpu.HBM) for x in (queries, keys, values))
        self.gain = gain.reshape(1, HEADS * HEAD)
        self.groups, self.swaps, self.parts, self.chunks = (
            split(widths, HEADS // n) for widths in (LOCAL, SWAP, PREFIX, MIXED)
        )
        self.shifts = sorted(range(1, n), key=lambda k: (-min(k // 2, self.m - k // 2), k))
        self.made = {}

    def has(self, key):
        limit = {"message": self.m, "prefix": self.m, "sent": self.n - 1}.get(key[0], 0)
        chunks = {"group": self.groups, "swap": self.swaps, "mixed": self.chunks, "sent": self.chunks}
        chunks = chunks.get(key[0], self.parts)
        return key[1] < len(chunks) and (len(key) < 3 or key[2] <= limit)

    def get(self, *key):
        if key not in self.made:
            self.made[key] = getattr(self, key[0])(*key[1:])
        return self.made[key]

    def hold(self, value, *key):
        others = []
        for other in ORDER.get(key, ()):
            if self.has(other):
                result = self.get(*other)
                while isinstance(result, (list, tuple)):
                    result = result[-1]
                others.append(result)
        return lax.optimization_barrier((value, *others))[0] if others else value

    def group(self, g):
        low, width = self.groups[g]
        widths = tuple(self.parts[c][1] for c in inside(self.parts, low, width))
        swaps = tuple(self.swaps[c][1] for c in inside(self.swaps, low, width))
        _, keys, values = self.arrays
        place = self.hold(self.place, "group", g)
        arrays = local_states(place, keys, values, self.n, low, widths, swaps)
        return arrays[: len(widths)], arrays[len(widths) :]

    def around(self, chunks, low):
        return next(c for c, (start, width) in enumerate(chunks) if start <= low < start + width)

    def swap(self, w):
        g = self.around(self.groups, self.swaps[w][0])
        spot = inside(self.swaps, *self.groups[g]).index(w)
        other = self.hold(self.get("group", g)[1][spot], "swap", w)
        return lax.ppermute(other, "seq", [(d, d ^ 1) for d in range(self.n)])

    def local(self, c):
        low, width = self.parts[c]
        g, w = self.around(self.groups, low), self.around(self.swaps, low)
        near = self.get("swap", w)[:, low - self.swaps[w][0] :][:, :width].astype(jnp.float32)
        return self.get("group", g)[0][inside(self.parts, *self.groups[g]).index(c)], near

    def total(self, c):
        parts = [self.get("prefix", c, s) for s in range(1, self.m)]
        return sum(parts[1:], parts[0]).astype(jnp.float32)

    def message(self, c, s):
        own, near = self.get("local", c)
        if s == self.m:
            value = self.get("total", c) + jnp.where(self.col == 0, own, 0.0)
        else:
            value = own + near
            if s > 1:
                value = self.get("prefix", c, s - 1).astype(jnp.float32) + value
        return self.hold(value.astype(jnp.bfloat16), "message", c, s)

    def prefix(self, c, s):
        if s == self.m:
            pairs = [(d, d ^ 1) for d in range(self.n)]
        else:
            pairs = [(2 * (s - 1) + y, 2 * s + y) for y in range(2)]
        return lax.ppermute(self.get("message", c, s), "seq", pairs)

    def states(self, c):
        _, near = self.get("local", c)
        own = (self.get("total", c) + jnp.where(self.col == 1, near, 0.0)).astype(jnp.bfloat16)
        return own, self.get("prefix", c, self.m)

    def mixed(self, c):
        low, width = self.chunks[c]
        place = self.get("put", c - 3)[1] if c > 2 else self.place
        place = self.hold(place, "mixed", c)
        states, spans = [], []
        for part, (start, size) in enumerate(self.parts):
            first, last = max(low, start), min(low + width, start + size)
            if first < last:
                states.append(self.get("states", part))
                spans.append((first - start, last - first))
        return attend(place, *self.arrays, self.gain, states, tuple(spans), (0, *self.shifts), self.n, low)

    def sent(self, c, k):
        shift = self.shifts[k - 1]
        pairs = [
            (2 * z + y, 2 * ((z + shift // 2) % self.m) + (y + shift) % 2) for z in range(self.m) for y in range(2)
        ]
        return lax.ppermute(self.hold(self.get("mixed", c)[k], "sent", c, k), "seq", pairs)

    def put(self, c):
        parts = [self.get("mixed", c)[0]] + [self.get("sent", c, k) for k in range(1, self.n)]
        out, order, low = self.get("put", c - 1)[0] if c else None, (0, *self.shifts), self.chunks[c][0]
        if c == len(self.chunks) - 1:
            late = self.n // 2 + 1
            out, _ = put(self.place, parts[:late], out, order[:late], self.n, low)
            parts, order = parts[late:], order[late:]
        return put(self.place, parts, out, order, self.n, low)


def per_device(n, *arrays):
    plan = Plan(n, *arrays)
    return plan.get("put", len(plan.chunks) - 1)[0]


def solution(mesh):
    tokens = P(("batch", "seq"), None)
    return jax.shard_map(
        functools.partial(per_device, mesh.shape["seq"]),
        mesh=mesh,
        in_specs=(tokens, tokens, tokens, P()),
        out_specs=P("batch", "seq"),
        check_vma=False,
    )
```
